128 devices in a mesh: outer: 8 (over y_hi, x), inner: 16 (over y_lo, z, core).
Axes of the slice: x: 4, y: 4 (y_hi: 2, y_lo: 2; y = y_hi * 2 + y_lo), z: 4, core: 2. Of those that a mesh axis runs over, the one named last changes fastest.
Arguments:
- pseudo_grad: float32 [8, 8192, 2048], P('outer', 'inner'), may hold values from -450 to 450, as said below
- params: float32 [8192, 2048], P('inner'), may hold values from -0.75 to 0.75
- momentum: float32 [8192, 2048], P('inner'), may hold values from -6 to 6
Outputs:
- new_params: float32 [8192, 2048], P('inner')
- new_momentum: float32 [8192, 2048], P('inner')
The draws below stay inside these ranges and needn't reach their ends.
Inputs may be any that keep to these rules, and one draw needn't show every extreme that they name: `pseudo_grad`: finite real values.
All inputs are finite; a program needn't handle non-finite values.
Results may differ from the reference program's by a relative error of at most 0.00018.
Values sent between devices are 32-bit elements; how exact they have to be, the bound alone decides.
A program may use at most 64 MiB of HBM per device.

```python
import math
import jax
import jax.numpy as jnp
from jax import lax

D = 8192
KVW = 2048
GROUPS = 8


def draw_pseudo_grad(key, part):
    key = jax.random.fold_in(key, 11)
    noise_key, column_key = jax.random.split(key, 2)
    row_scale = 10.0 ** (jnp.arange(D, dtype=jnp.float32) / max(D - 1, 1))
    column_scale = jnp.exp(jax.random.uniform(column_key, (KVW,), jnp.float32, 0.0, math.log(10.0)))
    group_scale = 1.0 + 2.0 * jnp.arange(GROUPS, dtype=jnp.float32) / max(GROUPS - 1, 1)
    base = jax.random.truncated_normal(noise_key, -4.0, 4.0, (GROUPS, D, KVW), jnp.float32)
    scaled = 0.3 * base * group_scale[:, None, None] * row_scale[None, :, None] * column_scale[None, None, :]
    return scaled.astype(jnp.float32)


def shard_levels(key, dims, cuts, low, largest):
    gain, own = 1.0, jax.random.fold_in(key, 6)
    for dim, parts in cuts:
        steps = jnp.exp(jax.random.uniform(jax.random.fold_in(own, dim), (parts,), jnp.float32, low / len(cuts), largest / len(cuts)))
        gain = gain * jnp.repeat(steps, dims[dim] // parts).reshape([-1 if axis == dim else 1 for axis in range(len(dims))])
    return gain


def scatter_about(key, extent, deviation, limit, shards=(), kind=jnp.bfloat16):
    factor_of = shard_levels(key, extent, shards, -0.22, 0.18) if shards else 1.0
    values = jax.random.normal(key, extent, jnp.float32) * deviation * factor_of
    return jnp.minimum(jnp.maximum(values, -limit), limit).astype(kind)


def setup_inputs(seed: int = 0) -> dict:
    arg_keys = jax.random.split(jax.random.key(seed), 4)
    pseudo_grad = draw_pseudo_grad(jax.random.fold_in(arg_keys[3], 71), 0)
    params = scatter_about(arg_keys[1], (D, KVW), 0.05, 0.75, ((0, 16),), jnp.float32)
    momentum = scatter_about(arg_keys[2], (D, KVW), 0.5, 6.0, ((0, 16),), jnp.float32)
    return {"pseudo_grad": pseudo_grad, "params": params, "momentum": momentum}


def reference(pseudo_grad, params, momentum):
    averaged = lax.optimization_barrier(jnp.sum(pseudo_grad, axis=0)) / jnp.float32(GROUPS)
    entries = averaged.shape[0] * averaged.shape[1]
    total_norm = jnp.sqrt(jnp.sum(averaged * averaged) + 1e-06)
    factor = jnp.minimum(1.0, 0.5 * math.sqrt(entries) / total_norm)
    clipped = factor * averaged
    new_momentum = 0.9 * momentum + clipped
    new_params = params - 0.7 * (clipped + 0.9 * new_momentum)
    return (new_params, new_momentum)
```

```python
import functools
import math

import jax
import jax.numpy as jnp
from jax import lax
from jax.experimental import pallas as pl
from jax.experimental.pallas import tpu as pltpu
from jax.sharding import PartitionSpec as P

MESH = pl.DeviceIdType.MESH
TILE = (8, 128)
TILES = 1024
A = 36
B = 28
STEP = 4
GROUPS = 8


def tiles_of(block):
    rows, columns = block.shape
    cut = block.reshape(rows // 8, 8, columns // 128, 128)
    return cut.transpose(0, 2, 1, 3).reshape(-1, 8, 128)


def block_of(tiles, rows, columns):
    cut = tiles.reshape(rows // 8, columns // 128, 8, 128)
    return cut.transpose(0, 2, 1, 3).reshape(rows, columns)


def over_tiles(count, body):
    def step(i, carry):
        body(pl.multiple_of(i * STEP, STEP))
        return carry

    lax.fori_loop(0, count // STEP, step, 0)


class Copies:
    def __init__(self, send_sem, recv_sem):
        self.send_sem, self.recv_sem, self.all = send_sem, recv_sem, []

    def send(self, src, dst, device):
        number = len(self.all)
        copy = pltpu.make_async_remote_copy(
            src_ref=src,
            dst_ref=dst,
            send_sem=self.send_sem.at[number],
            recv_sem=self.recv_sem.at[number],
            device_id=device,
            device_id_type=MESH,
        )
        copy.start()
        self.all.append(copy)
        return copy

    def finish(self):
        for copy in self.all:
            copy.wait_send()


COPIES = 65


def kernel(
    entries,
    grad_hbm,
    params_hbm,
    momentum_hbm,
    new_params,
    new_momentum,
    grad,
    params,
    momentum,
    mean,
    x_first,
    x_second,
    x_third,
    x_sum,
    x_from_y,
    y_sum,
    q_first,
    q_second,
    q_third,
    squares,
    norm_z,
    norm_core,
    norm_x,
    norm_y,
    send_sem,
    recv_sem,
    load_sem,
):
    outer, inner = lax.axis_index("outer"), lax.axis_index("inner")
    x, half = lax.rem(outer, 4), lax.div(outer, 4)
    low, z, core = lax.div(inner, 8), lax.rem(lax.div(inner, 2), 4), lax.rem(inner, 2)
    y = half * 2 + low

    def device(x=x, y=y, z=z, core=core):
        return (lax.div(y, 2) * 4 + x, (lax.rem(y, 2) * 4 + z) * 2 + core)

    def ring(at, by):
        return lax.rem(at + by, 4)

    east, west = device(x=ring(x, 1)), device(x=ring(x, 3))
    across = device(y=ring(y, 2))
    x_peers = [device(x=ring(x, k)) for k in (1, 2, 3)]
    y_peers = [device(y=ring(y, k)) for k in (1, 2, 3)]
    z_peers = [device(z=ring(z, k)) for k in (1, 2, 3)]
    core_peer = device(core=1 - core)

    barrier = pltpu.get_barrier_semaphore()
    peers = x_peers + y_peers + z_peers + [core_peer]
    for peer in peers:
        pl.semaphore_signal(barrier, inc=1, device_id=peer, device_id_type=MESH)
    loads = [
        pltpu.make_async_copy(src, dst, load_sem.at[i])
        for i, (src, dst) in enumerate(
            ((grad_hbm, grad), (params_hbm, params), (momentum_hbm, momentum))
        )
    ]
    loads[0].start()
    pl.semaphore_wait(barrier, len(peers))

    copies = Copies(send_sem, recv_sem)
    other = 1 - half

    def at_x(chunk, h, d, pieces=1):
        return pl.ds(((ring(x, chunk) * 2 + h) * 2 + d) * A, pieces * A)

    def at_y(h, chunk, d):
        return pl.ds(16 * A + ((h * 4 + ring(x, chunk)) * 2 + d) * B, B)

    def x_open(slot, h):
        return [
            copies.send(grad_hbm.at[at_x(2, h, 0)], x_first.at[slot, 0], west),
            copies.send(grad_hbm.at[at_x(2, h, 1)], x_first.at[slot, 1], east),
            copies.send(grad_hbm.at[at_x(1, h, 0)], x_second.at[slot, 0], east),
            copies.send(grad_hbm.at[at_x(3, h, 1)], x_second.at[slot, 1], west),
        ]

    def add_into(ref, term, start, count):
        def body(i):
            ref[pl.ds(i, STEP)] += term[pl.ds(start + i, STEP)]

        over_tiles(count, body)

    def x_pass(slot, h, opened):
        opened[1].wait_recv()
        add_into(x_first.at[slot, 1], grad, at_x(1, h, 1).start, A)
        one = copies.send(x_first.at[slot, 1], x_third.at[slot, 1], east)
        opened[0].wait_recv()
        add_into(x_first.at[slot, 0], grad, at_x(3, h, 0).start, A)
        two = copies.send(x_first.at[slot, 0], x_third.at[slot, 0], west)
        return [two, one]

    y_copies = {}

    def y_open(chunk, d):
        y_copies[chunk, d] = copies.send(
            grad_hbm.at[at_y(other, chunk, d)], y_sum.at[chunk * 2 + d], across
        )

    def y_add(chunk, d):
        y_copies[chunk, d].wait_recv()
        add_into(y_sum.at[chunk * 2 + d], grad, at_y(half, chunk, d).start, B)
        return y_sum.at[chunk * 2 + d]

    opened_a = x_open(0, other)
    y_open(2, 0)
    y_open(2, 1)
    y_open(1, 0)
    loads[1].start()
    loads[2].start()
    loads[0].wait()
    passed_a = x_pass(0, other, opened_a)
    y_open(3, 1)
    opened_b = x_open(1, half)
    y_open(1, 1)
    for d in (0, 1):
        opened_a[2 + d].wait_recv()
        passed_a[d].wait_recv()
        base = at_x(0, other, d).start

        def body(i, d=d, base=base):
            at = pl.ds(i, STEP)
            x_sum[d, at] = (
                grad[pl.ds(base + i, STEP)] + x_second[0, d, at] + x_third[0, d, at]
            )

        over_tiles(A, body)
        crossed = copies.send(x_sum.at[d], x_from_y.at[d], across)
        y_copies["x", d] = crossed
    y_open(3, 0)
    passed_b = x_pass(1, half, opened_b)
    y_open(0, 0)
    y_open(0, 1)
    q_opened = [
        copies.send(y_add(2, 0), q_first.at[0], west),
        copies.send(y_add(2, 1), q_first.at[1], east),
        copies.send(y_add(1, 0), q_second.at[0], east),
        copies.send(y_add(3, 1), q_second.at[1], west),
    ]
    y_add(1, 1)
    y_add(3, 0)

    squares[...] = jnp.zeros(TILE, jnp.float32)

    def store_mean(at, value):
        value = value / jnp.float32(GROUPS)
        mean[at] = value
        squares[...] += jnp.sum(value * value, axis=0)

    for d in (0, 1):
        opened_b[2 + d].wait_recv()
        passed_b[d].wait_recv()
        y_copies["x", d].wait_recv()
        base = at_x(0, half, d).start

        def body(i, d=d, base=base):
            at = pl.ds(i, STEP)
            own = grad[pl.ds(base + i, STEP)] + x_second[1, d, at] + x_third[1, d, at]
            store_mean(pl.ds(base + i, STEP), own + x_from_y[d, at])

        over_tiles(A, body)

    def gather(at, to):
        return copies.send(mean.at[at], mean.at[at], to)

    def x_gather(h):
        return [
            gather(at_x(0, h, 0), east),
            gather(at_x(0, h, 1), west),
            gather(at_x(0, h, 1), east),
            gather(at_x(0, h, 0), west),
        ]

    x_crossed = gather(at_x(0, half, 0, 2), across)
    x_own = x_gather(half)

    q_opened[1].wait_recv()
    add_into(q_first.at[1], y_sum.at[3], 0, B)
    q_east = copies.send(q_first.at[1], q_third.at[1], east)
    q_opened[0].wait_recv()
    add_into(q_first.at[0], y_sum.at[6], 0, B)
    q_west = copies.send(q_first.at[0], q_third.at[0], west)
    q_passed = [q_west, q_east]

    for d in (0, 1):
        y_add(0, d)
        q_opened[2 + d].wait_recv()
        q_passed[d].wait_recv()
        base = at_y(half, 0, d).start

        def body(i, d=d, base=base):
            at = pl.ds(i, STEP)
            store_mean(
                pl.ds(base + i, STEP), y_sum[d, at] + q_second[d, at] + q_third[d, at]
            )

        over_tiles(B, body)

    def norm_send(slots, mine, value, to):
        slots[mine] = value
        return [copies.send(slots.at[mine], slots.at[mine], peer) for peer in to]

    def norm_take(slots, sent):
        for copy in sent:
            copy.wait_recv()
        total = slots[0]
        for i in range(1, slots.shape[0]):
            total = total + slots[i]
        return total

    sent = norm_send(norm_z, z, squares[...], z_peers)
    q_own = [
        gather(at_y(half, 0, 0), east),
        gather(at_y(half, 0, 1), west),
        gather(at_y(half, 0, 1), east),
        gather(at_y(half, 0, 0), west),
    ]
    y_gathered = {}

    def y_gather(chunk, d):
        y_gathered[chunk, d] = gather(at_y(half, chunk, d), across)

    y_gather(0, 0)
    y_gather(0, 1)

    x_own[0].wait_recv()
    x_on = [gather(at_x(3, half, 0), east)]
    x_own[1].wait_recv()
    x_on += [gather(at_x(1, half, 1), west)]
    value = norm_take(norm_z, sent)
    sent = norm_send(norm_core, core, value, [core_peer])

    q_own[0].wait_recv()
    q_on = [gather(at_y(half, 3, 0), east)]
    y_gather(3, 0)
    q_own[1].wait_recv()
    q_on += [gather(at_y(half, 1, 1), west)]
    y_gather(1, 1)
    value = norm_take(norm_core, sent)
    sent = norm_send(norm_x, x, value, x_peers)
    q_own[2].wait_recv()
    y_gather(3, 1)
    q_own[3].wait_recv()
    y_gather(1, 0)
    x_crossed.wait_recv()
    x_far = x_gather(other)
    value = norm_take(norm_x, sent)
    sent = norm_send(norm_y, y, value, y_peers)
    q_on[0].wait_recv()
    y_gather(2, 0)
    q_on[1].wait_recv()
    y_gather(2, 1)
    x_far[0].wait_recv()
    x_far_on = [gather(at_x(3, other, 0), east)]
    x_far[1].wait_recv()
    x_far_on += [gather(at_x(1, other, 1), west)]
    total = norm_take(norm_y, sent)
    norm = jnp.sqrt(jnp.sum(total, keepdims=True) + 1e-06)
    factor = jnp.broadcast_to(
        jnp.minimum(1.0, 0.5 * math.sqrt(entries) / norm), TILE
    )[None]

    loads[1].wait()
    loads[2].wait()

    def update(at):
        start, count = at.start, at.size

        def body(i):
            at = pl.ds(start + i, STEP)
            clipped = factor * mean[at]
            moved = 0.9 * momentum[at] + clipped
            new_momentum[at] = moved
            new_params[at] = params[at] - 0.7 * (clipped + 0.9 * moved)

        over_tiles(count, body)

    update(at_x(0, half, 0, 2))
    update(at_x(3, half, 0))
    update(at_x(1, half, 1))
    x_own[2].wait_recv()
    update(at_x(3, half, 1))
    x_own[3].wait_recv()
    update(at_x(1, half, 0))
    x_on[0].wait_recv()
    update(at_x(2, half, 0))
    x_on[1].wait_recv()
    update(at_x(2, half, 1))
    update(at_x(0, other, 0, 2))
    for chunk in range(4):
        for d in (0, 1):
            update(at_y(half, chunk, d))
    order = ((0, 0), (0, 1), (3, 0), (1, 1), (3, 1), (1, 0))
    for chunk, d in order:
        y_gathered[chunk, d].wait_recv()
        update(at_y(other, chunk, d))
    update(at_x(3, other, 0))
    update(at_x(1, other, 1))
    x_far[2].wait_recv()
    update(at_x(3, other, 1))
    x_far[3].wait_recv()
    update(at_x(1, other, 0))
    for d in (0, 1):
        y_gathered[2, d].wait_recv()
        update(at_y(other, 2, d))
    x_far_on[0].wait_recv()
    update(at_x(2, other, 0))
    x_far_on[1].wait_recv()
    update(at_x(2, other, 1))
    copies.finish()


def store_kernel(params, momentum, params_out, momentum_out, sem):
    cuts = 4
    size = TILES // cuts
    copies = []
    for i in range(cuts):
        for j, (src, dst) in enumerate(((params, params_out), (momentum, momentum_out))):
            at = pl.ds(i * size, size)
            copy = pltpu.make_async_copy(src.at[at], dst.at[at], sem.at[i * 2 + j])
            copy.start()
            copies.append(copy)
    for copy in copies:
        copy.wait()


def per_device(pseudo_grad, params, momentum):
    rows, columns = params.shape
    entries = rows * lax.axis_size("inner") * columns
    f32 = jnp.float32
    near = pltpu.VMEM((TILES, *TILE), f32)
    far = jax.ShapeDtypeStruct((TILES, *TILE), f32)

    def vmem(*lead):
        return pltpu.VMEM((*lead, *TILE), f32)

    results = pl.pallas_call(
        functools.partial(kernel, entries),
        out_shape=[near, near],
        in_specs=[pl.BlockSpec(memory_space=pl.ANY)] * 3,
        out_specs=[pl.BlockSpec(memory_space=pltpu.VMEM)] * 2,
        scratch_shapes=[
            vmem(TILES),
            vmem(TILES),
            vmem(TILES),
            vmem(TILES),
            vmem(2, 2, A),
            vmem(2, 2, A),
            vmem(2, 2, A),
            vmem(2, A),
            vmem(2, A),
            vmem(8, B),
            vmem(2, B),
            vmem(2, B),
            vmem(2, B),
            vmem(),
            vmem(4),
            vmem(2),
            vmem(4),
            vmem(4),
            pltpu.SemaphoreType.DMA((COPIES,)),
            pltpu.SemaphoreType.DMA((COPIES,)),
            pltpu.SemaphoreType.DMA((3,)),
        ],
        compiler_params=pltpu.CompilerParams(
            collective_id=0, has_side_effects=True, vmem_limit_bytes=49 * 2**20
        ),
        name="outer_step",
    )(tiles_of(pseudo_grad[0]), tiles_of(params), tiles_of(momentum))
    results = pl.pallas_call(
        store_kernel,
        out_shape=[far, far],
        in_specs=[pl.BlockSpec(memory_space=pltpu.VMEM)] * 2,
        out_specs=[pl.BlockSpec(memory_space=pl.ANY)] * 2,
        scratch_shapes=[pltpu.SemaphoreType.DMA((8,))],
        compiler_params=pltpu.CompilerParams(vmem_limit_bytes=40 * 2**20),
        name="store",
    )(*results)
    return tuple(block_of(result, rows, columns) for result in results)


def solution(mesh):
    placed = (P("outer", "inner", None), P("inner", None), P("inner", None))
    return jax.shard_map(
        per_device,
        mesh=mesh,
        in_specs=placed,
        out_specs=(P("inner", None), P("inner", None)),
        check_vma=False,
    )
```

```python
import functools
import math

import jax
import jax.numpy as jnp
from jax import lax
from jax.experimental import pallas as pl
from jax.experimental.pallas import tpu as pltpu
from jax.sharding import PartitionSpec as P

MESH = pl.DeviceIdType.MESH
TILE = (8, 128)
TILES = 1024
A = 36
B = 28
STEP = 4
GROUPS = 8


def tiles_of(block):
    rows, columns = block.shape
    cut = block.reshape(rows // 8, 8, columns // 128, 128)
    return cut.transpose(0, 2, 1, 3).reshape(-1, 8, 128)


def block_of(tiles, rows, columns):
    cut = tiles.reshape(rows // 8, columns // 128, 8, 128)
    return cut.transpose(0, 2, 1, 3).reshape(rows, columns)


def over_tiles(count, body):
    def step(i, carry):
        body(pl.multiple_of(i * STEP, STEP))
        return carry

    lax.fori_loop(0, count // STEP, step, 0)


class Copies:
    def __init__(self, send_sem, recv_sem):
        self.send_sem, self.recv_sem, self.all = send_sem, recv_sem, []

    def send(self, src, dst, device):
        number = len(self.all)
        copy = pltpu.make_async_remote_copy(
            src_ref=src,
            dst_ref=dst,
            send_sem=self.send_sem.at[number],
            recv_sem=self.recv_sem.at[number],
            device_id=device,
            device_id_type=MESH,
        )
        copy.start()
        self.all.append(copy)
        return copy

    def finish(self):
        for copy in self.all:
            copy.wait_send()


COPIES = 65


def kernel(
    entries,
    grad_hbm,
    params_hbm,
    momentum_hbm,
    new_params,
    new_momentum,
    grad,
    params,
    momentum,
    mean,
    x_first,
    x_second,
    x_third,
    x_sum,
    x_from_y,
    y_sum,
    q_first,
    q_second,
    q_third,
    squares,
    norm_z,
    norm_core,
    norm_x,
    norm_y,
    send_sem,
    recv_sem,
    load_sem,
    met_sem,
):
    outer, inner = lax.axis_index("outer"), lax.axis_index("inner")
    x, half = lax.rem(outer, 4), lax.div(outer, 4)
    low, z, core = lax.div(inner, 8), lax.rem(lax.div(inner, 2), 4), lax.rem(inner, 2)
    y = half * 2 + low

    def device(x=x, y=y, z=z, core=core):
        return (lax.div(y, 2) * 4 + x, (lax.rem(y, 2) * 4 + z) * 2 + core)

    def ring(at, by):
        return lax.rem(at + by, 4)

    east, west = device(x=ring(x, 1)), device(x=ring(x, 3))
    across = device(y=ring(y, 2))
    x_peers = [device(x=ring(x, k)) for k in (1, 2, 3)]
    y_peers = [device(y=ring(y, k)) for k in (1, 2, 3)]
    z_peers = [device(z=ring(z, k)) for k in (1, 2, 3)]
    core_peer = device(core=1 - core)

    met = [(ring(z, k) > z, device(z=ring(z, k))) for k in (1, 2, 3)]
    met += [(ring(y, k) > y, device(y=ring(y, k))) for k in (1, 3)]
    met += [(core == 0, core_peer)]
    above = sum(jnp.where(later, 1, 0) for later, _ in met)

    barrier = pltpu.get_barrier_semaphore()
    group = [east, west, across]
    for peer in group:
        pl.semaphore_signal(barrier, inc=1, device_id=peer, device_id_type=MESH)
    for later, peer in met:

        @pl.when(later)
        def greet(peer=peer):
            pl.semaphore_signal(barrier, inc=1, device_id=peer, device_id_type=MESH)

    loads = [
        pltpu.make_async_copy(src, dst, load_sem.at[i])
        for i, (src, dst) in enumerate(
            ((grad_hbm, grad), (params_hbm, params), (momentum_hbm, momentum))
        )
    ]
    loads[0].start()
    pl.semaphore_wait(barrier, len(group) + len(met) - above)

    copies = Copies(send_sem, recv_sem)
    other = 1 - half

    def at_x(chunk, h, d, pieces=1):
        return pl.ds(((ring(x, chunk) * 2 + h) * 2 + d) * A, pieces * A)

    def at_y(h, chunk, d):
        return pl.ds(16 * A + ((h * 4 + ring(x, chunk)) * 2 + d) * B, B)

    def x_open(slot, h):
        return [
            copies.send(grad_hbm.at[at_x(2, h, 0)], x_first.at[slot, 0], west),
            copies.send(grad_hbm.at[at_x(2, h, 1)], x_first.at[slot, 1], east),
            copies.send(grad_hbm.at[at_x(1, h, 0)], x_second.at[slot, 0], east),
            copies.send(grad_hbm.at[at_x(3, h, 1)], x_second.at[slot, 1], west),
        ]

    def add_into(ref, term, start, count):
        def body(i):
            ref[pl.ds(i, STEP)] += term[pl.ds(start + i, STEP)]

        over_tiles(count, body)

    def x_pass(slot, h, opened):
        opened[1].wait_recv()
        add_into(x_first.at[slot, 1], grad, at_x(1, h, 1).start, A)
        one = copies.send(x_first.at[slot, 1], x_third.at[slot, 1], east)
        opened[0].wait_recv()
        add_into(x_first.at[slot, 0], grad, at_x(3, h, 0).start, A)
        two = copies.send(x_first.at[slot, 0], x_third.at[slot, 0], west)
        return [two, one]

    y_copies = {}

    def y_open(chunk, d):
        y_copies[chunk, d] = copies.send(
            grad_hbm.at[at_y(other, chunk, d)], y_sum.at[chunk * 2 + d], across
        )

    def y_add(chunk, d):
        y_copies[chunk, d].wait_recv()
        add_into(y_sum.at[chunk * 2 + d], grad, at_y(half, chunk, d).start, B)
        return y_sum.at[chunk * 2 + d]

    opened_a = x_open(0, other)
    y_open(2, 0)
    y_open(2, 1)
    y_open(1, 0)
    for later, peer in met:

        @pl.when(jnp.logical_not(later))
        def answer(peer=peer):
            pl.semaphore_signal(met_sem, inc=1, device_id=peer, device_id_type=MESH)

    loads[1].start()
    loads[2].start()
    loads[0].wait()
    passed_a = x_pass(0, other, opened_a)
    y_open(3, 1)
    opened_b = x_open(1, half)
    y_open(1, 1)
    for d in (0, 1):
        opened_a[2 + d].wait_recv()
        passed_a[d].wait_recv()
        base = at_x(0, other, d).start

        def body(i, d=d, base=base):
            at = pl.ds(i, STEP)
            x_sum[d, at] = (
                grad[pl.ds(base + i, STEP)] + x_second[0, d, at] + x_third[0, d, at]
            )

        over_tiles(A, body)
        crossed = copies.send(x_sum.at[d], x_from_y.at[d], across)
        y_copies["x", d] = crossed
    y_open(3, 0)
    passed_b = x_pass(1, half, opened_b)
    y_open(0, 0)
    y_open(0, 1)
    q_opened = [
        copies.send(y_add(2, 0), q_first.at[0], west),
        copies.send(y_add(2, 1), q_first.at[1], east),
        copies.send(y_add(1, 0), q_second.at[0], east),
        copies.send(y_add(3, 1), q_second.at[1], west),
    ]
    y_add(1, 1)
    y_add(3, 0)

    squares[...] = jnp.zeros(TILE, jnp.float32)

    def store_mean(at, value):
        value = value / jnp.float32(GROUPS)
        mean[at] = value
        squares[...] += jnp.sum(value * value, axis=0)

    for d in (0, 1):
        opened_b[2 + d].wait_recv()
        passed_b[d].wait_recv()
        y_copies["x", d].wait_recv()
        base = at_x(0, half, d).start

        def body(i, d=d, base=base):
            at = pl.ds(i, STEP)
            own = grad[pl.ds(base + i, STEP)] + x_second[1, d, at] + x_third[1, d, at]
            store_mean(pl.ds(base + i, STEP), own + x_from_y[d, at])

        over_tiles(A, body)

    def gather(at, to):
        return copies.send(mean.at[at], mean.at[at], to)

    def x_gather(h):
        return [
            gather(at_x(0, h, 0), east),
            gather(at_x(0, h, 1), west),
            gather(at_x(0, h, 1), east),
            gather(at_x(0, h, 0), west),
        ]

    x_crossed = gather(at_x(0, half, 0, 2), across)
    x_own = x_gather(half)

    q_opened[1].wait_recv()
    add_into(q_first.at[1], y_sum.at[3], 0, B)
    q_east = copies.send(q_first.at[1], q_third.at[1], east)
    q_opened[0].wait_recv()
    add_into(q_first.at[0], y_sum.at[6], 0, B)
    q_west = copies.send(q_first.at[0], q_third.at[0], west)
    q_passed = [q_west, q_east]

    for d in (0, 1):
        y_add(0, d)
        q_opened[2 + d].wait_recv()
        q_passed[d].wait_recv()
        base = at_y(half, 0, d).start

        def body(i, d=d, base=base):
            at = pl.ds(i, STEP)
            store_mean(
                pl.ds(base + i, STEP), y_sum[d, at] + q_second[d, at] + q_third[d, at]
            )

        over_tiles(B, body)

    def norm_send(slots, mine, value, to):
        slots[mine] = value
        return [copies.send(slots.at[mine], slots.at[mine], peer) for peer in to]

    def norm_take(slots, sent):
        for copy in sent:
            copy.wait_recv()
        total = slots[0]
        for i in range(1, slots.shape[0]):
            total = total + slots[i]
        return total

    @pl.when(above > 0)
    def all_met():
        pl.semaphore_wait(met_sem, above)

    sent = norm_send(norm_z, z, squares[...], z_peers)
    q_own = [
        gather(at_y(half, 0, 0), east),
        gather(at_y(half, 0, 1), west),
        gather(at_y(half, 0, 1), east),
        gather(at_y(half, 0, 0), west),
    ]
    y_gathered = {}

    def y_gather(chunk, d):
        y_gathered[chunk, d] = gather(at_y(half, chunk, d), across)

    y_gather(0, 0)
    y_gather(0, 1)

    x_own[0].wait_recv()
    x_on = [gather(at_x(3, half, 0), east)]
    x_own[1].wait_recv()
    x_on += [gather(at_x(1, half, 1), west)]
    value = norm_take(norm_z, sent)
    sent = norm_send(norm_core, core, value, [core_peer])

    q_own[0].wait_recv()
    q_on = [gather(at_y(half, 3, 0), east)]
    y_gather(3, 0)
    q_own[1].wait_recv()
    q_on += [gather(at_y(half, 1, 1), west)]
    y_gather(1, 1)
    value = norm_take(norm_core, sent)
    sent = norm_send(norm_x, x, value, x_peers)
    q_own[2].wait_recv()
    y_gather(3, 1)
    q_own[3].wait_recv()
    y_gather(1, 0)
    x_crossed.wait_recv()
    x_far = x_gather(other)
    value = norm_take(norm_x, sent)
    sent = norm_send(norm_y, y, value, y_peers)
    q_on[0].wait_recv()
    y_gather(2, 0)
    q_on[1].wait_recv()
    y_gather(2, 1)
    x_far[0].wait_recv()
    x_far_on = [gather(at_x(3, other, 0), east)]
    x_far[1].wait_recv()
    x_far_on += [gather(at_x(1, other, 1), west)]
    total = norm_take(norm_y, sent)
    norm = jnp.sqrt(jnp.sum(total, keepdims=True) + 1e-06)
    factor = jnp.broadcast_to(
        jnp.minimum(1.0, 0.5 * math.sqrt(entries) / norm), TILE
    )[None]

    loads[1].wait()
    loads[2].wait()

    def update(at):
        start, count = at.start, at.size

        def body(i):
            at = pl.ds(start + i, STEP)
            clipped = factor * mean[at]
            moved = 0.9 * momentum[at] + clipped
            new_momentum[at] = moved
            new_params[at] = params[at] - 0.7 * (clipped + 0.9 * moved)

        over_tiles(count, body)

    update(at_x(0, half, 0, 2))
    update(at_x(3, half, 0))
    update(at_x(1, half, 1))
    x_own[2].wait_recv()
    update(at_x(3, half, 1))
    x_own[3].wait_recv()
    update(at_x(1, half, 0))
    x_on[0].wait_recv()
    update(at_x(2, half, 0))
    x_on[1].wait_recv()
    update(at_x(2, half, 1))
    update(at_x(0, other, 0, 2))
    for chunk in range(4):
        for d in (0, 1):
            update(at_y(half, chunk, d))
    order = ((0, 0), (0, 1), (3, 0), (1, 1), (3, 1), (1, 0))
    for chunk, d in order:
        y_gathered[chunk, d].wait_recv()
        update(at_y(other, chunk, d))
    update(at_x(3, other, 0))
    update(at_x(1, other, 1))
    x_far[2].wait_recv()
    update(at_x(3, other, 1))
    x_far[3].wait_recv()
    update(at_x(1, other, 0))
    for d in (0, 1):
        y_gathered[2, d].wait_recv()
        update(at_y(other, 2, d))
    x_far_on[0].wait_recv()
    update(at_x(2, other, 0))
    x_far_on[1].wait_recv()
    update(at_x(2, other, 1))
    copies.finish()


def store_kernel(params, momentum, params_out, momentum_out, sem):
    cuts = 4
    size = TILES // cuts
    copies = []
    for i in range(cuts):
        for j, (src, dst) in enumerate(((params, params_out), (momentum, momentum_out))):
            at = pl.ds(i * size, size)
            copy = pltpu.make_async_copy(src.at[at], dst.at[at], sem.at[i * 2 + j])
            copy.start()
            copies.append(copy)
    for copy in copies:
        copy.wait()


def per_device(pseudo_grad, params, momentum):
    rows, columns = params.shape
    entries = rows * lax.axis_size("inner") * columns
    f32 = jnp.float32
    near = pltpu.VMEM((TILES, *TILE), f32)
    far = jax.ShapeDtypeStruct((TILES, *TILE), f32)

    def vmem(*lead):
        return pltpu.VMEM((*lead, *TILE), f32)

    results = pl.pallas_call(
        functools.partial(kernel, entries),
        out_shape=[near, near],
        in_specs=[pl.BlockSpec(memory_space=pl.ANY)] * 3,
        out_specs=[pl.BlockSpec(memory_space=pltpu.VMEM)] * 2,
        scratch_shapes=[
            vmem(TILES),
            vmem(TILES),
            vmem(TILES),
            vmem(TILES),
            vmem(2, 2, A),
            vmem(2, 2, A),
            vmem(2, 2, A),
            vmem(2, A),
            vmem(2, A),
            vmem(8, B),
            vmem(2, B),
            vmem(2, B),
            vmem(2, B),
            vmem(),
            vmem(4),
            vmem(2),
            vmem(4),
            vmem(4),
            pltpu.SemaphoreType.DMA((COPIES,)),
            pltpu.SemaphoreType.DMA((COPIES,)),
            pltpu.SemaphoreType.DMA((3,)),
            pltpu.SemaphoreType.REGULAR,
        ],
        compiler_params=pltpu.CompilerParams(
            collective_id=0, has_side_effects=True, vmem_limit_bytes=49 * 2**20
        ),
        name="outer_step",
    )(tiles_of(pseudo_grad[0]), tiles_of(params), tiles_of(momentum))
    results = pl.pallas_call(
        store_kernel,
        out_shape=[far, far],
        in_specs=[pl.BlockSpec(memory_space=pltpu.VMEM)] * 2,
        out_specs=[pl.BlockSpec(memory_space=pl.ANY)] * 2,
        scratch_shapes=[pltpu.SemaphoreType.DMA((8,))],
        compiler_params=pltpu.CompilerParams(vmem_limit_bytes=40 * 2**20),
        name="store",
    )(*results)
    return tuple(block_of(result, rows, columns) for result in results)


def solution(mesh):
    placed = (P("outer", "inner", None), P("inner", None), P("inner", None))
    return jax.shard_map(
        per_device,
        mesh=mesh,
        in_specs=placed,
        out_specs=(P("inner", None), P("inner", None)),
        check_vma=False,
    )
```

```python
import functools
import math

import jax
import jax.numpy as jnp
from jax import lax
from jax.experimental import pallas as pl
from jax.experimental.pallas import tpu as pltpu
from jax.sharding import PartitionSpec as P

MESH = pl.DeviceIdType.MESH
TILE = (8, 128)
TILES = 1024
A = 36
B = 28
STEP = 4
GROUPS = 8


def tiles_of(block):
    rows, columns = block.shape
    cut = block.reshape(rows // 8, 8, columns // 128, 128)
    return cut.transpose(0, 2, 1, 3).reshape(-1, 8, 128)


def block_of(tiles, rows, columns):
    cut = tiles.reshape(rows // 8, columns // 128, 8, 128)
    return cut.transpose(0, 2, 1, 3).reshape(rows, columns)


def over_tiles(count, body):
    def step(i, carry):
        body(pl.multiple_of(i * STEP, STEP))
        return carry

    lax.fori_loop(0, count // STEP, step, 0)


class Copies:
    def __init__(self, send_sem, recv_sem):
        self.send_sem, self.recv_sem, self.all = send_sem, recv_sem, []

    def send(self, src, dst, device):
        number = len(self.all)
        copy = pltpu.make_async_remote_copy(
            src_ref=src,
            dst_ref=dst,
            send_sem=self.send_sem.at[number],
            recv_sem=self.recv_sem.at[number],
            device_id=device,
            device_id_type=MESH,
        )
        copy.start()
        self.all.append(copy)
        return copy

    def finish(self):
        for copy in self.all:
            copy.wait_send()


COPIES = 65


def kernel(
    entries,
    grad_hbm,
    params_hbm,
    momentum_hbm,
    new_params,
    new_momentum,
    grad,
    params,
    momentum,
    mean,
    x_first,
    x_second,
    x_third,
    x_sum,
    x_from_y,
    y_sum,
    q_first,
    q_second,
    q_third,
    squares,
    norm_z,
    norm_core,
    norm_x,
    norm_y,
    send_sem,
    recv_sem,
    load_sem,
    met_sem,
):
    outer, inner = lax.axis_index("outer"), lax.axis_index("inner")
    x, half = lax.rem(outer, 4), lax.div(outer, 4)
    low, z, core = lax.div(inner, 8), lax.rem(lax.div(inner, 2), 4), lax.rem(inner, 2)
    y = half * 2 + low

    def device(x=x, y=y, z=z, core=core):
        return (lax.div(y, 2) * 4 + x, (lax.rem(y, 2) * 4 + z) * 2 + core)

    def ring(at, by):
        return lax.rem(at + by, 4)

    east, west = device(x=ring(x, 1)), device(x=ring(x, 3))
    across = device(y=ring(y, 2))
    x_peers = [device(x=ring(x, k)) for k in (1, 2, 3)]
    y_peers = [device(y=ring(y, k)) for k in (1, 2, 3)]
    z_peers = [device(z=ring(z, k)) for k in (1, 2, 3)]
    core_peer = device(core=1 - core)

    met = [(ring(z, k) > z, device(z=ring(z, k))) for k in (1, 2, 3)]
    met += [(ring(y, k) > y, device(y=ring(y, k))) for k in (1, 3)]
    met += [(core == 0, core_peer)]
    above = sum(jnp.where(later, 1, 0) for later, _ in met)

    barrier = pltpu.get_barrier_semaphore()
    group = [east, west, across]
    for peer in group:
        pl.semaphore_signal(barrier, inc=1, device_id=peer, device_id_type=MESH)
    for later, peer in met:

        @pl.when(later)
        def greet(peer=peer):
            pl.semaphore_signal(barrier, inc=1, device_id=peer, device_id_type=MESH)

    loads = [
        pltpu.make_async_copy(src, dst, load_sem.at[i])
        for i, (src, dst) in enumerate(
            ((grad_hbm, grad), (params_hbm, params), (momentum_hbm, momentum))
        )
    ]
    loads[0].start()
    pl.semaphore_wait(barrier, len(group) + len(met) - above)

    copies = Copies(send_sem, recv_sem)
    other = 1 - half

    def at_x(chunk, h, d, pieces=1):
        return pl.ds(((ring(x, chunk) * 2 + h) * 2 + d) * A, pieces * A)

    def at_y(h, chunk, d):
        return pl.ds(16 * A + ((h * 4 + ring(x, chunk)) * 2 + d) * B, B)

    def x_open(slot, h):
        return [
            copies.send(grad_hbm.at[at_x(2, h, 0)], x_first.at[slot, 0], west),
            copies.send(grad_hbm.at[at_x(2, h, 1)], x_first.at[slot, 1], east),
            copies.send(grad_hbm.at[at_x(1, h, 0)], x_second.at[slot, 0], east),
            copies.send(grad_hbm.at[at_x(3, h, 1)], x_second.at[slot, 1], west),
        ]

    def add_into(ref, term, start, count):
        def body(i):
            ref[pl.ds(i, STEP)] += term[pl.ds(start + i, STEP)]

        over_tiles(count, body)

    y_copies = {}

    def y_open(chunk, d):
        y_copies[chunk, d] = copies.send(
            grad_hbm.at[at_y(other, chunk, d)], y_sum.at[chunk * 2 + d], across
        )

    def y_add(chunk, d):
        y_copies[chunk, d].wait_recv()
        add_into(y_sum.at[chunk * 2 + d], grad, at_y(half, chunk, d).start, B)
        return y_sum.at[chunk * 2 + d]

    a_west, a_east, a_near_east, a_near_west = x_open(0, other)
    for chunk, d in ((2, 0), (2, 1), (1, 0), (3, 1), (1, 1), (3, 0), (0, 0), (0, 1)):
        y_open(chunk, d)
    for later, peer in met:

        @pl.when(jnp.logical_not(later))
        def answer(peer=peer):
            pl.semaphore_signal(met_sem, inc=1, device_id=peer, device_id_type=MESH)

    loads[1].start()
    loads[2].start()
    loads[0].wait()

    def pass_on(arrived, slot, start, to, land, term=grad, count=A):
        arrived.wait_recv()
        add_into(slot, term, start, count)
        return copies.send(slot, land, to)

    def x_pass(slot, h, to_east, to_west):
        one = pass_on(
            to_east, x_first.at[slot, 1], at_x(1, h, 1).start, east, x_third.at[slot, 1]
        )
        two = pass_on(
            to_west, x_first.at[slot, 0], at_x(3, h, 0).start, west, x_third.at[slot, 0]
        )
        return [two, one]

    a_passed = x_pass(0, other, a_east, a_west)
    q_west = copies.send(y_add(2, 0), q_first.at[0], west)
    q_east = copies.send(y_add(2, 1), q_first.at[1], east)
    b_west = copies.send(grad_hbm.at[at_x(2, half, 0)], x_first.at[1, 0], west)
    b_east = copies.send(grad_hbm.at[at_x(2, half, 1)], x_first.at[1, 1], east)
    for d, near in ((0, a_near_east), (1, a_near_west)):
        near.wait_recv()
        a_passed[d].wait_recv()
        base = at_x(0, other, d).start

        def body(i, d=d, base=base):
            at = pl.ds(i, STEP)
            x_sum[d, at] = (
                grad[pl.ds(base + i, STEP)] + x_second[0, d, at] + x_third[0, d, at]
            )

        over_tiles(A, body)
        y_copies["x", d] = copies.send(x_sum.at[d], x_from_y.at[d], across)
    q_near = [
        copies.send(y_add(1, 0), q_second.at[0], east),
        copies.send(y_add(3, 1), q_second.at[1], west),
    ]
    b_near = [
        copies.send(grad_hbm.at[at_x(1, half, 0)], x_second.at[1, 0], east),
        copies.send(grad_hbm.at[at_x(3, half, 1)], x_second.at[1, 1], west),
    ]
    y_add(1, 1)
    q_on_east = pass_on(q_east, q_first.at[1], 0, east, q_third.at[1], y_sum.at[3], B)
    y_add(3, 0)
    q_on_west = pass_on(q_west, q_first.at[0], 0, west, q_third.at[0], y_sum.at[6], B)
    b_passed = x_pass(1, half, b_east, b_west)

    squares[...] = jnp.zeros(TILE, jnp.float32)

    def store_mean(at, value):
        value = value / jnp.float32(GROUPS)
        mean[at] = value
        squares[...] += jnp.sum(value * value, axis=0)

    for d, passed in ((0, q_on_west), (1, q_on_east)):
        y_add(0, d)
        q_near[d].wait_recv()
        passed.wait_recv()
        base = at_y(half, 0, d).start

        def body(i, d=d, base=base):
            at = pl.ds(i, STEP)
            store_mean(
                pl.ds(base + i, STEP), y_sum[d, at] + q_second[d, at] + q_third[d, at]
            )

        over_tiles(B, body)

    def gather(at, to):
        return copies.send(mean.at[at], mean.at[at], to)

    def x_gather(h):
        return [
            gather(at_x(0, h, 0), east),
            gather(at_x(0, h, 1), west),
            gather(at_x(0, h, 1), east),
            gather(at_x(0, h, 0), west),
        ]

    q_own = [
        gather(at_y(half, 0, 0), east),
        gather(at_y(half, 0, 1), west),
        gather(at_y(half, 0, 1), east),
        gather(at_y(half, 0, 0), west),
    ]
    y_gathered = {}

    def y_gather(chunk, d):
        y_gathered[chunk, d] = gather(at_y(half, chunk, d), across)

    y_gather(0, 0)
    y_gather(0, 1)

    for d in (0, 1):
        b_near[d].wait_recv()
        b_passed[d].wait_recv()
        y_copies["x", d].wait_recv()
        base = at_x(0, half, d).start

        def body(i, d=d, base=base):
            at = pl.ds(i, STEP)
            own = grad[pl.ds(base + i, STEP)] + x_second[1, d, at] + x_third[1, d, at]
            store_mean(pl.ds(base + i, STEP), own + x_from_y[d, at])

        over_tiles(A, body)

    x_own = x_gather(half)
    x_crossed = gather(at_x(0, half, 0, 2), across)

    def norm_send(slots, mine, value, to):
        slots[mine] = value
        return [copies.send(slots.at[mine], slots.at[mine], peer) for peer in to]

    def norm_take(slots, sent):
        for copy in sent:
            copy.wait_recv()
        total = slots[0]
        for i in range(1, slots.shape[0]):
            total = total + slots[i]
        return total

    @pl.when(above > 0)
    def all_met():
        pl.semaphore_wait(met_sem, above)

    sent = norm_send(norm_z, z, squares[...], z_peers)

    q_own[0].wait_recv()
    q_on = [gather(at_y(half, 3, 0), east)]
    y_gather(3, 0)
    q_own[1].wait_recv()
    q_on += [gather(at_y(half, 1, 1), west)]
    y_gather(1, 1)
    value = norm_take(norm_z, sent)
    sent = norm_send(norm_core, core, value, [core_peer])
    q_own[2].wait_recv()
    y_gather(3, 1)
    q_own[3].wait_recv()
    y_gather(1, 0)
    value = norm_take(norm_core, sent)
    sent = norm_send(norm_x, x, value, x_peers)
    x_own[0].wait_recv()
    x_on = [gather(at_x(3, half, 0), east)]
    x_own[1].wait_recv()
    x_on += [gather(at_x(1, half, 1), west)]
    x_crossed.wait_recv()
    x_far = x_gather(other)
    value = norm_take(norm_x, sent)
    sent = norm_send(norm_y, y, value, y_peers)
    q_on[0].wait_recv()
    y_gather(2, 0)
    q_on[1].wait_recv()
    y_gather(2, 1)
    x_far[0].wait_recv()
    x_far_on = [gather(at_x(3, other, 0), east)]
    x_far[1].wait_recv()
    x_far_on += [gather(at_x(1, other, 1), west)]
    total = norm_take(norm_y, sent)
    norm = jnp.sqrt(jnp.sum(total, keepdims=True) + 1e-06)
    factor = jnp.broadcast_to(
        jnp.minimum(1.0, 0.5 * math.sqrt(entries) / norm), TILE
    )[None]

    loads[1].wait()
    loads[2].wait()

    def update(at):
        start, count = at.start, at.size

        def body(i):
            at = pl.ds(start + i, STEP)
            clipped = factor * mean[at]
            moved = 0.9 * momentum[at] + clipped
            new_momentum[at] = moved
            new_params[at] = params[at] - 0.7 * (clipped + 0.9 * moved)

        over_tiles(count, body)

    update(at_x(0, half, 0, 2))
    update(at_x(3, half, 0))
    update(at_x(1, half, 1))
    x_own[2].wait_recv()
    update(at_x(3, half, 1))
    x_own[3].wait_recv()
    update(at_x(1, half, 0))
    x_on[0].wait_recv()
    update(at_x(2, half, 0))
    x_on[1].wait_recv()
    update(at_x(2, half, 1))
    update(at_x(0, other, 0, 2))
    for chunk in range(4):
        for d in (0, 1):
            update(at_y(half, chunk, d))
    order = ((0, 0), (0, 1), (3, 0), (1, 1), (3, 1), (1, 0))
    for chunk, d in order:
        y_gathered[chunk, d].wait_recv()
        update(at_y(other, chunk, d))
    update(at_x(3, other, 0))
    update(at_x(1, other, 1))
    x_far[2].wait_recv()
    update(at_x(3, other, 1))
    x_far[3].wait_recv()
    update(at_x(1, other, 0))
    for d in (0, 1):
        y_gathered[2, d].wait_recv()
        update(at_y(other, 2, d))
    x_far_on[0].wait_recv()
    update(at_x(2, other, 0))
    x_far_on[1].wait_recv()
    update(at_x(2, other, 1))
    copies.finish()


def store_kernel(params, momentum, params_out, momentum_out, sem):
    cuts = 4
    size = TILES // cuts
    copies = []
    for i in range(cuts):
        for j, (src, dst) in enumerate(((params, params_out), (momentum, momentum_out))):
            at = pl.ds(i * size, size)
            copy = pltpu.make_async_copy(src.at[at], dst.at[at], sem.at[i * 2 + j])
            copy.start()
            copies.append(copy)
    for copy in copies:
        copy.wait()


def per_device(pseudo_grad, params, momentum):
    rows, columns = params.shape
    entries = rows * lax.axis_size("inner") * columns
    f32 = jnp.float32
    near = pltpu.VMEM((TILES, *TILE), f32)
    far = jax.ShapeDtypeStruct((TILES, *TILE), f32)

    def vmem(*lead):
        return pltpu.VMEM((*lead, *TILE), f32)

    results = pl.pallas_call(
        functools.partial(kernel, entries),
        out_shape=[near, near],
        in_specs=[pl.BlockSpec(memory_space=pl.ANY)] * 3,
        out_specs=[pl.BlockSpec(memory_space=pltpu.VMEM)] * 2,
        scratch_shapes=[
            vmem(TILES),
            vmem(TILES),
            vmem(TILES),
            vmem(TILES),
            vmem(2, 2, A),
            vmem(2, 2, A),
            vmem(2, 2, A),
            vmem(2, A),
            vmem(2, A),
            vmem(8, B),
            vmem(2, B),
            vmem(2, B),
            vmem(2, B),
            vmem(),
            vmem(4),
            vmem(2),
            vmem(4),
            vmem(4),
            pltpu.SemaphoreType.DMA((COPIES,)),
            pltpu.SemaphoreType.DMA((COPIES,)),
            pltpu.SemaphoreType.DMA((3,)),
            pltpu.SemaphoreType.REGULAR,
        ],
        compiler_params=pltpu.CompilerParams(
            collective_id=0, has_side_effects=True, vmem_limit_bytes=49 * 2**20
        ),
        name="outer_step",
    )(tiles_of(pseudo_grad[0]), tiles_of(params), tiles_of(momentum))
    results = pl.pallas_call(
        store_kernel,
        out_shape=[far, far],
        in_specs=[pl.BlockSpec(memory_space=pltpu.VMEM)] * 2,
        out_specs=[pl.BlockSpec(memory_space=pl.ANY)] * 2,
        scratch_shapes=[pltpu.SemaphoreType.DMA((8,))],
        compiler_params=pltpu.CompilerParams(vmem_limit_bytes=40 * 2**20),
        name="store",
    )(*results)
    return tuple(block_of(result, rows, columns) for result in results)


def solution(mesh):
    placed = (P("outer", "inner", None), P("inner", None), P("inner", None))
    return jax.shard_map(
        per_device,
        mesh=mesh,
        in_specs=placed,
        out_specs=(P("inner", None), P("inner", None)),
        check_vma=False,
    )
```

```python
import functools
import math

import jax
import jax.numpy as jnp
from jax import lax
from jax.experimental import pallas as pl
from jax.experimental.pallas import tpu as pltpu
from jax.sharding import PartitionSpec as P

MESH = pl.DeviceIdType.MESH
TILE = (8, 128)
TILES = 1024
A = 36
B = 28
STEP = 4
FIRST, REST = pl.ds(0, 16), pl.ds(16, A - 16)
GROUPS = 8


def tiles_of(block):
    rows, columns = block.shape
    cut = block.reshape(rows // 8, 8, columns // 128, 128)
    return cut.transpose(0, 2, 1, 3).reshape(-1, 8, 128)


def block_of(tiles, rows, columns):
    cut = tiles.reshape(rows // 8, columns // 128, 8, 128)
    return cut.transpose(0, 2, 1, 3).reshape(rows, columns)


def over_tiles(count, body):
    def step(i, carry):
        body(pl.multiple_of(i * STEP, STEP))
        return carry

    lax.fori_loop(0, count // STEP, step, 0)


class Copies:
    def __init__(self, send_sem, recv_sem, any_tiles):
        self.send_sem, self.recv_sem, self.any_tiles = send_sem, recv_sem, any_tiles
        self.groups, self.sent = 0, {}

    def group(self):
        self.groups += 1
        return Group(self, self.recv_sem.at[self.groups - 1])

    def wait(self, tiles, send=None, recv=None):
        some = self.any_tiles.at[pl.ds(0, tiles)]
        copy = pltpu.make_async_remote_copy(
            src_ref=some,
            dst_ref=some,
            send_sem=self.send_sem.at[0] if send is None else send,
            recv_sem=self.recv_sem.at[0] if recv is None else recv,
            device_id=self.anyone,
            device_id_type=MESH,
        )
        if recv is None:
            copy.wait_send()
        else:
            copy.wait_recv()

    def finish(self):
        for number, tiles in self.sent.items():
            self.wait(tiles, send=self.send_sem.at[number])


class Group:
    def __init__(self, copies, sem):
        self.copies, self.sem, self.tiles = copies, sem, 0

    def send(self, src, dst, to):
        number, device = to
        tiles = math.prod(src.shape) // math.prod(TILE)
        pltpu.make_async_remote_copy(
            src_ref=src,
            dst_ref=dst,
            send_sem=self.copies.send_sem.at[number],
            recv_sem=self.sem,
            device_id=device,
            device_id_type=MESH,
        ).start()
        self.tiles += tiles
        self.copies.sent[number] = self.copies.sent.get(number, 0) + tiles

    def wait(self):
        self.copies.wait(self.tiles, recv=self.sem)


GROUPS_OF_COPIES = 33


def kernel(
    entries,
    grad_hbm,
    params_hbm,
    momentum_hbm,
    new_params,
    new_momentum,
    grad,
    params,
    momentum,
    mean,
    x_first,
    x_second,
    x_third,
    x_sum,
    x_from_y,
    y_sum,
    q_first,
    q_second,
    q_third,
    squares,
    norm_z,
    norm_core,
    norm_x,
    norm_y,
    send_sem,
    recv_sem,
    load_sem,
    met_sem,
):
    outer, inner = lax.axis_index("outer"), lax.axis_index("inner")
    x, half = lax.rem(outer, 4), lax.div(outer, 4)
    low, z, core = lax.div(inner, 8), lax.rem(lax.div(inner, 2), 4), lax.rem(inner, 2)
    y = half * 2 + low

    def device(x=x, y=y, z=z, core=core):
        return (lax.div(y, 2) * 4 + x, (lax.rem(y, 2) * 4 + z) * 2 + core)

    def ring(at, by):
        return lax.rem(at + by, 4)

    east, west, across = [
        (0, device(x=ring(x, 1))),
        (1, device(x=ring(x, 3))),
        (2, device(y=ring(y, 2))),
    ]
    x_peers = [(3, device(x=ring(x, k))) for k in (1, 2, 3)]
    y_peers = [(3, device(y=ring(y, k))) for k in (1, 2, 3)]
    z_peers = [(3, device(z=ring(z, k))) for k in (1, 2, 3)]
    core_peer = (3, device(core=1 - core))

    met = [(ring(z, k) > z, device(z=ring(z, k))) for k in (1, 2, 3)]
    met += [(ring(y, k) > y, device(y=ring(y, k))) for k in (1, 3)]
    met += [(core == 0, core_peer[1])]
    above = sum(jnp.where(later, 1, 0) for later, _ in met)

    barrier = pltpu.get_barrier_semaphore()
    group = [east, west, across]
    for _, peer in group:
        pl.semaphore_signal(barrier, inc=1, device_id=peer, device_id_type=MESH)
    for later, peer in met:

        @pl.when(later)
        def greet(peer=peer):
            pl.semaphore_signal(barrier, inc=1, device_id=peer, device_id_type=MESH)

    loads = [
        pltpu.make_async_copy(src, dst, load_sem.at[i])
        for i, (src, dst) in enumerate(
            ((grad_hbm, grad), (params_hbm, params), (momentum_hbm, momentum))
        )
    ]
    loads[0].start()
    pl.semaphore_wait(barrier, len(group) + len(met) - above)

    copies = Copies(send_sem, recv_sem, mean)
    copies.anyone = east[1]
    other = 1 - half

    def at_x(chunk, h, d, pieces=1):
        return pl.ds(((ring(x, chunk) * 2 + h) * 2 + d) * A, pieces * A)

    def at_y(h, chunk, d, pieces=1):
        return pl.ds(16 * A + ((h * 4 + ring(x, chunk)) * 2 + d) * B, pieces * B)

    a_west, a_east, a_rest = copies.group(), copies.group(), copies.group()
    b_west, b_east, b_rest = copies.group(), copies.group(), copies.group()
    q_west, q_east, q_rest = copies.group(), copies.group(), copies.group()
    y_first = {(chunk, d): copies.group() for chunk, d in ((2, 0), (1, 0), (3, 1), (1, 1), (3, 0))}

    def x_open(group, chunk, h, d, land, to, cut=None):
        at = at_x(chunk, h, d)
        if cut is not None:
            at, land = cut_of(at, cut), land.at[cut]
        group.send(grad_hbm.at[at], land, to)

    def y_open(group, chunk, d, pieces=1):
        group.send(
            grad_hbm.at[at_y(other, chunk, d, pieces)],
            y_sum.at[chunk, pl.ds(d * B, pieces * B)],
            across,
        )

    def cut_of(at, cut):
        return pl.ds(at.start + cut.start, cut.size)

    def add_into(ref, term, start, count):
        def body(i):
            ref[pl.ds(i, STEP)] += term[pl.ds(start + i, STEP)]

        over_tiles(count, body)

    def y_add(chunk, d, pieces=1):
        piece = y_sum.at[chunk, pl.ds(d * B, pieces * B)]
        add_into(piece, grad, at_y(half, chunk, d).start, pieces * B)
        return piece

    x_open(a_west, 2, other, 0, x_first.at[0, 0], west)
    x_open(a_east, 2, other, 1, x_first.at[0, 1], east)
    x_open(a_rest, 1, other, 0, x_second.at[0, 0], east)
    x_open(a_rest, 3, other, 1, x_second.at[0, 1], west)
    y_open(y_first[2, 0], 2, 0, 2)
    x_open(b_west, 2, half, 0, x_first.at[1, 0], west)
    x_open(b_east, 2, half, 1, x_first.at[1, 1], east)
    for chunk, d in ((1, 0), (3, 1), (1, 1), (3, 0)):
        y_open(y_first[chunk, d], chunk, d)
    y_open(q_rest, 0, 0, 2)
    for later, peer in met:

        @pl.when(jnp.logical_not(later))
        def answer(peer=peer):
            pl.semaphore_signal(met_sem, inc=1, device_id=peer, device_id_type=MESH)

    loads[1].start()
    loads[2].start()
    loads[0].wait()

    def pass_on(arrived, rest, ref, land, to, term, start, count):
        arrived.wait()
        add_into(ref, term, start, count)
        rest.send(ref, land, to)

    def x_pass(slot, h, from_east, from_west, rest):
        for arrived, d, chunk, to in ((from_west, 1, 1, east), (from_east, 0, 3, west)):
            pass_on(
                arrived,
                rest,
                x_first.at[slot, d],
                x_third.at[slot, d],
                to,
                grad,
                at_x(chunk, h, d).start,
                A,
            )

    x_pass(0, other, a_west, a_east, a_rest)
    y_first[2, 0].wait()
    y_add(2, 0, 2)
    q_west.send(y_sum.at[2, pl.ds(0, B)], q_first.at[0], west)
    q_east.send(y_sum.at[2, pl.ds(B, B)], q_first.at[1], east)
    y_first[1, 0].wait()
    q_rest.send(y_add(1, 0), q_second.at[0], east)
    y_first[3, 1].wait()
    q_rest.send(y_add(3, 1), q_second.at[1], west)
    a_rest.wait()
    for d in (0, 1):
        base = at_x(0, other, d).start

        def body(i, d=d, base=base):
            x_sum[pl.ds(d * A + i, STEP)] = (
                grad[pl.ds(base + i, STEP)]
                + x_second[0, d, pl.ds(i, STEP)]
                + x_third[0, d, pl.ds(i, STEP)]
            )

        over_tiles(A, body)
    b_rest.send(x_sum, x_from_y, across)
    x_open(b_rest, 1, half, 0, x_second.at[1, 0], east, FIRST)
    x_open(b_rest, 3, half, 1, x_second.at[1, 1], west, FIRST)
    y_first[1, 1].wait()
    y_add(1, 1)
    pass_on(q_east, q_rest, q_first.at[1], q_third.at[1], east, y_sum.at[1], B, B)
    y_first[3, 0].wait()
    y_add(3, 0)
    pass_on(q_west, q_rest, q_first.at[0], q_third.at[0], west, y_sum.at[3], 0, B)
    x_open(b_rest, 1, half, 0, x_second.at[1, 0], east, REST)
    x_open(b_rest, 3, half, 1, x_second.at[1, 1], west, REST)
    x_pass(1, half, b_west, b_east, b_rest)

    squares[...] = jnp.zeros(TILE, jnp.float32)

    def store_mean(at, value):
        value = value / jnp.float32(GROUPS)
        mean[at] = value
        squares[...] += jnp.sum(value * value, axis=0)

    q_rest.wait()
    y_add(0, 0, 2)
    for d in (0, 1):
        base = at_y(half, 0, d).start

        def body(i, d=d, base=base):
            at = pl.ds(i, STEP)
            store_mean(
                pl.ds(base + i, STEP),
                y_sum[0, pl.ds(d * B + i, STEP)] + q_second[d, at] + q_third[d, at],
            )

        over_tiles(B, body)

    def gather(group, at, to):
        group.send(mean.at[at], mean.at[at], to)

    q_from_west, q_from_east, q_far = copies.group(), copies.group(), copies.group()
    x_from_west, x_from_east, crossed = copies.group(), copies.group(), copies.group()
    x_cuts = [(cut, copies.group(), copies.group()) for cut in (FIRST, REST)]
    early, late, last_first, last_rest, last_y = [copies.group() for _ in range(5)]

    gather(q_from_west, at_y(half, 0, 0, 2), east)
    gather(q_from_east, at_y(half, 0, 0, 2), west)
    gather(early, at_y(half, 0, 0, 2), across)

    b_rest.wait()
    for d in (0, 1):
        base = at_x(0, half, d).start

        def body(i, d=d, base=base):
            at = pl.ds(i, STEP)
            own = grad[pl.ds(base + i, STEP)] + x_second[1, d, at] + x_third[1, d, at]
            store_mean(pl.ds(base + i, STEP), own + x_from_y[pl.ds(d * A + i, STEP)])

        over_tiles(A, body)

    gather(x_from_west, at_x(0, half, 0), east)
    gather(x_from_east, at_x(0, half, 1), west)
    gather(early, at_x(0, half, 1), east)
    gather(early, at_x(0, half, 0), west)
    gather(crossed, at_x(0, half, 0, 2), across)

    def norm_send(slots, mine, value, to):
        group = copies.group()
        slots[mine] = value
        for peer in to:
            group.send(slots.at[mine], slots.at[mine], peer)
        return group

    def norm_take(slots, group):
        group.wait()
        total = slots[0]
        for i in range(1, slots.shape[0]):
            total = total + slots[i]
        return total

    @pl.when(above > 0)
    def all_met():
        pl.semaphore_wait(met_sem, above)

    sent = norm_send(norm_z, z, squares[...], z_peers)

    q_from_west.wait()
    gather(q_far, at_y(half, 3, 0), east)
    gather(early, at_y(half, 3, 0, 2), across)
    q_from_east.wait()
    gather(q_far, at_y(half, 1, 1), west)
    gather(early, at_y(half, 1, 0, 2), across)
    value = norm_take(norm_z, sent)
    sent = norm_send(norm_core, core, value, [core_peer])
    value = norm_take(norm_core, sent)
    sent = norm_send(norm_x, x, value, x_peers)
    x_from_west.wait()
    gather(early, at_x(3, half, 0), east)
    x_from_east.wait()
    gather(early, at_x(1, half, 1), west)
    crossed.wait()
    for cut, from_west, from_east in x_cuts:
        gather(from_west, cut_of(at_x(0, other, 0), cut), east)
        gather(from_east, cut_of(at_x(0, other, 1), cut), west)
    gather(late, at_x(0, other, 1), east)
    gather(late, at_x(0, other, 0), west)
    value = norm_take(norm_x, sent)
    sent = norm_send(norm_y, y, value, y_peers)
    q_far.wait()
    gather(last_y, at_y(half, 2, 0, 2), across)
    for (cut, from_west, from_east), last in zip(x_cuts, (last_first, last_rest)):
        from_west.wait()
        gather(last, cut_of(at_x(3, other, 0), cut), east)
        from_east.wait()
        gather(last, cut_of(at_x(1, other, 1), cut), west)
    total = norm_take(norm_y, sent)
    norm = jnp.sqrt(jnp.sum(total, keepdims=True) + 1e-06)
    factor = jnp.broadcast_to(
        jnp.minimum(1.0, 0.5 * math.sqrt(entries) / norm), TILE
    )[None]

    loads[1].wait()
    loads[2].wait()

    def update(at):
        start, count = at.start, at.size

        def body(i):
            at = pl.ds(start + i, STEP)
            clipped = factor * mean[at]
            moved = 0.9 * momentum[at] + clipped
            new_momentum[at] = moved
            new_params[at] = params[at] - 0.7 * (clipped + 0.9 * moved)

        over_tiles(count, body)

    update(at_x(0, half, 0, 2))
    update(at_x(3, half, 0))
    update(at_x(1, half, 1))
    for chunk in range(4):
        update(at_y(half, chunk, 0, 2))
    update(at_x(0, other, 0, 2))
    update(at_x(3, other, 0))
    update(at_x(1, other, 1))
    early.wait()
    update(at_x(3, half, 1))
    update(at_x(1, half, 0))
    update(at_x(2, half, 0, 2))
    for chunk in (0, 3, 1):
        update(at_y(other, chunk, 0, 2))
    late.wait()
    update(at_x(3, other, 1))
    update(at_x(1, other, 0))
    last_first.wait()
    update(cut_of(at_x(2, other, 0), FIRST))
    update(cut_of(at_x(2, other, 1), FIRST))
    last_y.wait()
    update(at_y(other, 2, 0, 2))
    last_rest.wait()
    update(cut_of(at_x(2, other, 0), REST))
    update(cut_of(at_x(2, other, 1), REST))
    copies.finish()
    assert copies.groups == GROUPS_OF_COPIES, copies.groups


def store_kernel(params, momentum, params_out, momentum_out, sem):
    cuts = 1
    size = TILES // cuts
    copies = []
    for i in range(cuts):
        for j, (src, dst) in enumerate(((params, params_out), (momentum, momentum_out))):
            at = pl.ds(i * size, size)
            copy = pltpu.make_async_copy(src.at[at], dst.at[at], sem.at[i * 2 + j])
            copy.start()
            copies.append(copy)
    for copy in copies:
        copy.wait()


def per_device(pseudo_grad, params, momentum):
    rows, columns = params.shape
    entries = rows * lax.axis_size("inner") * columns
    f32 = jnp.float32
    near = pltpu.VMEM((TILES, *TILE), f32)
    far = jax.ShapeDtypeStruct((TILES, *TILE), f32)

    def vmem(*lead):
        return pltpu.VMEM((*lead, *TILE), f32)

    results = pl.pallas_call(
        functools.partial(kernel, entries),
        out_shape=[near, near],
        in_specs=[pl.BlockSpec(memory_space=pl.ANY)] * 3,
        out_specs=[pl.BlockSpec(memory_space=pltpu.VMEM)] * 2,
        scratch_shapes=[
            vmem(TILES),
            vmem(TILES),
            vmem(TILES),
            vmem(TILES),
            vmem(2, 2, A),
            vmem(2, 2, A),
            vmem(2, 2, A),
            vmem(2 * A),
            vmem(2 * A),
            vmem(4, 2 * B),
            vmem(2, B),
            vmem(2, B),
            vmem(2, B),
            vmem(),
            vmem(4),
            vmem(2),
            vmem(4),
            vmem(4),
            pltpu.SemaphoreType.DMA((4,)),
            pltpu.SemaphoreType.DMA((GROUPS_OF_COPIES,)),
            pltpu.SemaphoreType.DMA((3,)),
            pltpu.SemaphoreType.REGULAR,
        ],
        compiler_params=pltpu.CompilerParams(
            collective_id=0, has_side_effects=True, vmem_limit_bytes=49 * 2**20
        ),
        name="outer_step",
    )(tiles_of(pseudo_grad[0]), tiles_of(params), tiles_of(momentum))
    results = pl.pallas_call(
        store_kernel,
        out_shape=[far, far],
        in_specs=[pl.BlockSpec(memory_space=pltpu.VMEM)] * 2,
        out_specs=[pl.BlockSpec(memory_space=pl.ANY)] * 2,
        scratch_shapes=[pltpu.SemaphoreType.DMA((2,))],
        compiler_params=pltpu.CompilerParams(vmem_limit_bytes=40 * 2**20),
        name="store",
    )(*results)
    return tuple(block_of(result, rows, columns) for result in results)


def solution(mesh):
    placed = (P("outer", "inner", None), P("inner", None), P("inner", None))
    return jax.shard_map(
        per_device,
        mesh=mesh,
        in_specs=placed,
        out_specs=(P("inner", None), P("inner", None)),
        check_vma=False,
    )
```

```python
import functools
import math

import jax
import jax.numpy as jnp
from jax import lax
from jax.experimental import pallas as pl
from jax.experimental.pallas import tpu as pltpu
from jax.sharding import PartitionSpec as P

MESH = pl.DeviceIdType.MESH
TILE = (8, 128)
TILES = 1024
A = 36
B = 28
STEP = 4
FIRST, REST = pl.ds(0, 16), pl.ds(16, A - 16)
GROUPS = 8


def tiles_of(block):
    rows, columns = block.shape
    cut = block.reshape(rows // 8, 8, columns // 128, 128)
    return cut.transpose(0, 2, 1, 3).reshape(-1, 8, 128)


def block_of(tiles, rows, columns):
    cut = tiles.reshape(rows // 8, columns // 128, 8, 128)
    return cut.transpose(0, 2, 1, 3).reshape(rows, columns)


def over_tiles(count, body):
    def step(i, carry):
        body(pl.multiple_of(i * STEP, STEP))
        return carry

    lax.fori_loop(0, count // STEP, step, 0)


class Copies:
    def __init__(self, send_sem, recv_sem, any_tiles):
        self.send_sem, self.recv_sem, self.any_tiles = send_sem, recv_sem, any_tiles
        self.groups, self.sent = 0, {}

    def group(self):
        self.groups += 1
        return Group(self, self.recv_sem.at[self.groups - 1])

    def wait(self, tiles, send=None, recv=None):
        some = self.any_tiles.at[pl.ds(0, tiles)]
        copy = pltpu.make_async_remote_copy(
            src_ref=some,
            dst_ref=some,
            send_sem=self.send_sem.at[0] if send is None else send,
            recv_sem=self.recv_sem.at[0] if recv is None else recv,
            device_id=self.anyone,
            device_id_type=MESH,
        )
        if recv is None:
            copy.wait_send()
        else:
            copy.wait_recv()

    def finish(self):
        for number, tiles in self.sent.items():
            self.wait(tiles, send=self.send_sem.at[number])


class Group:
    def __init__(self, copies, sem):
        self.copies, self.sem, self.tiles = copies, sem, 0

    def send(self, src, dst, to):
        number, device = to
        tiles = math.prod(src.shape) // math.prod(TILE)
        pltpu.make_async_remote_copy(
            src_ref=src,
            dst_ref=dst,
            send_sem=self.copies.send_sem.at[number],
            recv_sem=self.sem,
            device_id=device,
            device_id_type=MESH,
        ).start()
        self.tiles += tiles
        self.copies.sent[number] = self.copies.sent.get(number, 0) + tiles

    def wait(self):
        self.copies.wait(self.tiles, recv=self.sem)


GROUPS_OF_COPIES = 33


def kernel(
    entries,
    grad_hbm,
    params_hbm,
    momentum_hbm,
    new_params,
    new_momentum,
    grad,
    params,
    momentum,
    mean,
    x_first,
    x_second,
    x_third,
    x_sum,
    x_from_y,
    y_sum,
    q_first,
    q_second,
    q_third,
    squares,
    norm_z,
    norm_core,
    norm_x,
    norm_y,
    send_sem,
    recv_sem,
    load_sem,
    west_sem,
    east_sem,
    across_sem,
    met_sem,
):
    outer, inner = lax.axis_index("outer"), lax.axis_index("inner")
    x, half = lax.rem(outer, 4), lax.div(outer, 4)
    low, z, core = lax.div(inner, 8), lax.rem(lax.div(inner, 2), 4), lax.rem(inner, 2)
    y = half * 2 + low

    def device(x=x, y=y, z=z, core=core):
        return (lax.div(y, 2) * 4 + x, (lax.rem(y, 2) * 4 + z) * 2 + core)

    def ring(at, by):
        return lax.rem(at + by, 4)

    east, west, across = [
        (0, device(x=ring(x, 1))),
        (1, device(x=ring(x, 3))),
        (2, device(y=ring(y, 2))),
    ]
    x_peers = [(3, device(x=ring(x, k))) for k in (1, 2, 3)]
    y_peers = [(3, device(y=ring(y, k))) for k in (1, 2, 3)]
    z_peers = [(3, device(z=ring(z, k))) for k in (1, 2, 3)]
    core_peer = (3, device(core=1 - core))

    met = [
        (ring(x, 3) > x, west, west_sem, east_sem),
        (ring(x, 1) > x, east, east_sem, west_sem),
        (half == 0, across, across_sem, across_sem),
    ]
    met += [(ring(y, k) > y, (3, device(y=ring(y, k))), met_sem, met_sem) for k in (1, 3)]
    met += [(core == 1, core_peer, met_sem, met_sem)]
    met += [(ring(z, k) > z, (3, device(z=ring(z, k))), met_sem, met_sem) for k in (1, 2, 3)]
    lower = sum(jnp.where(higher, 0, 1) for higher, *_ in met)
    above = sum(jnp.where(higher, 1, 0) for higher, *_ in met[3:])

    barrier = pltpu.get_barrier_semaphore()
    for higher, (_, peer), _, _ in met:

        @pl.when(higher)
        def greet(peer=peer):
            pl.semaphore_signal(barrier, inc=1, device_id=peer, device_id_type=MESH)

    loads = [
        pltpu.make_async_copy(src, dst, load_sem.at[i])
        for i, (src, dst) in enumerate(
            ((grad_hbm, grad), (params_hbm, params), (momentum_hbm, momentum))
        )
    ]
    loads[0].start()

    @pl.when(lower > 0)
    def all_lower():
        pl.semaphore_wait(barrier, lower)

    def answer(higher, peer, _, theirs):
        @pl.when(jnp.logical_not(higher))
        def signal():
            pl.semaphore_signal(theirs, inc=1, device_id=peer[1], device_id_type=MESH)

    def answered(higher, _, mine, __):
        @pl.when(higher)
        def wait():
            pl.semaphore_wait(mine, 1)

    for entry in met[:3]:
        answer(*entry)

    copies = Copies(send_sem, recv_sem, mean)
    copies.anyone = east[1]
    other = 1 - half

    def at_x(chunk, h, d, pieces=1):
        return pl.ds(((ring(x, chunk) * 2 + h) * 2 + d) * A, pieces * A)

    def at_y(h, chunk, d, pieces=1):
        return pl.ds(16 * A + ((h * 4 + ring(x, chunk)) * 2 + d) * B, pieces * B)

    a_west, a_east, a_rest = copies.group(), copies.group(), copies.group()
    b_west, b_east, b_rest = copies.group(), copies.group(), copies.group()
    q_west, q_east, q_rest = copies.group(), copies.group(), copies.group()
    y_first = {(chunk, d): copies.group() for chunk, d in ((2, 0), (1, 0), (3, 1), (1, 1), (3, 0))}

    def x_open(group, chunk, h, d, land, to, cut=None):
        at = at_x(chunk, h, d)
        if cut is not None:
            at, land = cut_of(at, cut), land.at[cut]
        group.send(grad_hbm.at[at], land, to)

    def y_open(group, chunk, d, pieces=1):
        group.send(
            grad_hbm.at[at_y(other, chunk, d, pieces)],
            y_sum.at[chunk, pl.ds(d * B, pieces * B)],
            across,
        )

    def cut_of(at, cut):
        return pl.ds(at.start + cut.start, cut.size)

    def add_into(ref, term, start, count):
        def body(i):
            ref[pl.ds(i, STEP)] += term[pl.ds(start + i, STEP)]

        over_tiles(count, body)

    def y_add(chunk, d, pieces=1):
        piece = y_sum.at[chunk, pl.ds(d * B, pieces * B)]
        add_into(piece, grad, at_y(half, chunk, d).start, pieces * B)
        return piece

    def y_open_all():
        y_open(y_first[2, 0], 2, 0, 2)
        for chunk, d in ((1, 0), (3, 1), (1, 1), (3, 0)):
            y_open(y_first[chunk, d], chunk, d)
        y_open(q_rest, 0, 0, 2)

    counts = copies.sent.get(2, 0), {g: g.tiles for g in (*y_first.values(), q_rest)}

    @pl.when(half == 1)
    def y_now():
        y_open_all()

    copies.sent[2] = counts[0]
    for group, tiles in counts[1].items():
        group.tiles = tiles

    answered(*met[0])
    x_open(a_west, 2, other, 0, x_first.at[0, 0], west)
    x_open(a_rest, 3, other, 1, x_second.at[0, 1], west)
    x_open(b_west, 2, half, 0, x_first.at[1, 0], west)
    answered(*met[1])
    x_open(a_east, 2, other, 1, x_first.at[0, 1], east)
    x_open(a_rest, 1, other, 0, x_second.at[0, 0], east)
    x_open(b_east, 2, half, 1, x_first.at[1, 1], east)

    @pl.when(half == 0)
    def y_answered():
        pl.semaphore_wait(across_sem, 1)
        y_open_all()

    for entry in met[3:]:
        answer(*entry)

    loads[1].start()
    loads[2].start()
    loads[0].wait()

    def pass_on(arrived, rest, ref, land, to, term, start, count):
        arrived.wait()
        add_into(ref, term, start, count)
        rest.send(ref, land, to)

    def x_pass(slot, h, from_east, from_west, rest):
        for arrived, d, chunk, to in ((from_west, 1, 1, east), (from_east, 0, 3, west)):
            pass_on(
                arrived,
                rest,
                x_first.at[slot, d],
                x_third.at[slot, d],
                to,
                grad,
                at_x(chunk, h, d).start,
                A,
            )

    x_pass(0, other, a_west, a_east, a_rest)
    y_first[2, 0].wait()
    y_add(2, 0, 2)
    q_west.send(y_sum.at[2, pl.ds(0, B)], q_first.at[0], west)
    q_east.send(y_sum.at[2, pl.ds(B, B)], q_first.at[1], east)
    y_first[1, 0].wait()
    q_rest.send(y_add(1, 0), q_second.at[0], east)
    y_first[3, 1].wait()
    q_rest.send(y_add(3, 1), q_second.at[1], west)
    a_rest.wait()
    for d in (0, 1):
        base = at_x(0, other, d).start

        def body(i, d=d, base=base):
            x_sum[pl.ds(d * A + i, STEP)] = (
                grad[pl.ds(base + i, STEP)]
                + x_second[0, d, pl.ds(i, STEP)]
                + x_third[0, d, pl.ds(i, STEP)]
            )

        over_tiles(A, body)
    b_rest.send(x_sum, x_from_y, across)
    x_open(b_rest, 1, half, 0, x_second.at[1, 0], east, FIRST)
    x_open(b_rest, 3, half, 1, x_second.at[1, 1], west, FIRST)
    y_first[1, 1].wait()
    y_add(1, 1)
    pass_on(q_east, q_rest, q_first.at[1], q_third.at[1], east, y_sum.at[1], B, B)
    y_first[3, 0].wait()
    y_add(3, 0)
    pass_on(q_west, q_rest, q_first.at[0], q_third.at[0], west, y_sum.at[3], 0, B)
    x_open(b_rest, 1, half, 0, x_second.at[1, 0], east, REST)
    x_open(b_rest, 3, half, 1, x_second.at[1, 1], west, REST)
    x_pass(1, half, b_west, b_east, b_rest)

    squares[...] = jnp.zeros(TILE, jnp.float32)

    def store_mean(at, value):
        value = value / jnp.float32(GROUPS)
        mean[at] = value
        squares[...] += jnp.sum(value * value, axis=0)

    q_rest.wait()
    y_add(0, 0, 2)
    for d in (0, 1):
        base = at_y(half, 0, d).start

        def body(i, d=d, base=base):
            at = pl.ds(i, STEP)
            store_mean(
                pl.ds(base + i, STEP),
                y_sum[0, pl.ds(d * B + i, STEP)] + q_second[d, at] + q_third[d, at],
            )

        over_tiles(B, body)

    def gather(group, at, to):
        group.send(mean.at[at], mean.at[at], to)

    q_from_west, q_from_east, q_far = copies.group(), copies.group(), copies.group()
    x_from_west, x_from_east, crossed = copies.group(), copies.group(), copies.group()
    x_cuts = [(cut, copies.group(), copies.group()) for cut in (FIRST, REST)]
    early, late, last_first, last_rest, last_y = [copies.group() for _ in range(5)]

    gather(q_from_west, at_y(half, 0, 0, 2), east)
    gather(q_from_east, at_y(half, 0, 0, 2), west)
    gather(early, at_y(half, 0, 0, 2), across)

    b_rest.wait()
    for d in (0, 1):
        base = at_x(0, half, d).start

        def body(i, d=d, base=base):
            at = pl.ds(i, STEP)
            own = grad[pl.ds(base + i, STEP)] + x_second[1, d, at] + x_third[1, d, at]
            store_mean(pl.ds(base + i, STEP), own + x_from_y[pl.ds(d * A + i, STEP)])

        over_tiles(A, body)

    gather(x_from_west, at_x(0, half, 0), east)
    gather(x_from_east, at_x(0, half, 1), west)
    gather(early, at_x(0, half, 1), east)
    gather(early, at_x(0, half, 0), west)
    gather(crossed, at_x(0, half, 0, 2), across)

    def norm_send(slots, mine, value, to):
        group = copies.group()
        slots[mine] = value
        for peer in to:
            group.send(slots.at[mine], slots.at[mine], peer)
        return group

    def norm_take(slots, group):
        group.wait()
        total = slots[0]
        for i in range(1, slots.shape[0]):
            total = total + slots[i]
        return total

    @pl.when(above > 0)
    def all_met():
        pl.semaphore_wait(met_sem, above)

    sent = norm_send(norm_z, z, squares[...], z_peers)

    q_from_west.wait()
    gather(q_far, at_y(half, 3, 0), east)
    gather(early, at_y(half, 3, 0, 2), across)
    q_from_east.wait()
    gather(q_far, at_y(half, 1, 1), west)
    gather(early, at_y(half, 1, 0, 2), across)
    value = norm_take(norm_z, sent)
    sent = norm_send(norm_core, core, value, [core_peer])
    value = norm_take(norm_core, sent)
    sent = norm_send(norm_x, x, value, x_peers)
    x_from_west.wait()
    gather(early, at_x(3, half, 0), east)
    x_from_east.wait()
    gather(early, at_x(1, half, 1), west)
    crossed.wait()
    for cut, from_west, from_east in x_cuts:
        gather(from_west, cut_of(at_x(0, other, 0), cut), east)
        gather(from_east, cut_of(at_x(0, other, 1), cut), west)
    gather(late, at_x(0, other, 1), east)
    gather(late, at_x(0, other, 0), west)
    value = norm_take(norm_x, sent)
    sent = norm_send(norm_y, y, value, y_peers)
    q_far.wait()
    gather(last_y, at_y(half, 2, 0, 2), across)
    for (cut, from_west, from_east), last in zip(x_cuts, (last_first, last_rest)):
        from_west.wait()
        gather(last, cut_of(at_x(3, other, 0), cut), east)
        from_east.wait()
        gather(last, cut_of(at_x(1, other, 1), cut), west)
    total = norm_take(norm_y, sent)
    norm = jnp.sqrt(jnp.sum(total, keepdims=True) + 1e-06)
    factor = jnp.broadcast_to(
        jnp.minimum(1.0, 0.5 * math.sqrt(entries) / norm), TILE
    )[None]

    loads[1].wait()
    loads[2].wait()

    def update(at):
        start, count = at.start, at.size

        def body(i):
            at = pl.ds(start + i, STEP)
            clipped = factor * mean[at]
            moved = 0.9 * momentum[at] + clipped
            new_momentum[at] = moved
            new_params[at] = params[at] - 0.7 * (clipped + 0.9 * moved)

        over_tiles(count, body)

    update(at_x(0, half, 0, 2))
    update(at_x(3, half, 0))
    update(at_x(1, half, 1))
    for chunk in range(4):
        update(at_y(half, chunk, 0, 2))
    update(at_x(0, other, 0, 2))
    update(at_x(3, other, 0))
    update(at_x(1, other, 1))
    early.wait()
    update(at_x(3, half, 1))
    update(at_x(1, half, 0))
    update(at_x(2, half, 0, 2))
    for chunk in (0, 3, 1):
        update(at_y(other, chunk, 0, 2))
    late.wait()
    update(at_x(3, other, 1))
    update(at_x(1, other, 0))
    last_first.wait()
    update(cut_of(at_x(2, other, 0), FIRST))
    update(cut_of(at_x(2, other, 1), FIRST))
    last_y.wait()
    update(at_y(other, 2, 0, 2))
    last_rest.wait()
    update(cut_of(at_x(2, other, 0), REST))
    update(cut_of(at_x(2, other, 1), REST))
    copies.finish()
    assert copies.groups == GROUPS_OF_COPIES, copies.groups


def store_kernel(params, momentum, params_out, momentum_out, sem):
    cuts = 1
    size = TILES // cuts
    copies = []
    for i in range(cuts):
        for j, (src, dst) in enumerate(((params, params_out), (momentum, momentum_out))):
            at = pl.ds(i * size, size)
            copy = pltpu.make_async_copy(src.at[at], dst.at[at], sem.at[i * 2 + j])
            copy.start()
            copies.append(copy)
    for copy in copies:
        copy.wait()


def per_device(pseudo_grad, params, momentum):
    rows, columns = params.shape
    entries = rows * lax.axis_size("inner") * columns
    f32 = jnp.float32
    near = pltpu.VMEM((TILES, *TILE), f32)
    far = jax.ShapeDtypeStruct((TILES, *TILE), f32)

    def vmem(*lead):
        return pltpu.VMEM((*lead, *TILE), f32)

    results = pl.pallas_call(
        functools.partial(kernel, entries),
        out_shape=[near, near],
        in_specs=[pl.BlockSpec(memory_space=pl.ANY)] * 3,
        out_specs=[pl.BlockSpec(memory_space=pltpu.VMEM)] * 2,
        scratch_shapes=[
            vmem(TILES),
            vmem(TILES),
            vmem(TILES),
            vmem(TILES),
            vmem(2, 2, A),
            vmem(2, 2, A),
            vmem(2, 2, A),
            vmem(2 * A),
            vmem(2 * A),
            vmem(4, 2 * B),
            vmem(2, B),
            vmem(2, B),
            vmem(2, B),
            vmem(),
            vmem(4),
            vmem(2),
            vmem(4),
            vmem(4),
            pltpu.SemaphoreType.DMA((4,)),
            pltpu.SemaphoreType.DMA((GROUPS_OF_COPIES,)),
            pltpu.SemaphoreType.DMA((3,)),
            pltpu.SemaphoreType.REGULAR,
            pltpu.SemaphoreType.REGULAR,
            pltpu.SemaphoreType.REGULAR,
            pltpu.SemaphoreType.REGULAR,
        ],
        compiler_params=pltpu.CompilerParams(
            collective_id=0, has_side_effects=True, vmem_limit_bytes=49 * 2**20
        ),
        name="outer_step",
    )(tiles_of(pseudo_grad[0]), tiles_of(params), tiles_of(momentum))
    results = pl.pallas_call(
        store_kernel,
        out_shape=[far, far],
        in_specs=[pl.BlockSpec(memory_space=pltpu.VMEM)] * 2,
        out_specs=[pl.BlockSpec(memory_space=pl.ANY)] * 2,
        scratch_shapes=[pltpu.SemaphoreType.DMA((2,))],
        compiler_params=pltpu.CompilerParams(vmem_limit_bytes=40 * 2**20),
        name="store",
    )(*results)
    return tuple(block_of(result, rows, columns) for result in results)


def solution(mesh):
    placed = (P("outer", "inner", None), P("inner", None), P("inner", None))
    return jax.shard_map(
        per_device,
        mesh=mesh,
        in_specs=placed,
        out_specs=(P("inner", None), P("inner", None)),
        check_vma=False,
    )
```

```python
import functools
import math

import jax
import jax.numpy as jnp
from jax import lax
from jax.experimental import pallas as pl
from jax.experimental.pallas import tpu as pltpu
from jax.sharding import PartitionSpec as P

MESH = pl.DeviceIdType.MESH
TILE = (8, 128)
TILES = 1024
A = 36
B = 28
STEP = 10
FIRST, REST = pl.ds(0, 16), pl.ds(16, A - 16)
GROUPS = 8


def tiles_of(block):
    rows, columns = block.shape
    cut = block.reshape(rows // 8, 8, columns // 128, 128)
    return cut.transpose(0, 2, 1, 3).reshape(-1, 8, 128)


def block_of(tiles, rows, columns):
    cut = tiles.reshape(rows // 8, columns // 128, 8, 128)
    return cut.transpose(0, 2, 1, 3).reshape(rows, columns)


def over_tiles(count, body):
    steps, rest = divmod(count, STEP)
    if steps == 1:
        body(0, STEP)
    elif steps > 1:

        def step(i, carry):
            body(i * STEP, STEP)
            return carry

        lax.fori_loop(0, steps, step, 0)
    if rest:
        body(steps * STEP, rest)


class Copies:
    def __init__(self, send_sem, recv_sem, any_tiles):
        self.send_sem, self.recv_sem, self.any_tiles = send_sem, recv_sem, any_tiles
        self.groups, self.sent = 0, {}

    def group(self):
        self.groups += 1
        return Group(self, self.recv_sem.at[self.groups - 1])

    def wait(self, tiles, send=None, recv=None):
        some = self.any_tiles.at[pl.ds(0, tiles)]
        copy = pltpu.make_async_remote_copy(
            src_ref=some,
            dst_ref=some,
            send_sem=self.send_sem.at[0] if send is None else send,
            recv_sem=self.recv_sem.at[0] if recv is None else recv,
            device_id=self.anyone,
            device_id_type=MESH,
        )
        if recv is None:
            copy.wait_send()
        else:
            copy.wait_recv()

    def finish(self):
        for number, tiles in self.sent.items():
            self.wait(tiles, send=self.send_sem.at[number])


class Group:
    def __init__(self, copies, sem):
        self.copies, self.sem, self.tiles = copies, sem, 0

    def send(self, src, dst, to):
        number, device = to
        tiles = math.prod(src.shape) // math.prod(TILE)
        pltpu.make_async_remote_copy(
            src_ref=src,
            dst_ref=dst,
            send_sem=self.copies.send_sem.at[number],
            recv_sem=self.sem,
            device_id=device,
            device_id_type=MESH,
        ).start()
        self.tiles += tiles
        self.copies.sent[number] = self.copies.sent.get(number, 0) + tiles

    def wait(self):
        self.copies.wait(self.tiles, recv=self.sem)


GROUPS_OF_COPIES = 33


def kernel(
    entries,
    grad_hbm,
    params_hbm,
    momentum_hbm,
    new_params,
    new_momentum,
    grad,
    params,
    momentum,
    mean,
    x_first,
    x_second,
    x_third,
    x_sum,
    x_from_y,
    y_sum,
    q_first,
    q_second,
    q_third,
    squares,
    norm_z,
    norm_core,
    norm_x,
    norm_y,
    send_sem,
    recv_sem,
    load_sem,
    west_sem,
    east_sem,
    across_sem,
    met_sem,
):
    outer, inner = lax.axis_index("outer"), lax.axis_index("inner")
    x, half = lax.rem(outer, 4), lax.div(outer, 4)
    low, z, core = lax.div(inner, 8), lax.rem(lax.div(inner, 2), 4), lax.rem(inner, 2)
    y = half * 2 + low

    def device(x=x, y=y, z=z, core=core):
        return (lax.div(y, 2) * 4 + x, (lax.rem(y, 2) * 4 + z) * 2 + core)

    def ring(at, by):
        return lax.rem(at + by, 4)

    east, west, across = [
        (0, device(x=ring(x, 1))),
        (1, device(x=ring(x, 3))),
        (2, device(y=ring(y, 2))),
    ]
    x_peers = [(3, device(x=ring(x, k))) for k in (1, 2, 3)]
    y_peers = [(3, device(y=ring(y, k))) for k in (1, 2, 3)]
    z_peers = [(3, device(z=ring(z, k))) for k in (1, 2, 3)]
    core_peer = (3, device(core=1 - core))

    met = [
        (ring(x, 3) > x, west, west_sem, east_sem),
        (ring(x, 1) > x, east, east_sem, west_sem),
        (half == 0, across, across_sem, across_sem),
    ]
    met += [(ring(y, k) > y, (3, device(y=ring(y, k))), met_sem, met_sem) for k in (1, 3)]
    met += [(core == 1, core_peer, met_sem, met_sem)]
    met += [(ring(z, k) > z, (3, device(z=ring(z, k))), met_sem, met_sem) for k in (1, 2, 3)]
    lower = sum(jnp.where(higher, 0, 1) for higher, *_ in met)
    above = sum(jnp.where(higher, 1, 0) for higher, *_ in met[3:])

    barrier = pltpu.get_barrier_semaphore()
    for higher, (_, peer), _, _ in met:

        @pl.when(higher)
        def greet(peer=peer):
            pl.semaphore_signal(barrier, inc=1, device_id=peer, device_id_type=MESH)

    loads = [
        pltpu.make_async_copy(src, dst, load_sem.at[i])
        for i, (src, dst) in enumerate(
            ((grad_hbm, grad), (params_hbm, params), (momentum_hbm, momentum))
        )
    ]
    loads[0].start()

    @pl.when(lower > 0)
    def all_lower():
        pl.semaphore_wait(barrier, lower)

    def answer(higher, peer, _, theirs):
        @pl.when(jnp.logical_not(higher))
        def signal():
            pl.semaphore_signal(theirs, inc=1, device_id=peer[1], device_id_type=MESH)

    def answered(higher, _, mine, __):
        @pl.when(higher)
        def wait():
            pl.semaphore_wait(mine, 1)

    for entry in met[:3]:
        answer(*entry)

    copies = Copies(send_sem, recv_sem, mean)
    copies.anyone = east[1]
    other = 1 - half

    def at_x(chunk, h, d, pieces=1):
        return pl.ds(((ring(x, chunk) * 2 + h) * 2 + d) * A, pieces * A)

    def at_y(h, chunk, d, pieces=1):
        return pl.ds(16 * A + ((h * 4 + ring(x, chunk)) * 2 + d) * B, pieces * B)

    a_west, a_east, a_rest = copies.group(), copies.group(), copies.group()
    b_west, b_east, b_rest = copies.group(), copies.group(), copies.group()
    q_west, q_east, q_rest = copies.group(), copies.group(), copies.group()
    y_first = {(chunk, d): copies.group() for chunk, d in ((2, 0), (1, 0), (3, 1), (1, 1), (3, 0))}

    def x_open(group, chunk, h, d, land, to, cut=None):
        at = at_x(chunk, h, d)
        if cut is not None:
            at, land = cut_of(at, cut), land.at[cut]
        group.send(grad_hbm.at[at], land, to)

    def y_open(group, chunk, d, pieces=1):
        group.send(
            grad_hbm.at[at_y(other, chunk, d, pieces)],
            y_sum.at[chunk, pl.ds(d * B, pieces * B)],
            across,
        )

    def cut_of(at, cut):
        return pl.ds(at.start + cut.start, cut.size)

    def add_into(ref, term, start, count):
        def body(i, n):
            ref[pl.ds(i, n)] += term[pl.ds(start + i, n)]

        over_tiles(count, body)

    def y_add(chunk, d, pieces=1):
        piece = y_sum.at[chunk, pl.ds(d * B, pieces * B)]
        add_into(piece, grad, at_y(half, chunk, d).start, pieces * B)
        return piece

    def y_open_all():
        y_open(y_first[2, 0], 2, 0, 2)
        for chunk, d in ((1, 0), (3, 1), (1, 1), (3, 0)):
            y_open(y_first[chunk, d], chunk, d)
        y_open(q_rest, 0, 0, 2)

    counts = copies.sent.get(2, 0), {g: g.tiles for g in (*y_first.values(), q_rest)}

    @pl.when(half == 1)
    def y_now():
        y_open_all()

    copies.sent[2] = counts[0]
    for group, tiles in counts[1].items():
        group.tiles = tiles

    answered(*met[1])
    x_open(a_east, 2, other, 1, x_first.at[0, 1], east)
    x_open(a_rest, 1, other, 0, x_second.at[0, 0], east)
    x_open(b_east, 2, half, 1, x_first.at[1, 1], east)
    answered(*met[0])
    x_open(a_west, 2, other, 0, x_first.at[0, 0], west)
    x_open(a_rest, 3, other, 1, x_second.at[0, 1], west)
    x_open(b_west, 2, half, 0, x_first.at[1, 0], west)

    @pl.when(half == 0)
    def y_answered():
        pl.semaphore_wait(across_sem, 1)
        y_open_all()

    for entry in met[3:]:
        answer(*entry)

    loads[1].start()
    loads[2].start()
    loads[0].wait()

    def pass_on(arrived, rest, ref, land, to, term, start, count):
        arrived.wait()
        add_into(ref, term, start, count)
        rest.send(ref, land, to)

    def x_pass(slot, h, from_east, from_west, rest):
        for arrived, d, chunk, to in ((from_west, 1, 1, east), (from_east, 0, 3, west)):
            pass_on(
                arrived,
                rest,
                x_first.at[slot, d],
                x_third.at[slot, d],
                to,
                grad,
                at_x(chunk, h, d).start,
                A,
            )

    x_pass(0, other, a_west, a_east, a_rest)
    y_first[2, 0].wait()
    y_add(2, 0, 2)
    q_west.send(y_sum.at[2, pl.ds(0, B)], q_first.at[0], west)
    q_east.send(y_sum.at[2, pl.ds(B, B)], q_first.at[1], east)
    y_first[1, 0].wait()
    q_rest.send(y_add(1, 0), q_second.at[0], east)
    y_first[3, 1].wait()
    q_rest.send(y_add(3, 1), q_second.at[1], west)
    a_rest.wait()
    for d in (0, 1):
        base = at_x(0, other, d).start

        def body(i, n, d=d, base=base):
            x_sum[pl.ds(d * A + i, n)] = (
                grad[pl.ds(base + i, n)]
                + x_second[0, d, pl.ds(i, n)]
                + x_third[0, d, pl.ds(i, n)]
            )

        over_tiles(A, body)
    b_rest.send(x_sum, x_from_y, across)
    x_open(b_rest, 1, half, 0, x_second.at[1, 0], east, FIRST)
    x_open(b_rest, 3, half, 1, x_second.at[1, 1], west, FIRST)
    y_first[1, 1].wait()
    y_add(1, 1)
    pass_on(q_east, q_rest, q_first.at[1], q_third.at[1], east, y_sum.at[1], B, B)
    y_first[3, 0].wait()
    y_add(3, 0)
    pass_on(q_west, q_rest, q_first.at[0], q_third.at[0], west, y_sum.at[3], 0, B)
    x_open(b_rest, 1, half, 0, x_second.at[1, 0], east, REST)
    x_open(b_rest, 3, half, 1, x_second.at[1, 1], west, REST)
    x_pass(1, half, b_west, b_east, b_rest)

    squares[...] = jnp.zeros(TILE, jnp.float32)

    def store_mean(at, value):
        value = value / jnp.float32(GROUPS)
        mean[at] = value
        squares[...] += jnp.sum(value * value, axis=0)

    q_rest.wait()
    y_add(0, 0, 2)
    for d in (0, 1):
        base = at_y(half, 0, d).start

        def body(i, n, d=d, base=base):
            at = pl.ds(i, n)
            store_mean(
                pl.ds(base + i, n),
                y_sum[0, pl.ds(d * B + i, n)] + q_second[d, at] + q_third[d, at],
            )

        over_tiles(B, body)

    def gather(group, at, to):
        group.send(mean.at[at], mean.at[at], to)

    q_from_west, q_from_east, q_far = copies.group(), copies.group(), copies.group()
    x_from_west, x_from_east, crossed = copies.group(), copies.group(), copies.group()
    x_cuts = [(cut, copies.group(), copies.group()) for cut in (FIRST, REST)]
    early, late, last_first, last_rest, last_y = [copies.group() for _ in range(5)]

    gather(q_from_west, at_y(half, 0, 0, 2), east)
    gather(q_from_east, at_y(half, 0, 0, 2), west)
    gather(early, at_y(half, 0, 0, 2), across)

    b_rest.wait()
    for d in (0, 1):
        base = at_x(0, half, d).start

        def body(i, n, d=d, base=base):
            at = pl.ds(i, n)
            own = grad[pl.ds(base + i, n)] + x_second[1, d, at] + x_third[1, d, at]
            store_mean(pl.ds(base + i, n), own + x_from_y[pl.ds(d * A + i, n)])

        over_tiles(A, body)

    gather(x_from_west, at_x(0, half, 0), east)
    gather(x_from_east, at_x(0, half, 1), west)
    gather(early, at_x(0, half, 1), east)
    gather(early, at_x(0, half, 0), west)
    gather(crossed, at_x(0, half, 0, 2), across)

    def norm_send(slots, mine, value, to):
        group = copies.group()
        slots[mine] = value
        for peer in to:
            group.send(slots.at[mine], slots.at[mine], peer)
        return group

    def norm_take(slots, group):
        group.wait()
        total = slots[0]
        for i in range(1, slots.shape[0]):
            total = total + slots[i]
        return total

    @pl.when(above > 0)
    def all_met():
        pl.semaphore_wait(met_sem, above)

    sent = norm_send(norm_z, z, squares[...], z_peers)

    q_from_west.wait()
    gather(q_far, at_y(half, 3, 0), east)
    gather(early, at_y(half, 3, 0, 2), across)
    q_from_east.wait()
    gather(q_far, at_y(half, 1, 1), west)
    gather(early, at_y(half, 1, 0, 2), across)
    value = norm_take(norm_z, sent)
    sent = norm_send(norm_core, core, value, [core_peer])
    value = norm_take(norm_core, sent)
    sent = norm_send(norm_x, x, value, x_peers)
    x_from_west.wait()
    gather(early, at_x(3, half, 0), east)
    x_from_east.wait()
    gather(early, at_x(1, half, 1), west)
    crossed.wait()
    for cut, from_west, from_east in x_cuts:
        gather(from_west, cut_of(at_x(0, other, 0), cut), east)
        gather(from_east, cut_of(at_x(0, other, 1), cut), west)
    gather(late, at_x(0, other, 1), east)
    gather(late, at_x(0, other, 0), west)
    value = norm_take(norm_x, sent)
    sent = norm_send(norm_y, y, value, y_peers)
    q_far.wait()
    gather(last_y, at_y(half, 2, 0, 2), across)
    for (cut, from_west, from_east), last in zip(x_cuts, (last_first, last_rest)):
        from_west.wait()
        gather(last, cut_of(at_x(3, other, 0), cut), east)
        from_east.wait()
        gather(last, cut_of(at_x(1, other, 1), cut), west)
    total = norm_take(norm_y, sent)
    norm = jnp.sqrt(jnp.sum(total, keepdims=True) + 1e-06)
    factor = jnp.broadcast_to(
        jnp.minimum(1.0, 0.5 * math.sqrt(entries) / norm), TILE
    )[None]

    loads[1].wait()
    loads[2].wait()

    def update(at):
        start, count = at.start, at.size

        def body(i, n):
            at = pl.ds(start + i, n)
            clipped = factor * mean[at]
            moved = 0.9 * momentum[at] + clipped
            new_momentum[at] = moved
            new_params[at] = params[at] - 0.7 * (clipped + 0.9 * moved)

        over_tiles(count, body)

    update(at_x(0, half, 0, 2))
    update(at_x(3, half, 0))
    update(at_x(1, half, 1))
    for chunk in range(4):
        update(at_y(half, chunk, 0, 2))
    update(at_x(0, other, 0, 2))
    update(at_x(3, other, 0))
    update(at_x(1, other, 1))
    early.wait()
    update(at_x(3, half, 1))
    update(at_x(1, half, 0))
    update(at_x(2, half, 0, 2))
    for chunk in (0, 3, 1):
        update(at_y(other, chunk, 0, 2))
    late.wait()
    update(at_x(3, other, 1))
    update(at_x(1, other, 0))
    last_first.wait()
    update(cut_of(at_x(2, other, 0), FIRST))
    update(cut_of(at_x(2, other, 1), FIRST))
    last_y.wait()
    update(at_y(other, 2, 0, 2))
    last_rest.wait()
    update(cut_of(at_x(2, other, 0), REST))
    update(cut_of(at_x(2, other, 1), REST))
    copies.finish()
    assert copies.groups == GROUPS_OF_COPIES, copies.groups


def store_kernel(params, momentum, params_out, momentum_out, sem):
    cuts = 1
    size = TILES // cuts
    copies = []
    for i in range(cuts):
        for j, (src, dst) in enumerate(((params, params_out), (momentum, momentum_out))):
            at = pl.ds(i * size, size)
            copy = pltpu.make_async_copy(src.at[at], dst.at[at], sem.at[i * 2 + j])
            copy.start()
            copies.append(copy)
    for copy in copies:
        copy.wait()


def per_device(pseudo_grad, params, momentum):
    rows, columns = params.shape
    entries = rows * lax.axis_size("inner") * columns
    f32 = jnp.float32
    near = pltpu.VMEM((TILES, *TILE), f32)
    far = jax.ShapeDtypeStruct((TILES, *TILE), f32)

    def vmem(*lead):
        return pltpu.VMEM((*lead, *TILE), f32)

    results = pl.pallas_call(
        functools.partial(kernel, entries),
        out_shape=[near, near],
        in_specs=[pl.BlockSpec(memory_space=pl.ANY)] * 3,
        out_specs=[pl.BlockSpec(memory_space=pltpu.VMEM)] * 2,
        scratch_shapes=[
            vmem(TILES),
            vmem(TILES),
            vmem(TILES),
            vmem(TILES),
            vmem(2, 2, A),
            vmem(2, 2, A),
            vmem(2, 2, A),
            vmem(2 * A),
            vmem(2 * A),
            vmem(4, 2 * B),
            vmem(2, B),
            vmem(2, B),
            vmem(2, B),
            vmem(),
            vmem(4),
            vmem(2),
            vmem(4),
            vmem(4),
            pltpu.SemaphoreType.DMA((4,)),
            pltpu.SemaphoreType.DMA((GROUPS_OF_COPIES,)),
            pltpu.SemaphoreType.DMA((3,)),
            pltpu.SemaphoreType.REGULAR,
            pltpu.SemaphoreType.REGULAR,
            pltpu.SemaphoreType.REGULAR,
            pltpu.SemaphoreType.REGULAR,
        ],
        compiler_params=pltpu.CompilerParams(
            collective_id=0, has_side_effects=True, vmem_limit_bytes=49 * 2**20
        ),
        name="outer_step",
    )(tiles_of(pseudo_grad[0]), tiles_of(params), tiles_of(momentum))
    results = pl.pallas_call(
        store_kernel,
        out_shape=[far, far],
        in_specs=[pl.BlockSpec(memory_space=pltpu.VMEM)] * 2,
        out_specs=[pl.BlockSpec(memory_space=pl.ANY)] * 2,
        scratch_shapes=[pltpu.SemaphoreType.DMA((2,))],
        compiler_params=pltpu.CompilerParams(vmem_limit_bytes=40 * 2**20),
        name="store",
    )(*results)
    return tuple(block_of(result, rows, columns) for result in results)


def solution(mesh):
    placed = (P("outer", "inner", None), P("inner", None), P("inner", None))
    return jax.shard_map(
        per_device,
        mesh=mesh,
        in_specs=placed,
        out_specs=(P("inner", None), P("inner", None)),
        check_vma=False,
    )
```

```python
import functools
import math

import jax
import jax.numpy as jnp
from jax import lax
from jax.experimental import pallas as pl
from jax.experimental.pallas import tpu as pltpu
from jax.sharding import PartitionSpec as P

MESH = pl.DeviceIdType.MESH
TILE = (8, 128)
TILES = 1024
A = 36
B = 28
STEP = 10
FIRST, REST = pl.ds(0, 16), pl.ds(16, A - 16)
GROUPS = 8


def tiles_of(block):
    rows, columns = block.shape
    cut = block.reshape(rows // 8, 8, columns // 128, 128)
    return cut.transpose(0, 2, 1, 3).reshape(-1, 8, 128)


def block_of(tiles, rows, columns):
    cut = tiles.reshape(rows // 8, columns // 128, 8, 128)
    return cut.transpose(0, 2, 1, 3).reshape(rows, columns)


def over_tiles(count, body):
    steps, rest = divmod(count, STEP)
    if steps == 1:
        body(0, STEP)
    elif steps > 1:

        def step(i, carry):
            body(i * STEP, STEP)
            return carry

        lax.fori_loop(0, steps, step, 0)
    if rest:
        body(steps * STEP, rest)


class Copies:
    def __init__(self, send_sem, recv_sem, any_tiles):
        self.send_sem, self.recv_sem, self.any_tiles = send_sem, recv_sem, any_tiles
        self.groups, self.sent = 0, {}

    def group(self):
        self.groups += 1
        return Group(self, self.recv_sem.at[self.groups - 1])

    def wait(self, tiles, send=None, recv=None):
        some = self.any_tiles.at[pl.ds(0, tiles)]
        copy = pltpu.make_async_remote_copy(
            src_ref=some,
            dst_ref=some,
            send_sem=self.send_sem.at[0] if send is None else send,
            recv_sem=self.recv_sem.at[0] if recv is None else recv,
            device_id=self.anyone,
            device_id_type=MESH,
        )
        if recv is None:
            copy.wait_send()
        else:
            copy.wait_recv()

    def finish(self):
        for number, tiles in self.sent.items():
            self.wait(tiles, send=self.send_sem.at[number])


class Group:
    def __init__(self, copies, sem):
        self.copies, self.sem, self.tiles = copies, sem, 0

    def send(self, src, dst, to):
        number, device = to
        tiles = math.prod(src.shape) // math.prod(TILE)
        pltpu.make_async_remote_copy(
            src_ref=src,
            dst_ref=dst,
            send_sem=self.copies.send_sem.at[number],
            recv_sem=self.sem,
            device_id=device,
            device_id_type=MESH,
        ).start()
        self.tiles += tiles
        self.copies.sent[number] = self.copies.sent.get(number, 0) + tiles

    def wait(self):
        self.copies.wait(self.tiles, recv=self.sem)


GROUPS_OF_COPIES = 33


def kernel(
    entries,
    grad_hbm,
    params_hbm,
    momentum_hbm,
    new_params,
    new_momentum,
    grad,
    params,
    momentum,
    mean,
    x_first,
    x_second,
    x_third,
    x_sum,
    x_from_y,
    y_sum,
    q_first,
    q_second,
    q_third,
    squares,
    norm_z,
    norm_core,
    norm_x,
    norm_y,
    send_sem,
    recv_sem,
    load_sem,
    west_sem,
    east_sem,
    across_sem,
    met_sem,
):
    outer, inner = lax.axis_index("outer"), lax.axis_index("inner")
    x, half = lax.rem(outer, 4), lax.div(outer, 4)
    low, z, core = lax.div(inner, 8), lax.rem(lax.div(inner, 2), 4), lax.rem(inner, 2)
    y = half * 2 + low

    def device(x=x, y=y, z=z, core=core):
        return (lax.div(y, 2) * 4 + x, (lax.rem(y, 2) * 4 + z) * 2 + core)

    def ring(at, by):
        return lax.rem(at + by, 4)

    east, west, across = [
        (0, device(x=ring(x, 1))),
        (1, device(x=ring(x, 3))),
        (2, device(y=ring(y, 2))),
    ]
    x_peers = [(3, device(x=ring(x, k))) for k in (1, 2, 3)]
    y_peers = [(3, device(y=ring(y, k))) for k in (1, 2, 3)]
    z_peers = [(3, device(z=ring(z, k))) for k in (1, 2, 3)]
    core_peer = (3, device(core=1 - core))

    met = [
        (ring(x, 3) > x, west, west_sem, east_sem),
        (ring(x, 1) > x, east, east_sem, west_sem),
        (half == 0, across, across_sem, across_sem),
    ]
    met += [(half == 0, (3, device(y=3 - y)), met_sem, met_sem)]
    met += [(core == 1, core_peer, met_sem, met_sem)]
    met += [(ring(z, k) > z, (3, device(z=ring(z, k))), met_sem, met_sem) for k in (1, 2, 3)]
    lower = sum(jnp.where(higher, 0, 1) for higher, *_ in met)
    above = sum(jnp.where(higher, 1, 0) for higher, *_ in met[3:])

    barrier = pltpu.get_barrier_semaphore()
    for higher, (_, peer), _, _ in met:

        @pl.when(higher)
        def greet(peer=peer):
            pl.semaphore_signal(barrier, inc=1, device_id=peer, device_id_type=MESH)

    loads = [
        pltpu.make_async_copy(src, dst, load_sem.at[i])
        for i, (src, dst) in enumerate(
            ((grad_hbm, grad), (params_hbm, params), (momentum_hbm, momentum))
        )
    ]
    loads[0].start()

    @pl.when(lower > 0)
    def all_lower():
        pl.semaphore_wait(barrier, lower)

    def answer(higher, peer, _, theirs):
        @pl.when(jnp.logical_not(higher))
        def signal():
            pl.semaphore_signal(theirs, inc=1, device_id=peer[1], device_id_type=MESH)

    def answered(higher, _, mine, __):
        @pl.when(higher)
        def wait():
            pl.semaphore_wait(mine, 1)

    for entry in met[:3]:
        answer(*entry)

    copies = Copies(send_sem, recv_sem, mean)
    copies.anyone = east[1]
    other = 1 - half

    def at_x(chunk, h, d, pieces=1):
        return pl.ds(((ring(x, chunk) * 2 + h) * 2 + d) * A, pieces * A)

    def at_y(h, chunk, d, pieces=1):
        return pl.ds(16 * A + ((h * 4 + ring(x, chunk)) * 2 + d) * B, pieces * B)

    a_west, a_east, a_rest = copies.group(), copies.group(), copies.group()
    b_west, b_east, b_rest = copies.group(), copies.group(), copies.group()
    q_west, q_east, q_rest = copies.group(), copies.group(), copies.group()
    y_first = {(chunk, d): copies.group() for chunk, d in ((2, 0), (1, 0), (3, 1), (1, 1), (3, 0))}

    def x_open(group, chunk, h, d, land, to, cut=None):
        at = at_x(chunk, h, d)
        if cut is not None:
            at, land = cut_of(at, cut), land.at[cut]
        group.send(grad_hbm.at[at], land, to)

    def y_open(group, chunk, d, pieces=1):
        group.send(
            grad_hbm.at[at_y(other, chunk, d, pieces)],
            y_sum.at[chunk, pl.ds(d * B, pieces * B)],
            across,
        )

    def cut_of(at, cut):
        return pl.ds(at.start + cut.start, cut.size)

    def add_into(ref, term, start, count):
        def body(i, n):
            ref[pl.ds(i, n)] += term[pl.ds(start + i, n)]

        over_tiles(count, body)

    def y_add(chunk, d, pieces=1):
        piece = y_sum.at[chunk, pl.ds(d * B, pieces * B)]
        add_into(piece, grad, at_y(half, chunk, d).start, pieces * B)
        return piece

    def y_open_all():
        y_open(y_first[2, 0], 2, 0, 2)
        for chunk, d in ((1, 0), (3, 1), (1, 1), (3, 0)):
            y_open(y_first[chunk, d], chunk, d)
        y_open(q_rest, 0, 0, 2)

    counts = copies.sent.get(2, 0), {g: g.tiles for g in (*y_first.values(), q_rest)}

    @pl.when(half == 1)
    def y_now():
        y_open_all()

    copies.sent[2] = counts[0]
    for group, tiles in counts[1].items():
        group.tiles = tiles

    answered(*met[1])
    x_open(a_east, 2, other, 1, x_first.at[0, 1], east)
    x_open(a_rest, 1, other, 0, x_second.at[0, 0], east)
    x_open(b_east, 2, half, 1, x_first.at[1, 1], east)
    answered(*met[0])
    x_open(a_west, 2, other, 0, x_first.at[0, 0], west)
    x_open(a_rest, 3, other, 1, x_second.at[0, 1], west)
    x_open(b_west, 2, half, 0, x_first.at[1, 0], west)

    @pl.when(half == 0)
    def y_answered():
        pl.semaphore_wait(across_sem, 1)
        y_open_all()

    for entry in met[3:]:
        answer(*entry)

    loads[1].start()
    loads[2].start()
    loads[0].wait()

    def pass_on(arrived, rest, ref, land, to, term, start, count):
        arrived.wait()
        add_into(ref, term, start, count)
        rest.send(ref, land, to)

    def x_pass(slot, h, from_east, from_west, rest):
        for arrived, d, chunk, to in ((from_west, 1, 1, east), (from_east, 0, 3, west)):
            pass_on(
                arrived,
                rest,
                x_first.at[slot, d],
                x_third.at[slot, d],
                to,
                grad,
                at_x(chunk, h, d).start,
                A,
            )

    x_pass(0, other, a_west, a_east, a_rest)
    y_first[2, 0].wait()
    y_add(2, 0, 2)
    q_west.send(y_sum.at[2, pl.ds(0, B)], q_first.at[0], west)
    q_east.send(y_sum.at[2, pl.ds(B, B)], q_first.at[1], east)
    y_first[1, 0].wait()
    q_rest.send(y_add(1, 0), q_second.at[0], east)
    y_first[3, 1].wait()
    q_rest.send(y_add(3, 1), q_second.at[1], west)
    a_rest.wait()
    for d in (0, 1):
        base = at_x(0, other, d).start

        def body(i, n, d=d, base=base):
            x_sum[pl.ds(d * A + i, n)] = (
                grad[pl.ds(base + i, n)]
                + x_second[0, d, pl.ds(i, n)]
                + x_third[0, d, pl.ds(i, n)]
            )

        over_tiles(A, body)
    @pl.when(above > 0)
    def all_met():
        pl.semaphore_wait(met_sem, above)

    b_rest.send(x_sum, x_from_y, across)
    x_open(b_rest, 1, half, 0, x_second.at[1, 0], east, FIRST)
    x_open(b_rest, 3, half, 1, x_second.at[1, 1], west, FIRST)
    y_first[1, 1].wait()
    y_add(1, 1)
    pass_on(q_east, q_rest, q_first.at[1], q_third.at[1], east, y_sum.at[1], B, B)
    y_first[3, 0].wait()
    y_add(3, 0)
    pass_on(q_west, q_rest, q_first.at[0], q_third.at[0], west, y_sum.at[3], 0, B)
    x_open(b_rest, 1, half, 0, x_second.at[1, 0], east, REST)
    x_open(b_rest, 3, half, 1, x_second.at[1, 1], west, REST)
    x_pass(1, half, b_west, b_east, b_rest)

    squares[...] = jnp.zeros(TILE, jnp.float32)

    def store_mean(at, value):
        value = value / jnp.float32(GROUPS)
        mean[at] = value
        squares[...] += jnp.sum(value * value, axis=0)

    q_rest.wait()
    y_add(0, 0, 2)
    for d in (0, 1):
        base = at_y(half, 0, d).start

        def body(i, n, d=d, base=base):
            at = pl.ds(i, n)
            store_mean(
                pl.ds(base + i, n),
                y_sum[0, pl.ds(d * B + i, n)] + q_second[d, at] + q_third[d, at],
            )

        over_tiles(B, body)

    def gather(group, at, to):
        group.send(mean.at[at], mean.at[at], to)

    q_from_west, q_from_east, q_far = copies.group(), copies.group(), copies.group()
    x_from_west, x_from_east, crossed = copies.group(), copies.group(), copies.group()
    x_cuts = [(cut, copies.group(), copies.group()) for cut in (FIRST, REST)]
    early, late, last_first, last_rest, last_y = [copies.group() for _ in range(5)]

    gather(q_from_west, at_y(half, 0, 0, 2), east)
    gather(q_from_east, at_y(half, 0, 0, 2), west)
    gather(early, at_y(half, 0, 0, 2), across)

    b_rest.wait()
    for d in (0, 1):
        base = at_x(0, half, d).start

        def body(i, n, d=d, base=base):
            at = pl.ds(i, n)
            own = grad[pl.ds(base + i, n)] + x_second[1, d, at] + x_third[1, d, at]
            store_mean(pl.ds(base + i, n), own + x_from_y[pl.ds(d * A + i, n)])

        over_tiles(A, body)

    gather(x_from_west, at_x(0, half, 0), east)
    gather(x_from_east, at_x(0, half, 1), west)
    gather(early, at_x(0, half, 1), east)
    gather(early, at_x(0, half, 0), west)
    gather(crossed, at_x(0, half, 0, 2), across)

    def norm_send(slots, mine, value, to):
        group = copies.group()
        slots[mine] = value
        for peer in to:
            group.send(slots.at[mine], slots.at[mine], peer)
        return group

    def norm_take(slots, group):
        group.wait()
        total = slots[0]
        for i in range(1, slots.shape[0]):
            total = total + slots[i]
        return total

    sent = norm_send(norm_z, z, squares[...], z_peers)

    q_from_west.wait()
    gather(q_far, at_y(half, 3, 0), east)
    gather(early, at_y(half, 3, 0, 2), across)
    q_from_east.wait()
    gather(q_far, at_y(half, 1, 1), west)
    gather(early, at_y(half, 1, 0, 2), across)
    value = norm_take(norm_z, sent)
    sent = norm_send(norm_core, core, value, [core_peer])
    value = norm_take(norm_core, sent)
    sent = norm_send(norm_x, x, value, x_peers)
    x_from_west.wait()
    gather(early, at_x(3, half, 0), east)
    x_from_east.wait()
    gather(early, at_x(1, half, 1), west)
    crossed.wait()
    for cut, from_west, from_east in x_cuts:
        gather(from_west, cut_of(at_x(0, other, 0), cut), east)
        gather(from_east, cut_of(at_x(0, other, 1), cut), west)
    gather(late, at_x(0, other, 1), east)
    gather(late, at_x(0, other, 0), west)
    value = norm_take(norm_x, sent)
    sent = norm_send(norm_y, y, value, y_peers)
    q_far.wait()
    gather(last_y, at_y(half, 2, 0, 2), across)
    for (cut, from_west, from_east), last in zip(x_cuts, (last_first, last_rest)):
        from_west.wait()
        gather(last, cut_of(at_x(3, other, 0), cut), east)
        from_east.wait()
        gather(last, cut_of(at_x(1, other, 1), cut), west)
    total = norm_take(norm_y, sent)
    norm = jnp.sqrt(jnp.sum(total, keepdims=True) + 1e-06)
    factor = jnp.broadcast_to(
        jnp.minimum(1.0, 0.5 * math.sqrt(entries) / norm), TILE
    )[None]

    loads[1].wait()
    loads[2].wait()

    def update(at):
        start, count = at.start, at.size

        def body(i, n):
            at = pl.ds(start + i, n)
            clipped = factor * mean[at]
            moved = 0.9 * momentum[at] + clipped
            new_momentum[at] = moved
            new_params[at] = params[at] - 0.7 * (clipped + 0.9 * moved)

        over_tiles(count, body)

    update(at_x(0, half, 0, 2))
    update(at_x(3, half, 0))
    update(at_x(1, half, 1))
    for chunk in range(4):
        update(at_y(half, chunk, 0, 2))
    update(at_x(0, other, 0, 2))
    update(at_x(3, other, 0))
    update(at_x(1, other, 1))
    early.wait()
    update(at_x(3, half, 1))
    update(at_x(1, half, 0))
    update(at_x(2, half, 0, 2))
    for chunk in (0, 3, 1):
        update(at_y(other, chunk, 0, 2))
    late.wait()
    update(at_x(3, other, 1))
    update(at_x(1, other, 0))
    last_first.wait()
    update(cut_of(at_x(2, other, 0), FIRST))
    update(cut_of(at_x(2, other, 1), FIRST))
    last_y.wait()
    update(at_y(other, 2, 0, 2))
    last_rest.wait()
    update(cut_of(at_x(2, other, 0), REST))
    update(cut_of(at_x(2, other, 1), REST))
    copies.finish()
    assert copies.groups == GROUPS_OF_COPIES, copies.groups


def store_kernel(params, momentum, params_out, momentum_out, sem):
    cuts = 1
    size = TILES // cuts
    copies = []
    for i in range(cuts):
        for j, (src, dst) in enumerate(((params, params_out), (momentum, momentum_out))):
            at = pl.ds(i * size, size)
            copy = pltpu.make_async_copy(src.at[at], dst.at[at], sem.at[i * 2 + j])
            copy.start()
            copies.append(copy)
    for copy in copies:
        copy.wait()


def per_device(pseudo_grad, params, momentum):
    rows, columns = params.shape
    entries = rows * lax.axis_size("inner") * columns
    f32 = jnp.float32
    near = pltpu.VMEM((TILES, *TILE), f32)
    far = jax.ShapeDtypeStruct((TILES, *TILE), f32)

    def vmem(*lead):
        return pltpu.VMEM((*lead, *TILE), f32)

    results = pl.pallas_call(
        functools.partial(kernel, entries),
        out_shape=[near, near],
        in_specs=[pl.BlockSpec(memory_space=pl.ANY)] * 3,
        out_specs=[pl.BlockSpec(memory_space=pltpu.VMEM)] * 2,
        scratch_shapes=[
            vmem(TILES),
            vmem(TILES),
            vmem(TILES),
            vmem(TILES),
            vmem(2, 2, A),
            vmem(2, 2, A),
            vmem(2, 2, A),
            vmem(2 * A),
            vmem(2 * A),
            vmem(4, 2 * B),
            vmem(2, B),
            vmem(2, B),
            vmem(2, B),
            vmem(),
            vmem(4),
            vmem(2),
            vmem(4),
            vmem(4),
            pltpu.SemaphoreType.DMA((4,)),
            pltpu.SemaphoreType.DMA((GROUPS_OF_COPIES,)),
            pltpu.SemaphoreType.DMA((3,)),
            pltpu.SemaphoreType.REGULAR,
            pltpu.SemaphoreType.REGULAR,
            pltpu.SemaphoreType.REGULAR,
            pltpu.SemaphoreType.REGULAR,
        ],
        compiler_params=pltpu.CompilerParams(
            collective_id=0, has_side_effects=True, vmem_limit_bytes=49 * 2**20
        ),
        name="outer_step",
    )(tiles_of(pseudo_grad[0]), tiles_of(params), tiles_of(momentum))
    results = pl.pallas_call(
        store_kernel,
        out_shape=[far, far],
        in_specs=[pl.BlockSpec(memory_space=pltpu.VMEM)] * 2,
        out_specs=[pl.BlockSpec(memory_space=pl.ANY)] * 2,
        scratch_shapes=[pltpu.SemaphoreType.DMA((2,))],
        compiler_params=pltpu.CompilerParams(vmem_limit_bytes=40 * 2**20),
        name="store",
    )(*results)
    return tuple(block_of(result, rows, columns) for result in results)


def solution(mesh):
    placed = (P("outer", "inner", None), P("inner", None), P("inner", None))
    return jax.shard_map(
        per_device,
        mesh=mesh,
        in_specs=placed,
        out_specs=(P("inner", None), P("inner", None)),
        check_vma=False,
    )
```

```python
import functools
import math

import jax
import jax.numpy as jnp
from jax import lax
from jax.experimental import pallas as pl
from jax.experimental.pallas import tpu as pltpu
from jax.sharding import PartitionSpec as P

MESH = pl.DeviceIdType.MESH
TILE = (8, 128)
TILES = 1024
A = 36
B = 28
STEP = 10
FIRST, REST = pl.ds(0, 16), pl.ds(16, A - 16)
GROUPS = 8


def tiles_of(block):
    rows, columns = block.shape
    cut = block.reshape(rows // 8, 8, columns // 128, 128)
    return cut.transpose(0, 2, 1, 3).reshape(-1, 8, 128)


def block_of(tiles, rows, columns):
    cut = tiles.reshape(rows // 8, columns // 128, 8, 128)
    return cut.transpose(0, 2, 1, 3).reshape(rows, columns)


def over_tiles(count, body):
    steps, rest = divmod(count, STEP)
    if steps == 1:
        body(0, STEP)
    elif steps > 1:

        def step(i, carry):
            body(i * STEP, STEP)
            return carry

        lax.fori_loop(0, steps, step, 0)
    if rest:
        body(steps * STEP, rest)


class Copies:
    def __init__(self, send_sem, recv_sem, any_tiles):
        self.send_sem, self.recv_sem, self.any_tiles = send_sem, recv_sem, any_tiles
        self.groups, self.sent = 0, {}

    def group(self):
        self.groups += 1
        return Group(self, self.recv_sem.at[self.groups - 1])

    def wait(self, tiles, send=None, recv=None):
        some = self.any_tiles.at[pl.ds(0, tiles)]
        copy = pltpu.make_async_remote_copy(
            src_ref=some,
            dst_ref=some,
            send_sem=self.send_sem.at[0] if send is None else send,
            recv_sem=self.recv_sem.at[0] if recv is None else recv,
            device_id=self.anyone,
            device_id_type=MESH,
        )
        if recv is None:
            copy.wait_send()
        else:
            copy.wait_recv()

    def finish(self):
        for number, tiles in self.sent.items():
            self.wait(tiles, send=self.send_sem.at[number])


class Group:
    def __init__(self, copies, sem):
        self.copies, self.sem, self.tiles = copies, sem, 0

    def send(self, src, dst, to):
        number, device = to
        tiles = math.prod(src.shape) // math.prod(TILE)
        pltpu.make_async_remote_copy(
            src_ref=src,
            dst_ref=dst,
            send_sem=self.copies.send_sem.at[number],
            recv_sem=self.sem,
            device_id=device,
            device_id_type=MESH,
        ).start()
        self.tiles += tiles
        self.copies.sent[number] = self.copies.sent.get(number, 0) + tiles

    def wait(self):
        self.copies.wait(self.tiles, recv=self.sem)


GROUPS_OF_COPIES = 33


def kernel(
    entries,
    grad_hbm,
    params_hbm,
    momentum_hbm,
    new_params,
    new_momentum,
    grad,
    params,
    momentum,
    mean,
    x_first,
    x_second,
    x_third,
    x_sum,
    x_from_y,
    y_sum,
    q_first,
    q_second,
    q_third,
    squares,
    norm_z,
    norm_core,
    norm_x,
    norm_y,
    send_sem,
    recv_sem,
    load_sem,
    west_sem,
    east_sem,
    across_sem,
    met_sem,
):
    outer, inner = lax.axis_index("outer"), lax.axis_index("inner")
    x, half = lax.rem(outer, 4), lax.div(outer, 4)
    low, z, core = lax.div(inner, 8), lax.rem(lax.div(inner, 2), 4), lax.rem(inner, 2)
    y = half * 2 + low

    def device(x=x, y=y, z=z, core=core):
        return (lax.div(y, 2) * 4 + x, (lax.rem(y, 2) * 4 + z) * 2 + core)

    def ring(at, by):
        return lax.rem(at + by, 4)

    east, west, across = [
        (0, device(x=ring(x, 1))),
        (1, device(x=ring(x, 3))),
        (2, device(y=ring(y, 2))),
    ]
    x_peers = [(3, device(x=ring(x, k))) for k in (1, 2, 3)]
    y_peers = [(3, device(y=ring(y, k))) for k in (1, 2, 3)]
    z_peers = [(3, device(z=ring(z, k))) for k in (1, 2, 3)]
    core_peer = (3, device(core=1 - core))

    met = [
        (ring(x, 3) > x, west, west_sem, east_sem),
        (ring(x, 1) > x, east, east_sem, west_sem),
        (half == 0, across, across_sem, across_sem),
    ]
    met += [(half == 0, (3, device(y=3 - y)), met_sem, met_sem)]
    met += [(core == 1, core_peer, met_sem, met_sem)]
    met += [(ring(z, k) > z, (3, device(z=ring(z, k))), met_sem, met_sem) for k in (1, 2, 3)]
    lower = sum(jnp.where(higher, 0, 1) for higher, *_ in met)
    above = sum(jnp.where(higher, 1, 0) for higher, *_ in met[3:])

    barrier = pltpu.get_barrier_semaphore()
    for higher, (_, peer), _, _ in met:

        @pl.when(higher)
        def greet(peer=peer):
            pl.semaphore_signal(barrier, inc=1, device_id=peer, device_id_type=MESH)

    loads = [
        pltpu.make_async_copy(src, dst, load_sem.at[i])
        for i, (src, dst) in enumerate(
            ((grad_hbm, grad), (params_hbm, params), (momentum_hbm, momentum))
        )
    ]
    loads[0].start()

    @pl.when(lower > 0)
    def all_lower():
        pl.semaphore_wait(barrier, lower)

    def answer(higher, peer, _, theirs):
        @pl.when(jnp.logical_not(higher))
        def signal():
            pl.semaphore_signal(theirs, inc=1, device_id=peer[1], device_id_type=MESH)

    def answered(higher, _, mine, __):
        @pl.when(higher)
        def wait():
            pl.semaphore_wait(mine, 1)

    for entry in met[:3]:
        answer(*entry)

    copies = Copies(send_sem, recv_sem, mean)
    copies.anyone = east[1]
    other = 1 - half

    def at_x(chunk, h, d, pieces=1):
        return pl.ds(((ring(x, chunk) * 2 + h) * 2 + d) * A, pieces * A)

    def at_y(h, chunk, d, pieces=1):
        return pl.ds(16 * A + ((h * 4 + ring(x, chunk)) * 2 + d) * B, pieces * B)

    a_west, a_east, a_rest = copies.group(), copies.group(), copies.group()
    b_west, b_east, b_rest = copies.group(), copies.group(), copies.group()
    q_west, q_east, q_rest = copies.group(), copies.group(), copies.group()
    y_first = {(chunk, d): copies.group() for chunk, d in ((2, 0), (1, 0), (3, 1), (1, 1), (3, 0))}

    def x_open(group, chunk, h, d, land, to, cut=None):
        at = at_x(chunk, h, d)
        if cut is not None:
            at, land = cut_of(at, cut), land.at[cut]
        group.send(grad_hbm.at[at], land, to)

    def y_open(group, chunk, d, pieces=1):
        group.send(
            grad_hbm.at[at_y(other, chunk, d, pieces)],
            y_sum.at[chunk, pl.ds(d * B, pieces * B)],
            across,
        )

    def cut_of(at, cut):
        return pl.ds(at.start + cut.start, cut.size)

    def add_into(ref, term, start, count):
        def body(i, n):
            ref[pl.ds(i, n)] += term[pl.ds(start + i, n)]

        over_tiles(count, body)

    def y_add(chunk, d, pieces=1):
        piece = y_sum.at[chunk, pl.ds(d * B, pieces * B)]
        add_into(piece, grad, at_y(half, chunk, d).start, pieces * B)
        return piece

    def y_open_all():
        y_open(y_first[2, 0], 2, 0, 2)
        for chunk, d in ((1, 0), (3, 1), (1, 1), (3, 0)):
            y_open(y_first[chunk, d], chunk, d)
        y_open(q_rest, 0, 0, 2)

    counts = copies.sent.get(2, 0), {g: g.tiles for g in (*y_first.values(), q_rest)}

    @pl.when(half == 1)
    def y_now():
        y_open_all()

    copies.sent[2] = counts[0]
    for group, tiles in counts[1].items():
        group.tiles = tiles

    answered(*met[1])
    x_open(a_east, 2, other, 1, x_first.at[0, 1], east)
    x_open(a_rest, 1, other, 0, x_second.at[0, 0], east)
    x_open(b_east, 2, half, 1, x_first.at[1, 1], east)
    answered(*met[0])
    x_open(a_west, 2, other, 0, x_first.at[0, 0], west)
    x_open(a_rest, 3, other, 1, x_second.at[0, 1], west)
    x_open(b_west, 2, half, 0, x_first.at[1, 0], west)

    @pl.when(half == 0)
    def y_answered():
        pl.semaphore_wait(across_sem, 1)
        y_open_all()

    for entry in met[3:]:
        answer(*entry)

    loads[1].start()
    loads[2].start()
    loads[0].wait()

    def pass_on(arrived, rest, ref, land, to, term, start, count):
        arrived.wait()
        add_into(ref, term, start, count)
        rest.send(ref, land, to)

    def x_pass(slot, h, from_east, from_west, rest):
        for arrived, d, chunk, to in ((from_east, 0, 3, west), (from_west, 1, 1, east)):
            pass_on(
                arrived,
                rest,
                x_first.at[slot, d],
                x_third.at[slot, d],
                to,
                grad,
                at_x(chunk, h, d).start,
                A,
            )

    x_pass(0, other, a_west, a_east, a_rest)
    y_first[2, 0].wait()
    y_add(2, 0, 2)
    q_west.send(y_sum.at[2, pl.ds(0, B)], q_first.at[0], west)
    q_east.send(y_sum.at[2, pl.ds(B, B)], q_first.at[1], east)
    y_first[1, 0].wait()
    q_rest.send(y_add(1, 0), q_second.at[0], east)
    y_first[3, 1].wait()
    q_rest.send(y_add(3, 1), q_second.at[1], west)
    a_rest.wait()
    for d in (0, 1):
        base = at_x(0, other, d).start

        def body(i, n, d=d, base=base):
            x_sum[pl.ds(d * A + i, n)] = (
                grad[pl.ds(base + i, n)]
                + x_second[0, d, pl.ds(i, n)]
                + x_third[0, d, pl.ds(i, n)]
            )

        over_tiles(A, body)
    @pl.when(above > 0)
    def all_met():
        pl.semaphore_wait(met_sem, above)

    b_rest.send(x_sum, x_from_y, across)
    x_open(b_rest, 1, half, 0, x_second.at[1, 0], east, FIRST)
    x_open(b_rest, 3, half, 1, x_second.at[1, 1], west, FIRST)
    y_first[1, 1].wait()
    y_add(1, 1)
    pass_on(q_east, q_rest, q_first.at[1], q_third.at[1], east, y_sum.at[1], B, B)
    y_first[3, 0].wait()
    y_add(3, 0)
    pass_on(q_west, q_rest, q_first.at[0], q_third.at[0], west, y_sum.at[3], 0, B)
    x_open(b_rest, 1, half, 0, x_second.at[1, 0], east, REST)
    x_open(b_rest, 3, half, 1, x_second.at[1, 1], west, REST)
    x_pass(1, half, b_west, b_east, b_rest)

    squares[...] = jnp.zeros(TILE, jnp.float32)

    def store_mean(at, value):
        value = value / jnp.float32(GROUPS)
        mean[at] = value
        squares[...] += jnp.sum(value * value, axis=0)

    q_rest.wait()
    y_add(0, 0, 2)
    for d in (0, 1):
        base = at_y(half, 0, d).start

        def body(i, n, d=d, base=base):
            at = pl.ds(i, n)
            store_mean(
                pl.ds(base + i, n),
                y_sum[0, pl.ds(d * B + i, n)] + q_second[d, at] + q_third[d, at],
            )

        over_tiles(B, body)

    def gather(group, at, to):
        group.send(mean.at[at], mean.at[at], to)

    q_from_west, q_from_east, q_far = copies.group(), copies.group(), copies.group()
    x_from_west, x_from_east, crossed = copies.group(), copies.group(), copies.group()
    x_cuts = [(cut, copies.group(), copies.group()) for cut in (FIRST, REST)]
    early, late, last_first, last_rest, last_y = [copies.group() for _ in range(5)]

    gather(q_from_west, at_y(half, 0, 0, 2), east)
    gather(q_from_east, at_y(half, 0, 0, 2), west)
    gather(early, at_y(half, 0, 0, 2), across)

    b_rest.wait()
    for d in (0, 1):
        base = at_x(0, half, d).start

        def body(i, n, d=d, base=base):
            at = pl.ds(i, n)
            own = grad[pl.ds(base + i, n)] + x_second[1, d, at] + x_third[1, d, at]
            store_mean(pl.ds(base + i, n), own + x_from_y[pl.ds(d * A + i, n)])

        over_tiles(A, body)

    gather(x_from_west, at_x(0, half, 0), east)
    gather(x_from_east, at_x(0, half, 1), west)
    gather(early, at_x(0, half, 1), east)
    gather(early, at_x(0, half, 0), west)
    gather(crossed, at_x(0, half, 0, 2), across)

    def norm_send(slots, mine, value, to):
        group = copies.group()
        slots[mine] = value
        for peer in to:
            group.send(slots.at[mine], slots.at[mine], peer)
        return group

    def norm_take(slots, group):
        group.wait()
        total = slots[0]
        for i in range(1, slots.shape[0]):
            total = total + slots[i]
        return total

    sent = norm_send(norm_z, z, squares[...], z_peers)

    q_from_west.wait()
    gather(q_far, at_y(half, 3, 0), east)
    gather(early, at_y(half, 3, 0, 2), across)
    q_from_east.wait()
    gather(q_far, at_y(half, 1, 1), west)
    gather(early, at_y(half, 1, 0, 2), across)
    value = norm_take(norm_z, sent)
    sent = norm_send(norm_core, core, value, [core_peer])
    value = norm_take(norm_core, sent)
    sent = norm_send(norm_x, x, value, x_peers)
    x_from_west.wait()
    gather(early, at_x(3, half, 0), east)
    x_from_east.wait()
    gather(early, at_x(1, half, 1), west)
    crossed.wait()
    for cut, from_west, from_east in x_cuts:
        gather(from_west, cut_of(at_x(0, other, 0), cut), east)
        gather(from_east, cut_of(at_x(0, other, 1), cut), west)
    gather(late, at_x(0, other, 1), east)
    gather(late, at_x(0, other, 0), west)
    value = norm_take(norm_x, sent)
    sent = norm_send(norm_y, y, value, y_peers)
    q_far.wait()
    gather(last_y, at_y(half, 2, 0, 2), across)
    for (cut, from_west, from_east), last in zip(x_cuts, (last_first, last_rest)):
        from_west.wait()
        gather(last, cut_of(at_x(3, other, 0), cut), east)
        from_east.wait()
        gather(last, cut_of(at_x(1, other, 1), cut), west)
    total = norm_take(norm_y, sent)
    norm = jnp.sqrt(jnp.sum(total, keepdims=True) + 1e-06)
    factor = jnp.broadcast_to(
        jnp.minimum(1.0, 0.5 * math.sqrt(entries) / norm), TILE
    )[None]

    loads[1].wait()
    loads[2].wait()

    def update(at):
        start, count = at.start, at.size

        def body(i, n):
            at = pl.ds(start + i, n)
            clipped = factor * mean[at]
            moved = 0.9 * momentum[at] + clipped
            new_momentum[at] = moved
            new_params[at] = params[at] - 0.7 * (clipped + 0.9 * moved)

        over_tiles(count, body)

    update(at_x(0, half, 0, 2))
    update(at_x(3, half, 0))
    update(at_x(1, half, 1))
    for chunk in range(4):
        update(at_y(half, chunk, 0, 2))
    update(at_x(0, other, 0, 2))
    update(at_x(3, other, 0))
    update(at_x(1, other, 1))
    early.wait()
    update(at_x(3, half, 1))
    update(at_x(1, half, 0))
    update(at_x(2, half, 0, 2))
    for chunk in (0, 3, 1):
        update(at_y(other, chunk, 0, 2))
    late.wait()
    update(at_x(3, other, 1))
    update(at_x(1, other, 0))
    last_first.wait()
    update(cut_of(at_x(2, other, 0), FIRST))
    update(cut_of(at_x(2, other, 1), FIRST))
    last_y.wait()
    update(at_y(other, 2, 0, 2))
    last_rest.wait()
    update(cut_of(at_x(2, other, 0), REST))
    update(cut_of(at_x(2, other, 1), REST))
    copies.finish()
    assert copies.groups == GROUPS_OF_COPIES, copies.groups


def store_kernel(params, momentum, params_out, momentum_out, sem):
    cuts = 1
    size = TILES // cuts
    copies = []
    for i in range(cuts):
        for j, (src, dst) in enumerate(((params, params_out), (momentum, momentum_out))):
            at = pl.ds(i * size, size)
            copy = pltpu.make_async_copy(src.at[at], dst.at[at], sem.at[i * 2 + j])
            copy.start()
            copies.append(copy)
    for copy in copies:
        copy.wait()


def per_device(pseudo_grad, params, momentum):
    rows, columns = params.shape
    entries = rows * lax.axis_size("inner") * columns
    f32 = jnp.float32
    near = pltpu.VMEM((TILES, *TILE), f32)
    far = jax.ShapeDtypeStruct((TILES, *TILE), f32)

    def vmem(*lead):
        return pltpu.VMEM((*lead, *TILE), f32)

    results = pl.pallas_call(
        functools.partial(kernel, entries),
        out_shape=[near, near],
        in_specs=[pl.BlockSpec(memory_space=pl.ANY)] * 3,
        out_specs=[pl.BlockSpec(memory_space=pltpu.VMEM)] * 2,
        scratch_shapes=[
            vmem(TILES),
            vmem(TILES),
            vmem(TILES),
            vmem(TILES),
            vmem(2, 2, A),
            vmem(2, 2, A),
            vmem(2, 2, A),
            vmem(2 * A),
            vmem(2 * A),
            vmem(4, 2 * B),
            vmem(2, B),
            vmem(2, B),
            vmem(2, B),
            vmem(),
            vmem(4),
            vmem(2),
            vmem(4),
            vmem(4),
            pltpu.SemaphoreType.DMA((4,)),
            pltpu.SemaphoreType.DMA((GROUPS_OF_COPIES,)),
            pltpu.SemaphoreType.DMA((3,)),
            pltpu.SemaphoreType.REGULAR,
            pltpu.SemaphoreType.REGULAR,
            pltpu.SemaphoreType.REGULAR,
            pltpu.SemaphoreType.REGULAR,
        ],
        compiler_params=pltpu.CompilerParams(
            collective_id=0, has_side_effects=True, vmem_limit_bytes=49 * 2**20
        ),
        name="outer_step",
    )(tiles_of(pseudo_grad[0]), tiles_of(params), tiles_of(momentum))
    results = pl.pallas_call(
        store_kernel,
        out_shape=[far, far],
        in_specs=[pl.BlockSpec(memory_space=pltpu.VMEM)] * 2,
        out_specs=[pl.BlockSpec(memory_space=pl.ANY)] * 2,
        scratch_shapes=[pltpu.SemaphoreType.DMA((2,))],
        compiler_params=pltpu.CompilerParams(vmem_limit_bytes=40 * 2**20),
        name="store",
    )(*results)
    return tuple(block_of(result, rows, columns) for result in results)


def solution(mesh):
    placed = (P("outer", "inner", None), P("inner", None), P("inner", None))
    return jax.shard_map(
        per_device,
        mesh=mesh,
        in_specs=placed,
        out_specs=(P("inner", None), P("inner", None)),
        check_vma=False,
    )
```

```python
import functools
import math

import jax
import jax.numpy as jnp
from jax import lax
from jax.experimental import pallas as pl
from jax.experimental.pallas import tpu as pltpu
from jax.sharding import PartitionSpec as P

MESH = pl.DeviceIdType.MESH
TILE = (8, 128)
TILES = 1024
A = 36
B = 28
STEP = 9
FIRST, REST = pl.ds(0, 16), pl.ds(16, A - 16)
GROUPS = 8


def tiles_of(block):
    rows, columns = block.shape
    cut = block.reshape(rows // 8, 8, columns // 128, 128)
    return cut.transpose(0, 2, 1, 3).reshape(-1, 8, 128)


def block_of(tiles, rows, columns):
    cut = tiles.reshape(rows // 8, columns // 128, 8, 128)
    return cut.transpose(0, 2, 1, 3).reshape(rows, columns)


def over_tiles(count, body):
    steps, rest = divmod(count, STEP)
    if steps == 1:
        body(0, STEP)
    elif steps > 1:

        def step(i, carry):
            body(i * STEP, STEP)
            return carry

        lax.fori_loop(0, steps, step, 0)
    if rest:
        body(steps * STEP, rest)


class Copies:
    def __init__(self, send_sem, recv_sem, any_tiles):
        self.send_sem, self.recv_sem, self.any_tiles = send_sem, recv_sem, any_tiles
        self.groups, self.sent = 0, {}

    def group(self):
        self.groups += 1
        return Group(self, self.recv_sem.at[self.groups - 1])

    def wait(self, tiles, send=None, recv=None):
        some = self.any_tiles.at[pl.ds(0, tiles)]
        copy = pltpu.make_async_remote_copy(
            src_ref=some,
            dst_ref=some,
            send_sem=self.send_sem.at[0] if send is None else send,
            recv_sem=self.recv_sem.at[0] if recv is None else recv,
            device_id=self.anyone,
            device_id_type=MESH,
        )
        if recv is None:
            copy.wait_send()
        else:
            copy.wait_recv()

    def finish(self):
        for number, tiles in self.sent.items():
            self.wait(tiles, send=self.send_sem.at[number])


class Group:
    def __init__(self, copies, sem):
        self.copies, self.sem, self.tiles = copies, sem, 0

    def send(self, src, dst, to):
        number, device = to
        tiles = math.prod(src.shape) // math.prod(TILE)
        pltpu.make_async_remote_copy(
            src_ref=src,
            dst_ref=dst,
            send_sem=self.copies.send_sem.at[number],
            recv_sem=self.sem,
            device_id=device,
            device_id_type=MESH,
        ).start()
        self.tiles += tiles
        self.copies.sent[number] = self.copies.sent.get(number, 0) + tiles

    def wait(self):
        self.copies.wait(self.tiles, recv=self.sem)


GROUPS_OF_COPIES = 33


def kernel(
    entries,
    grad_hbm,
    params_hbm,
    momentum_hbm,
    new_params,
    new_momentum,
    grad,
    params,
    momentum,
    mean,
    x_first,
    x_second,
    x_third,
    x_sum,
    x_from_y,
    y_sum,
    q_first,
    q_second,
    q_third,
    squares,
    norm_z,
    norm_core,
    norm_x,
    norm_y,
    send_sem,
    recv_sem,
    load_sem,
    west_sem,
    east_sem,
    across_sem,
    met_sem,
):
    outer, inner = lax.axis_index("outer"), lax.axis_index("inner")
    x, half = lax.rem(outer, 4), lax.div(outer, 4)
    low, z, core = lax.div(inner, 8), lax.rem(lax.div(inner, 2), 4), lax.rem(inner, 2)
    y = half * 2 + low

    def device(x=x, y=y, z=z, core=core):
        return (lax.div(y, 2) * 4 + x, (lax.rem(y, 2) * 4 + z) * 2 + core)

    def ring(at, by):
        return lax.rem(at + by, 4)

    east, west, across = [
        (0, device(x=ring(x, 1))),
        (1, device(x=ring(x, 3))),
        (2, device(y=ring(y, 2))),
    ]
    x_peers = [(2, device(x=ring(x, k))) for k in (1, 2, 3)]
    y_peers = [(2, device(y=ring(y, k))) for k in (1, 2, 3)]
    z_peers = [(2, device(z=ring(z, k))) for k in (1, 2, 3)]
    core_peer = (2, device(core=1 - core))

    met = [
        (ring(x, 3) > x, west, west_sem, east_sem),
        (ring(x, 1) > x, east, east_sem, west_sem),
        (half == 0, across, across_sem, across_sem),
    ]
    met += [(half == 0, (2, device(y=3 - y)), met_sem, met_sem)]
    met += [(core == 1, core_peer, met_sem, met_sem)]
    met += [(ring(z, k) > z, (2, device(z=ring(z, k))), met_sem, met_sem) for k in (1, 2, 3)]
    lower = sum(jnp.where(higher, 0, 1) for higher, *_ in met)
    above = sum(jnp.where(higher, 1, 0) for higher, *_ in met[3:])

    barrier = pltpu.get_barrier_semaphore()
    for higher, (_, peer), _, _ in met:

        @pl.when(higher)
        def greet(peer=peer):
            pl.semaphore_signal(barrier, inc=1, device_id=peer, device_id_type=MESH)

    loads = [
        pltpu.make_async_copy(src, dst, load_sem.at[i])
        for i, (src, dst) in enumerate(
            ((grad_hbm, grad), (params_hbm, params), (momentum_hbm, momentum))
        )
    ]
    loads[0].start()

    @pl.when(lower > 0)
    def all_lower():
        pl.semaphore_wait(barrier, lower)

    def answer(higher, peer, _, theirs):
        @pl.when(jnp.logical_not(higher))
        def signal():
            pl.semaphore_signal(theirs, inc=1, device_id=peer[1], device_id_type=MESH)

    def answered(higher, _, mine, __):
        @pl.when(higher)
        def wait():
            pl.semaphore_wait(mine, 1)

    for entry in met[:3]:
        answer(*entry)

    copies = Copies(send_sem, recv_sem, mean)
    copies.anyone = east[1]
    other = 1 - half

    def at_x(chunk, h, d, pieces=1):
        return pl.ds(((ring(x, chunk) * 2 + h) * 2 + d) * A, pieces * A)

    def at_y(h, chunk, d, pieces=1):
        return pl.ds(16 * A + ((h * 4 + ring(x, chunk)) * 2 + d) * B, pieces * B)

    a_west, a_east, a_rest = copies.group(), copies.group(), copies.group()
    b_west, b_east, b_rest = copies.group(), copies.group(), copies.group()
    q_west, q_east, q_rest = copies.group(), copies.group(), copies.group()
    y_first = {(chunk, d): copies.group() for chunk, d in ((2, 0), (1, 0), (3, 1), (1, 1), (3, 0))}

    def x_open(group, chunk, h, d, land, to, cut=None):
        at = at_x(chunk, h, d)
        if cut is not None:
            at, land = cut_of(at, cut), land.at[cut]
        group.send(grad_hbm.at[at], land, to)

    def y_open(group, chunk, d, pieces=1):
        group.send(
            grad_hbm.at[at_y(other, chunk, d, pieces)],
            y_sum.at[chunk, pl.ds(d * B, pieces * B)],
            across,
        )

    def cut_of(at, cut):
        return pl.ds(at.start + cut.start, cut.size)

    def add_into(ref, term, start, count):
        def body(i, n):
            ref[pl.ds(i, n)] += term[pl.ds(start + i, n)]

        over_tiles(count, body)

    def y_add(chunk, d, pieces=1):
        piece = y_sum.at[chunk, pl.ds(d * B, pieces * B)]
        add_into(piece, grad, at_y(half, chunk, d).start, pieces * B)
        return piece

    def y_open_all():
        y_open(y_first[2, 0], 2, 0, 2)
        for chunk, d in ((1, 0), (3, 1), (1, 1), (3, 0)):
            y_open(y_first[chunk, d], chunk, d)
        y_open(q_rest, 0, 0, 2)

    counts = copies.sent.get(2, 0), {g: g.tiles for g in (*y_first.values(), q_rest)}

    @pl.when(half == 1)
    def y_now():
        y_open_all()

    copies.sent[2] = counts[0]
    for group, tiles in counts[1].items():
        group.tiles = tiles

    answered(*met[1])
    x_open(a_east, 2, other, 1, x_first.at[0, 1], east)
    x_open(a_rest, 1, other, 0, x_second.at[0, 0], east)
    x_open(b_east, 2, half, 1, x_first.at[1, 1], east)
    answered(*met[0])
    x_open(a_west, 2, other, 0, x_first.at[0, 0], west)
    x_open(a_rest, 3, other, 1, x_second.at[0, 1], west)
    x_open(b_west, 2, half, 0, x_first.at[1, 0], west)

    @pl.when(half == 0)
    def y_answered():
        pl.semaphore_wait(across_sem, 1)
        y_open_all()

    for entry in met[3:]:
        answer(*entry)

    loads[1].start()
    loads[2].start()
    loads[0].wait()

    def pass_on(arrived, rest, ref, land, to, term, start, count):
        arrived.wait()
        add_into(ref, term, start, count)
        rest.send(ref, land, to)

    def x_pass(slot, h, from_east, from_west, rest):
        for arrived, d, chunk, to in ((from_east, 0, 3, west), (from_west, 1, 1, east)):
            pass_on(
                arrived,
                rest,
                x_first.at[slot, d],
                x_third.at[slot, d],
                to,
                grad,
                at_x(chunk, h, d).start,
                A,
            )

    x_pass(0, other, a_west, a_east, a_rest)
    y_first[2, 0].wait()
    y_add(2, 0, 2)
    q_west.send(y_sum.at[2, pl.ds(0, B)], q_first.at[0], west)
    q_east.send(y_sum.at[2, pl.ds(B, B)], q_first.at[1], east)
    y_first[1, 0].wait()
    q_rest.send(y_add(1, 0), q_second.at[0], east)
    y_first[3, 1].wait()
    q_rest.send(y_add(3, 1), q_second.at[1], west)
    a_rest.wait()
    for d in (0, 1):
        base = at_x(0, other, d).start

        def body(i, n, d=d, base=base):
            x_sum[pl.ds(d * A + i, n)] = (
                grad[pl.ds(base + i, n)]
                + x_second[0, d, pl.ds(i, n)]
                + x_third[0, d, pl.ds(i, n)]
            )

        over_tiles(A, body)
    @pl.when(above > 0)
    def all_met():
        pl.semaphore_wait(met_sem, above)

    b_rest.send(x_sum, x_from_y, across)
    x_open(b_rest, 1, half, 0, x_second.at[1, 0], east, FIRST)
    x_open(b_rest, 3, half, 1, x_second.at[1, 1], west, FIRST)
    y_first[1, 1].wait()
    y_add(1, 1)
    pass_on(q_east, q_rest, q_first.at[1], q_third.at[1], east, y_sum.at[1], B, B)
    y_first[3, 0].wait()
    y_add(3, 0)
    pass_on(q_west, q_rest, q_first.at[0], q_third.at[0], west, y_sum.at[3], 0, B)
    x_open(b_rest, 1, half, 0, x_second.at[1, 0], east, REST)
    x_open(b_rest, 3, half, 1, x_second.at[1, 1], west, REST)
    x_pass(1, half, b_west, b_east, b_rest)

    squares[...] = jnp.zeros(TILE, jnp.float32)

    def store_mean(at, value):
        value = value / jnp.float32(GROUPS)
        mean[at] = value
        squares[...] += jnp.sum(value * value, axis=0)

    q_rest.wait()
    y_add(0, 0, 2)
    for d in (0, 1):
        base = at_y(half, 0, d).start

        def body(i, n, d=d, base=base):
            at = pl.ds(i, n)
            store_mean(
                pl.ds(base + i, n),
                y_sum[0, pl.ds(d * B + i, n)] + q_second[d, at] + q_third[d, at],
            )

        over_tiles(B, body)

    def gather(group, at, to):
        group.send(mean.at[at], mean.at[at], to)

    q_from_west, q_from_east, q_far = copies.group(), copies.group(), copies.group()
    x_from_west, x_from_east, crossed = copies.group(), copies.group(), copies.group()
    x_cuts = [(cut, copies.group(), copies.group()) for cut in (FIRST, REST)]
    early, late, last_first, last_rest, last_y = [copies.group() for _ in range(5)]

    gather(q_from_west, at_y(half, 0, 0, 2), east)
    gather(q_from_east, at_y(half, 0, 0, 2), west)
    gather(early, at_y(half, 0, 0, 2), across)

    b_rest.wait()
    for d in (0, 1):
        base = at_x(0, half, d).start

        def body(i, n, d=d, base=base):
            at = pl.ds(i, n)
            own = grad[pl.ds(base + i, n)] + x_second[1, d, at] + x_third[1, d, at]
            store_mean(pl.ds(base + i, n), own + x_from_y[pl.ds(d * A + i, n)])

        over_tiles(A, body)

    gather(x_from_west, at_x(0, half, 0), east)
    gather(x_from_east, at_x(0, half, 1), west)
    gather(early, at_x(0, half, 1), east)
    gather(early, at_x(0, half, 0), west)
    gather(crossed, at_x(0, half, 0, 2), across)

    def norm_send(slots, mine, value, to):
        group = copies.group()
        slots[mine] = value
        for peer in to:
            group.send(slots.at[mine], slots.at[mine], peer)
        return group

    def norm_take(slots, group):
        group.wait()
        total = slots[0]
        for i in range(1, slots.shape[0]):
            total = total + slots[i]
        return total

    sent = norm_send(norm_z, z, squares[...], z_peers)

    q_from_west.wait()
    gather(q_far, at_y(half, 3, 0), east)
    gather(early, at_y(half, 3, 0, 2), across)
    q_from_east.wait()
    gather(q_far, at_y(half, 1, 1), west)
    gather(early, at_y(half, 1, 0, 2), across)
    value = norm_take(norm_z, sent)
    sent = norm_send(norm_core, core, value, [core_peer])
    value = norm_take(norm_core, sent)
    sent = norm_send(norm_x, x, value, x_peers)
    x_from_west.wait()
    gather(early, at_x(3, half, 0), east)
    x_from_east.wait()
    gather(early, at_x(1, half, 1), west)
    crossed.wait()
    for cut, from_west, from_east in x_cuts:
        gather(from_west, cut_of(at_x(0, other, 0), cut), east)
        gather(from_east, cut_of(at_x(0, other, 1), cut), west)
    gather(late, at_x(0, other, 1), east)
    gather(late, at_x(0, other, 0), west)
    value = norm_take(norm_x, sent)
    sent = norm_send(norm_y, y, value, y_peers)
    q_far.wait()
    gather(last_y, at_y(half, 2, 0, 2), across)
    for (cut, from_west, from_east), last in zip(x_cuts, (last_first, last_rest)):
        from_west.wait()
        gather(last, cut_of(at_x(3, other, 0), cut), east)
        from_east.wait()
        gather(last, cut_of(at_x(1, other, 1), cut), west)
    total = norm_take(norm_y, sent)
    norm = jnp.sqrt(jnp.sum(total, keepdims=True) + 1e-06)
    factor = jnp.broadcast_to(
        jnp.minimum(1.0, 0.5 * math.sqrt(entries) / norm), TILE
    )[None]

    loads[1].wait()
    loads[2].wait()

    def update(at):
        start, count = at.start, at.size

        def body(i, n):
            at = pl.ds(start + i, n)
            clipped = factor * mean[at]
            moved = 0.9 * momentum[at] + clipped
            new_momentum[at] = moved
            new_params[at] = params[at] - 0.7 * (clipped + 0.9 * moved)

        over_tiles(count, body)

    update(at_x(0, half, 0, 2))
    update(at_x(3, half, 0))
    update(at_x(1, half, 1))
    for chunk in range(4):
        update(at_y(half, chunk, 0, 2))
    update(at_x(0, other, 0, 2))
    update(at_x(3, other, 0))
    update(at_x(1, other, 1))
    early.wait()
    update(at_x(3, half, 1))
    update(at_x(1, half, 0))
    update(at_x(2, half, 0, 2))
    for chunk in (0, 3, 1):
        update(at_y(other, chunk, 0, 2))
    late.wait()
    update(at_x(3, other, 1))
    update(at_x(1, other, 0))
    last_first.wait()
    update(cut_of(at_x(2, other, 0), FIRST))
    update(cut_of(at_x(2, other, 1), FIRST))
    last_y.wait()
    update(at_y(other, 2, 0, 2))
    last_rest.wait()
    update(cut_of(at_x(2, other, 0), REST))
    update(cut_of(at_x(2, other, 1), REST))
    copies.finish()
    assert copies.groups == GROUPS_OF_COPIES, copies.groups


def store_kernel(params, momentum, params_out, momentum_out, sem):
    cuts = 1
    size = TILES // cuts
    copies = []
    for i in range(cuts):
        for j, (src, dst) in enumerate(((params, params_out), (momentum, momentum_out))):
            at = pl.ds(i * size, size)
            copy = pltpu.make_async_copy(src.at[at], dst.at[at], sem.at[i * 2 + j])
            copy.start()
            copies.append(copy)
    for copy in copies:
        copy.wait()


def per_device(pseudo_grad, params, momentum):
    rows, columns = params.shape
    entries = rows * lax.axis_size("inner") * columns
    f32 = jnp.float32
    near = pltpu.VMEM((TILES, *TILE), f32)
    far = jax.ShapeDtypeStruct((TILES, *TILE), f32)

    def vmem(*lead):
        return pltpu.VMEM((*lead, *TILE), f32)

    results = pl.pallas_call(
        functools.partial(kernel, entries),
        out_shape=[near, near],
        in_specs=[pl.BlockSpec(memory_space=pl.ANY)] * 3,
        out_specs=[pl.BlockSpec(memory_space=pltpu.VMEM)] * 2,
        scratch_shapes=[
            vmem(TILES),
            vmem(TILES),
            vmem(TILES),
            vmem(TILES),
            vmem(2, 2, A),
            vmem(2, 2, A),
            vmem(2, 2, A),
            vmem(2 * A),
            vmem(2 * A),
            vmem(4, 2 * B),
            vmem(2, B),
            vmem(2, B),
            vmem(2, B),
            vmem(),
            vmem(4),
            vmem(2),
            vmem(4),
            vmem(4),
            pltpu.SemaphoreType.DMA((3,)),
            pltpu.SemaphoreType.DMA((GROUPS_OF_COPIES,)),
            pltpu.SemaphoreType.DMA((3,)),
            pltpu.SemaphoreType.REGULAR,
            pltpu.SemaphoreType.REGULAR,
            pltpu.SemaphoreType.REGULAR,
            pltpu.SemaphoreType.REGULAR,
        ],
        compiler_params=pltpu.CompilerParams(
            collective_id=0, has_side_effects=True, vmem_limit_bytes=49 * 2**20
        ),
        name="outer_step",
    )(tiles_of(pseudo_grad[0]), tiles_of(params), tiles_of(momentum))
    results = pl.pallas_call(
        store_kernel,
        out_shape=[far, far],
        in_specs=[pl.BlockSpec(memory_space=pltpu.VMEM)] * 2,
        out_specs=[pl.BlockSpec(memory_space=pl.ANY)] * 2,
        scratch_shapes=[pltpu.SemaphoreType.DMA((2,))],
        compiler_params=pltpu.CompilerParams(vmem_limit_bytes=40 * 2**20),
        name="store",
    )(*results)
    return tuple(block_of(result, rows, columns) for result in results)


def solution(mesh):
    placed = (P("outer", "inner", None), P("inner", None), P("inner", None))
    return jax.shard_map(
        per_device,
        mesh=mesh,
        in_specs=placed,
        out_specs=(P("inner", None), P("inner", None)),
        check_vma=False,
    )
```

```python
import functools
import math

import jax
import jax.numpy as jnp
from jax import lax
from jax.experimental import pallas as pl
from jax.experimental.pallas import tpu as pltpu
from jax.sharding import PartitionSpec as P

MESH = pl.DeviceIdType.MESH
TILE = (8, 128)
TILES = 1024
A = 36
B = 28
STEP = 10
FIRST, REST = pl.ds(0, 16), pl.ds(16, A - 16)
GROUPS = 8


def tiles_of(block):
    rows, columns = block.shape
    cut = block.reshape(rows // 8, 8, columns // 128, 128)
    return cut.transpose(0, 2, 1, 3).reshape(-1, 8, 128)


def block_of(tiles, rows, columns):
    cut = tiles.reshape(rows // 8, columns // 128, 8, 128)
    return cut.transpose(0, 2, 1, 3).reshape(rows, columns)


def over_tiles(count, body):
    steps, rest = divmod(count, STEP)
    if steps == 1:
        body(0, STEP)
    elif steps > 1:

        def step(i, carry):
            body(i * STEP, STEP)
            return carry

        lax.fori_loop(0, steps, step, 0)
    if rest:
        body(steps * STEP, rest)


class Copies:
    def __init__(self, send_sem, recv_sem, any_tiles):
        self.send_sem, self.recv_sem, self.any_tiles = send_sem, recv_sem, any_tiles
        self.groups, self.sent = 0, {}

    def group(self):
        self.groups += 1
        return Group(self, self.recv_sem.at[self.groups - 1])

    def wait(self, tiles, send=None, recv=None):
        some = self.any_tiles.at[pl.ds(0, tiles)]
        copy = pltpu.make_async_remote_copy(
            src_ref=some,
            dst_ref=some,
            send_sem=self.send_sem.at[0] if send is None else send,
            recv_sem=self.recv_sem.at[0] if recv is None else recv,
            device_id=self.anyone,
            device_id_type=MESH,
        )
        if recv is None:
            copy.wait_send()
        else:
            copy.wait_recv()

    def finish(self):
        for number, tiles in self.sent.items():
            self.wait(tiles, send=self.send_sem.at[number])


class Group:
    def __init__(self, copies, sem):
        self.copies, self.sem, self.tiles = copies, sem, 0

    def send(self, src, dst, to):
        number, device = to
        tiles = math.prod(src.shape) // math.prod(TILE)
        pltpu.make_async_remote_copy(
            src_ref=src,
            dst_ref=dst,
            send_sem=self.copies.send_sem.at[number],
            recv_sem=self.sem,
            device_id=device,
            device_id_type=MESH,
        ).start()
        self.tiles += tiles
        self.copies.sent[number] = self.copies.sent.get(number, 0) + tiles

    def wait(self):
        self.copies.wait(self.tiles, recv=self.sem)


GROUPS_OF_COPIES = 30


def kernel(
    entries,
    grad_hbm,
    params_hbm,
    momentum_hbm,
    new_params,
    new_momentum,
    grad,
    params,
    momentum,
    mean,
    x_first,
    x_second,
    x_third,
    x_sum,
    x_from_y,
    y_sum,
    q_first,
    q_second,
    q_third,
    squares,
    norm_z,
    norm_core,
    norm_x,
    norm_y,
    send_sem,
    recv_sem,
    load_sem,
    west_sem,
    east_sem,
    across_sem,
    met_sem,
):
    outer, inner = lax.axis_index("outer"), lax.axis_index("inner")
    x, half = lax.rem(outer, 4), lax.div(outer, 4)
    low, z, core = lax.div(inner, 8), lax.rem(lax.div(inner, 2), 4), lax.rem(inner, 2)
    y = half * 2 + low

    def device(x=x, y=y, z=z, core=core):
        return (lax.div(y, 2) * 4 + x, (lax.rem(y, 2) * 4 + z) * 2 + core)

    def ring(at, by):
        return lax.rem(at + by, 4)

    east, west, across = [
        (0, device(x=ring(x, 1))),
        (1, device(x=ring(x, 3))),
        (2, device(y=ring(y, 2))),
    ]
    x_peers = [(2, device(x=ring(x, k))) for k in (1, 2, 3)]
    y_peers = [(2, device(y=ring(y, k))) for k in (1, 2, 3)]
    z_peers = [(2, device(z=ring(z, k))) for k in (1, 2, 3)]
    core_peer = (2, device(core=1 - core))

    met = [
        (ring(x, 3) > x, west, west_sem, east_sem),
        (ring(x, 1) > x, east, east_sem, west_sem),
        (half == 0, across, across_sem, across_sem),
    ]
    met += [(half == 0, (2, device(y=3 - y)), met_sem, met_sem)]
    met += [(core == 1, core_peer, met_sem, met_sem)]
    met += [(ring(z, k) > z, (2, device(z=ring(z, k))), met_sem, met_sem) for k in (1, 2, 3)]
    lower = sum(jnp.where(higher, 0, 1) for higher, *_ in met)
    above = sum(jnp.where(higher, 1, 0) for higher, *_ in met[3:])

    barrier = pltpu.get_barrier_semaphore()
    for higher, (_, peer), _, _ in met:

        @pl.when(higher)
        def greet(peer=peer):
            pl.semaphore_signal(barrier, inc=1, device_id=peer, device_id_type=MESH)

    loads = [
        pltpu.make_async_copy(src, dst, load_sem.at[i])
        for i, (src, dst) in enumerate(
            ((grad_hbm, grad), (params_hbm, params), (momentum_hbm, momentum))
        )
    ]
    loads[0].start()

    @pl.when(lower > 0)
    def all_lower():
        pl.semaphore_wait(barrier, lower)

    def answer(higher, peer, _, theirs):
        @pl.when(jnp.logical_not(higher))
        def signal():
            pl.semaphore_signal(theirs, inc=1, device_id=peer[1], device_id_type=MESH)

    def answered(higher, _, mine, __):
        @pl.when(higher)
        def wait():
            pl.semaphore_wait(mine, 1)

    for entry in met[:3]:
        answer(*entry)

    copies = Copies(send_sem, recv_sem, mean)
    copies.anyone = east[1]
    other = 1 - half

    def at_x(chunk, h, d, pieces=1):
        return pl.ds(((ring(x, chunk) * 2 + h) * 2 + d) * A, pieces * A)

    def at_y(h, chunk, d, pieces=1):
        return pl.ds(16 * A + ((h * 4 + ring(x, chunk)) * 2 + d) * B, pieces * B)

    a_both, a_rest, b_both, b_rest, q_both, q_rest = [copies.group() for _ in range(6)]
    y_first = {(chunk, d): copies.group() for chunk, d in ((2, 0), (1, 0), (3, 1), (1, 1), (3, 0))}

    def x_open(group, chunk, h, d, land, to, cut=None):
        at = at_x(chunk, h, d)
        if cut is not None:
            at, land = cut_of(at, cut), land.at[cut]
        group.send(grad_hbm.at[at], land, to)

    def y_open(group, chunk, d, pieces=1):
        group.send(
            grad_hbm.at[at_y(other, chunk, d, pieces)],
            y_sum.at[chunk, pl.ds(d * B, pieces * B)],
            across,
        )

    def cut_of(at, cut):
        return pl.ds(at.start + cut.start, cut.size)

    def add_into(ref, term, start, count):
        def body(i, n):
            ref[pl.ds(i, n)] += term[pl.ds(start + i, n)]

        over_tiles(count, body)

    def y_add(chunk, d, pieces=1):
        piece = y_sum.at[chunk, pl.ds(d * B, pieces * B)]
        add_into(piece, grad, at_y(half, chunk, d).start, pieces * B)
        return piece

    def y_open_all():
        y_open(y_first[2, 0], 2, 0, 2)
        for chunk, d in ((1, 0), (3, 1), (1, 1), (3, 0)):
            y_open(y_first[chunk, d], chunk, d)
        y_open(q_rest, 0, 0, 2)

    counts = copies.sent.get(2, 0), {g: g.tiles for g in (*y_first.values(), q_rest)}

    @pl.when(half == 1)
    def y_now():
        y_open_all()

    copies.sent[2] = counts[0]
    for group, tiles in counts[1].items():
        group.tiles = tiles

    answered(*met[1])
    x_open(a_both, 2, other, 1, x_first.at[0, 1], east)
    x_open(a_rest, 1, other, 0, x_second.at[0, 0], east)
    x_open(b_both, 2, half, 1, x_first.at[1, 1], east)
    answered(*met[0])
    x_open(a_both, 2, other, 0, x_first.at[0, 0], west)
    x_open(a_rest, 3, other, 1, x_second.at[0, 1], west)
    x_open(b_both, 2, half, 0, x_first.at[1, 0], west)

    @pl.when(half == 0)
    def y_answered():
        pl.semaphore_wait(across_sem, 1)
        y_open_all()

    for entry in met[3:]:
        answer(*entry)

    loads[1].start()
    loads[2].start()
    loads[0].wait()

    def pass_on(rest, ref, land, to, term, start, count):
        add_into(ref, term, start, count)
        rest.send(ref, land, to)

    def x_pass(slot, h, both, rest):
        both.wait()
        for d, chunk, to in ((0, 3, west), (1, 1, east)):
            pass_on(
                rest,
                x_first.at[slot, d],
                x_third.at[slot, d],
                to,
                grad,
                at_x(chunk, h, d).start,
                A,
            )

    x_pass(0, other, a_both, a_rest)
    y_first[2, 0].wait()
    y_add(2, 0, 2)
    q_both.send(y_sum.at[2, pl.ds(0, B)], q_first.at[0], west)
    q_both.send(y_sum.at[2, pl.ds(B, B)], q_first.at[1], east)
    y_first[1, 0].wait()
    q_rest.send(y_add(1, 0), q_second.at[0], east)
    y_first[3, 1].wait()
    q_rest.send(y_add(3, 1), q_second.at[1], west)
    a_rest.wait()
    for d in (0, 1):
        base = at_x(0, other, d).start

        def body(i, n, d=d, base=base):
            x_sum[pl.ds(d * A + i, n)] = (
                grad[pl.ds(base + i, n)]
                + x_second[0, d, pl.ds(i, n)]
                + x_third[0, d, pl.ds(i, n)]
            )

        over_tiles(A, body)
    @pl.when(above > 0)
    def all_met():
        pl.semaphore_wait(met_sem, above)

    b_rest.send(x_sum, x_from_y, across)
    x_open(b_rest, 1, half, 0, x_second.at[1, 0], east, FIRST)
    x_open(b_rest, 3, half, 1, x_second.at[1, 1], west, FIRST)
    y_first[1, 1].wait()
    y_add(1, 1)
    q_both.wait()
    pass_on(q_rest, q_first.at[1], q_third.at[1], east, y_sum.at[1], B, B)
    y_first[3, 0].wait()
    y_add(3, 0)
    pass_on(q_rest, q_first.at[0], q_third.at[0], west, y_sum.at[3], 0, B)
    x_open(b_rest, 1, half, 0, x_second.at[1, 0], east, REST)
    x_open(b_rest, 3, half, 1, x_second.at[1, 1], west, REST)
    x_pass(1, half, b_both, b_rest)

    squares[...] = jnp.zeros(TILE, jnp.float32)

    def store_mean(at, value):
        value = value / jnp.float32(GROUPS)
        mean[at] = value
        squares[...] += jnp.sum(value * value, axis=0)

    q_rest.wait()
    y_add(0, 0, 2)
    for d in (0, 1):
        base = at_y(half, 0, d).start

        def body(i, n, d=d, base=base):
            at = pl.ds(i, n)
            store_mean(
                pl.ds(base + i, n),
                y_sum[0, pl.ds(d * B + i, n)] + q_second[d, at] + q_third[d, at],
            )

        over_tiles(B, body)

    def gather(group, at, to):
        group.send(mean.at[at], mean.at[at], to)

    q_from_west, q_from_east, q_far = copies.group(), copies.group(), copies.group()
    x_from_west, x_from_east, crossed = copies.group(), copies.group(), copies.group()
    x_cuts = [(cut, copies.group(), copies.group()) for cut in (FIRST, REST)]
    early, late, last_first, last_rest, last_y = [copies.group() for _ in range(5)]

    gather(q_from_west, at_y(half, 0, 0, 2), east)
    gather(q_from_east, at_y(half, 0, 0, 2), west)
    gather(early, at_y(half, 0, 0, 2), across)

    b_rest.wait()
    for d in (0, 1):
        base = at_x(0, half, d).start

        def body(i, n, d=d, base=base):
            at = pl.ds(i, n)
            own = grad[pl.ds(base + i, n)] + x_second[1, d, at] + x_third[1, d, at]
            store_mean(pl.ds(base + i, n), own + x_from_y[pl.ds(d * A + i, n)])

        over_tiles(A, body)

    gather(x_from_west, at_x(0, half, 0), east)
    gather(x_from_east, at_x(0, half, 1), west)
    gather(early, at_x(0, half, 1), east)
    gather(early, at_x(0, half, 0), west)
    gather(crossed, at_x(0, half, 0, 2), across)

    def norm_send(slots, mine, value, to):
        group = copies.group()
        slots[mine] = value
        for peer in to:
            group.send(slots.at[mine], slots.at[mine], peer)
        return group

    def norm_take(slots, group):
        group.wait()
        total = slots[0]
        for i in range(1, slots.shape[0]):
            total = total + slots[i]
        return total

    sent = norm_send(norm_z, z, squares[...], z_peers)

    q_from_west.wait()
    gather(q_far, at_y(half, 3, 0), east)
    gather(early, at_y(half, 3, 0, 2), across)
    q_from_east.wait()
    gather(q_far, at_y(half, 1, 1), west)
    gather(early, at_y(half, 1, 0, 2), across)
    value = norm_take(norm_z, sent)
    sent = norm_send(norm_core, core, value, [core_peer])
    value = norm_take(norm_core, sent)
    sent = norm_send(norm_x, x, value, x_peers)
    x_from_west.wait()
    gather(early, at_x(3, half, 0), east)
    x_from_east.wait()
    gather(early, at_x(1, half, 1), west)
    crossed.wait()
    for cut, from_west, from_east in x_cuts:
        gather(from_west, cut_of(at_x(0, other, 0), cut), east)
        gather(from_east, cut_of(at_x(0, other, 1), cut), west)
    gather(late, at_x(0, other, 1), east)
    gather(late, at_x(0, other, 0), west)
    value = norm_take(norm_x, sent)
    sent = norm_send(norm_y, y, value, y_peers)
    q_far.wait()
    gather(last_y, at_y(half, 2, 0, 2), across)
    for (cut, from_west, from_east), last in zip(x_cuts, (last_first, last_rest)):
        from_west.wait()
        gather(last, cut_of(at_x(3, other, 0), cut), east)
        from_east.wait()
        gather(last, cut_of(at_x(1, other, 1), cut), west)
    total = norm_take(norm_y, sent)
    norm = jnp.sqrt(jnp.sum(total, keepdims=True) + 1e-06)
    factor = jnp.broadcast_to(
        jnp.minimum(1.0, 0.5 * math.sqrt(entries) / norm), TILE
    )[None]

    loads[1].wait()
    loads[2].wait()

    def update(at):
        start, count = at.start, at.size

        def body(i, n):
            at = pl.ds(start + i, n)
            clipped = factor * mean[at]
            moved = 0.9 * momentum[at] + clipped
            new_momentum[at] = moved
            new_params[at] = params[at] - 0.7 * (clipped + 0.9 * moved)

        over_tiles(count, body)

    update(at_x(0, half, 0, 2))
    update(at_x(3, half, 0))
    update(at_x(1, half, 1))
    for chunk in range(4):
        update(at_y(half, chunk, 0, 2))
    update(at_x(0, other, 0, 2))
    update(at_x(3, other, 0))
    update(at_x(1, other, 1))
    early.wait()
    update(at_x(3, half, 1))
    update(at_x(1, half, 0))
    update(at_x(2, half, 0, 2))
    for chunk in (0, 3, 1):
        update(at_y(other, chunk, 0, 2))
    late.wait()
    update(at_x(3, other, 1))
    update(at_x(1, other, 0))
    last_first.wait()
    update(cut_of(at_x(2, other, 0), FIRST))
    update(cut_of(at_x(2, other, 1), FIRST))
    last_y.wait()
    update(at_y(other, 2, 0, 2))
    last_rest.wait()
    update(cut_of(at_x(2, other, 0), REST))
    update(cut_of(at_x(2, other, 1), REST))
    copies.finish()
    assert copies.groups == GROUPS_OF_COPIES, copies.groups


def store_kernel(params, momentum, params_out, momentum_out, sem):
    cuts = 1
    size = TILES // cuts
    copies = []
    for i in range(cuts):
        for j, (src, dst) in enumerate(((params, params_out), (momentum, momentum_out))):
            at = pl.ds(i * size, size)
            copy = pltpu.make_async_copy(src.at[at], dst.at[at], sem.at[i * 2 + j])
            copy.start()
            copies.append(copy)
    for copy in copies:
        copy.wait()


def per_device(pseudo_grad, params, momentum):
    rows, columns = params.shape
    entries = rows * lax.axis_size("inner") * columns
    f32 = jnp.float32
    near = pltpu.VMEM((TILES, *TILE), f32)
    far = jax.ShapeDtypeStruct((TILES, *TILE), f32)

    def vmem(*lead):
        return pltpu.VMEM((*lead, *TILE), f32)

    results = pl.pallas_call(
        functools.partial(kernel, entries),
        out_shape=[near, near],
        in_specs=[pl.BlockSpec(memory_space=pl.ANY)] * 3,
        out_specs=[pl.BlockSpec(memory_space=pltpu.VMEM)] * 2,
        scratch_shapes=[
            vmem(TILES),
            vmem(TILES),
            vmem(TILES),
            vmem(TILES),
            vmem(2, 2, A),
            vmem(2, 2, A),
            vmem(2, 2, A),
            vmem(2 * A),
            vmem(2 * A),
            vmem(4, 2 * B),
            vmem(2, B),
            vmem(2, B),
            vmem(2, B),
            vmem(),
            vmem(4),
            vmem(2),
            vmem(4),
            vmem(4),
            pltpu.SemaphoreType.DMA((3,)),
            pltpu.SemaphoreType.DMA((GROUPS_OF_COPIES,)),
            pltpu.SemaphoreType.DMA((3,)),
            pltpu.SemaphoreType.REGULAR,
            pltpu.SemaphoreType.REGULAR,
            pltpu.SemaphoreType.REGULAR,
            pltpu.SemaphoreType.REGULAR,
        ],
        compiler_params=pltpu.CompilerParams(
            collective_id=0, has_side_effects=True, vmem_limit_bytes=49 * 2**20
        ),
        name="outer_step",
    )(tiles_of(pseudo_grad[0]), tiles_of(params), tiles_of(momentum))
    results = pl.pallas_call(
        store_kernel,
        out_shape=[far, far],
        in_specs=[pl.BlockSpec(memory_space=pltpu.VMEM)] * 2,
        out_specs=[pl.BlockSpec(memory_space=pl.ANY)] * 2,
        scratch_shapes=[pltpu.SemaphoreType.DMA((2,))],
        compiler_params=pltpu.CompilerParams(vmem_limit_bytes=40 * 2**20),
        name="store",
    )(*results)
    return tuple(block_of(result, rows, columns) for result in results)


def solution(mesh):
    placed = (P("outer", "inner", None), P("inner", None), P("inner", None))
    return jax.shard_map(
        per_device,
        mesh=mesh,
        in_specs=placed,
        out_specs=(P("inner", None), P("inner", None)),
        check_vma=False,
    )
```

```python
import functools
import math

import jax
import jax.numpy as jnp
from jax import lax
from jax.experimental import pallas as pl
from jax.experimental.pallas import tpu as pltpu
from jax.sharding import PartitionSpec as P

MESH = pl.DeviceIdType.MESH
TILE = (8, 128)
TILES = 1024
A = 36
B = 28
STEP = 9
FIRST, REST = pl.ds(0, 16), pl.ds(16, A - 16)
GROUPS = 8


def tiles_of(block):
    rows, columns = block.shape
    cut = block.reshape(rows // 8, 8, columns // 128, 128)
    return cut.transpose(0, 2, 1, 3).reshape(-1, 8, 128)


def block_of(tiles, rows, columns):
    cut = tiles.reshape(rows // 8, columns // 128, 8, 128)
    return cut.transpose(0, 2, 1, 3).reshape(rows, columns)


def over_tiles(count, body):
    steps, rest = divmod(count, STEP)
    if steps == 1:
        body(0, STEP)
    elif steps > 1:

        def step(i, carry):
            body(i * STEP, STEP)
            return carry

        lax.fori_loop(0, steps, step, 0)
    if rest:
        body(steps * STEP, rest)


class Copies:
    def __init__(self, send_sem, recv_sem, any_tiles):
        self.send_sem, self.recv_sem, self.any_tiles = send_sem, recv_sem, any_tiles
        self.groups, self.sent = 0, {}

    def group(self):
        self.groups += 1
        return Group(self, self.recv_sem.at[self.groups - 1])

    def wait(self, tiles, send=None, recv=None):
        some = self.any_tiles.at[pl.ds(0, tiles)]
        copy = pltpu.make_async_remote_copy(
            src_ref=some,
            dst_ref=some,
            send_sem=self.send_sem.at[0] if send is None else send,
            recv_sem=self.recv_sem.at[0] if recv is None else recv,
            device_id=self.anyone,
            device_id_type=MESH,
        )
        if recv is None:
            copy.wait_send()
        else:
            copy.wait_recv()

    def finish(self):
        for number, tiles in self.sent.items():
            self.wait(tiles, send=self.send_sem.at[number])


class Group:
    def __init__(self, copies, sem):
        self.copies, self.sem, self.tiles = copies, sem, 0

    def send(self, src, dst, to):
        number, device = to
        tiles = math.prod(src.shape) // math.prod(TILE)
        pltpu.make_async_remote_copy(
            src_ref=src,
            dst_ref=dst,
            send_sem=self.copies.send_sem.at[number],
            recv_sem=self.sem,
            device_id=device,
            device_id_type=MESH,
        ).start()
        self.tiles += tiles
        self.copies.sent[number] = self.copies.sent.get(number, 0) + tiles

    def wait(self):
        self.copies.wait(self.tiles, recv=self.sem)


GROUPS_OF_COPIES = 33


def kernel(
    entries,
    grad_hbm,
    params_hbm,
    momentum_hbm,
    new_params,
    new_momentum,
    grad,
    params,
    momentum,
    mean,
    x_first,
    x_second,
    x_third,
    x_sum,
    x_from_y,
    y_sum,
    q_first,
    q_second,
    q_third,
    squares,
    norm_z,
    norm_core,
    norm_x,
    norm_y,
    send_sem,
    recv_sem,
    load_sem,
    west_sem,
    east_sem,
    across_sem,
    met_sem,
):
    outer, inner = lax.axis_index("outer"), lax.axis_index("inner")
    x, half = lax.rem(outer, 4), lax.div(outer, 4)
    low, z, core = lax.div(inner, 8), lax.rem(lax.div(inner, 2), 4), lax.rem(inner, 2)
    y = half * 2 + low

    def device(x=x, y=y, z=z, core=core):
        return (lax.div(y, 2) * 4 + x, (lax.rem(y, 2) * 4 + z) * 2 + core)

    def ring(at, by):
        return lax.rem(at + by, 4)

    east, west, across = [
        (0, device(x=ring(x, 1))),
        (1, device(x=ring(x, 3))),
        (2, device(y=ring(y, 2))),
    ]
    x_peers = [(3, device(x=ring(x, k))) for k in (1, 2, 3)]
    y_peers = [(3, device(y=ring(y, k))) for k in (1, 2, 3)]
    z_peers = [(3, device(z=ring(z, k))) for k in (1, 2, 3)]
    core_peer = (3, device(core=1 - core))

    met = [
        (ring(x, 3) > x, west, west_sem, east_sem),
        (ring(x, 1) > x, east, east_sem, west_sem),
        (half == 0, across, across_sem, across_sem),
    ]
    met += [(half == 0, (3, device(y=3 - y)), met_sem, met_sem)]
    met += [(core == 1, core_peer, met_sem, met_sem)]
    met += [(ring(z, k) > z, (3, device(z=ring(z, k))), met_sem, met_sem) for k in (1, 2, 3)]
    lower = sum(jnp.where(higher, 0, 1) for higher, *_ in met)
    above = sum(jnp.where(higher, 1, 0) for higher, *_ in met[3:])

    barrier = pltpu.get_barrier_semaphore()
    for higher, (_, peer), _, _ in met:

        @pl.when(higher)
        def greet(peer=peer):
            pl.semaphore_signal(barrier, inc=1, device_id=peer, device_id_type=MESH)

    loads = [
        pltpu.make_async_copy(src, dst, load_sem.at[i])
        for i, (src, dst) in enumerate(
            ((grad_hbm, grad), (params_hbm, params), (momentum_hbm, momentum))
        )
    ]
    loads[0].start()

    @pl.when(lower > 0)
    def all_lower():
        pl.semaphore_wait(barrier, lower)

    def answer(higher, peer, _, theirs):
        @pl.when(jnp.logical_not(higher))
        def signal():
            pl.semaphore_signal(theirs, inc=1, device_id=peer[1], device_id_type=MESH)

    def answered(higher, _, mine, __):
        @pl.when(higher)
        def wait():
            pl.semaphore_wait(mine, 1)

    for entry in met[:3]:
        answer(*entry)

    copies = Copies(send_sem, recv_sem, mean)
    copies.anyone = east[1]
    other = 1 - half

    def at_x(chunk, h, d, pieces=1):
        return pl.ds(((ring(x, chunk) * 2 + h) * 2 + d) * A, pieces * A)

    def at_y(h, chunk, d, pieces=1):
        return pl.ds(16 * A + ((h * 4 + ring(x, chunk)) * 2 + d) * B, pieces * B)

    a_west, a_east, a_rest = copies.group(), copies.group(), copies.group()
    b_west, b_east, b_rest = copies.group(), copies.group(), copies.group()
    q_west, q_east, q_rest = copies.group(), copies.group(), copies.group()
    y_first = {(chunk, d): copies.group() for chunk, d in ((2, 0), (1, 0), (3, 1), (1, 1), (3, 0))}

    def x_open(group, chunk, h, d, land, to, cut=None):
        at = at_x(chunk, h, d)
        if cut is not None:
            at, land = cut_of(at, cut), land.at[cut]
        group.send(grad_hbm.at[at], land, to)

    def y_open(group, chunk, d, pieces=1):
        group.send(
            grad_hbm.at[at_y(other, chunk, d, pieces)],
            y_sum.at[chunk, pl.ds(d * B, pieces * B)],
            across,
        )

    def cut_of(at, cut):
        return pl.ds(at.start + cut.start, cut.size)

    def add_into(ref, term, start, count):
        def body(i, n):
            ref[pl.ds(i, n)] += term[pl.ds(start + i, n)]

        over_tiles(count, body)

    def y_add(chunk, d, pieces=1):
        piece = y_sum.at[chunk, pl.ds(d * B, pieces * B)]
        add_into(piece, grad, at_y(half, chunk, d).start, pieces * B)
        return piece

    def y_open_all():
        y_open(y_first[2, 0], 2, 0, 2)
        for chunk, d in ((1, 0), (3, 1), (1, 1), (3, 0)):
            y_open(y_first[chunk, d], chunk, d)
        y_open(q_rest, 0, 0, 2)

    counts = copies.sent.get(2, 0), {g: g.tiles for g in (*y_first.values(), q_rest)}

    @pl.when(half == 1)
    def y_now():
        y_open_all()

    copies.sent[2] = counts[0]
    for group, tiles in counts[1].items():
        group.tiles = tiles

    answered(*met[1])
    x_open(a_east, 2, other, 1, x_first.at[0, 1], east)
    x_open(a_rest, 1, other, 0, x_second.at[0, 0], east)
    x_open(b_east, 2, half, 1, x_first.at[1, 1], east)
    answered(*met[0])
    x_open(a_west, 2, other, 0, x_first.at[0, 0], west)
    x_open(a_rest, 3, other, 1, x_second.at[0, 1], west)
    x_open(b_west, 2, half, 0, x_first.at[1, 0], west)

    @pl.when(half == 0)
    def y_answered():
        pl.semaphore_wait(across_sem, 1)
        y_open_all()

    for entry in met[3:]:
        answer(*entry)

    loads[1].start()
    loads[2].start()
    loads[0].wait()

    def pass_on(arrived, rest, ref, land, to, term, start, count):
        arrived.wait()
        add_into(ref, term, start, count)
        rest.send(ref, land, to)

    def x_pass(slot, h, from_east, from_west, rest):
        for arrived, d, chunk, to in ((from_east, 0, 3, west), (from_west, 1, 1, east)):
            pass_on(
                arrived,
                rest,
                x_first.at[slot, d],
                x_third.at[slot, d],
                to,
                grad,
                at_x(chunk, h, d).start,
                A,
            )

    x_pass(0, other, a_west, a_east, a_rest)
    y_first[2, 0].wait()
    y_add(2, 0, 2)
    q_west.send(y_sum.at[2, pl.ds(0, B)], q_first.at[0], west)
    q_east.send(y_sum.at[2, pl.ds(B, B)], q_first.at[1], east)
    y_first[1, 0].wait()
    q_rest.send(y_add(1, 0), q_second.at[0], east)
    y_first[3, 1].wait()
    q_rest.send(y_add(3, 1), q_second.at[1], west)
    a_rest.wait()
    for d in (0, 1):
        base = at_x(0, other, d).start

        def body(i, n, d=d, base=base):
            x_sum[pl.ds(d * A + i, n)] = (
                grad[pl.ds(base + i, n)]
                + x_second[0, d, pl.ds(i, n)]
                + x_third[0, d, pl.ds(i, n)]
            )

        over_tiles(A, body)
    @pl.when(above > 0)
    def all_met():
        pl.semaphore_wait(met_sem, above)

    b_rest.send(x_sum, x_from_y, across)
    x_open(b_rest, 1, half, 0, x_second.at[1, 0], east, FIRST)
    x_open(b_rest, 3, half, 1, x_second.at[1, 1], west, FIRST)
    y_first[1, 1].wait()
    y_add(1, 1)
    pass_on(q_east, q_rest, q_first.at[1], q_third.at[1], east, y_sum.at[1], B, B)
    y_first[3, 0].wait()
    y_add(3, 0)
    pass_on(q_west, q_rest, q_first.at[0], q_third.at[0], west, y_sum.at[3], 0, B)
    x_open(b_rest, 1, half, 0, x_second.at[1, 0], east, REST)
    x_open(b_rest, 3, half, 1, x_second.at[1, 1], west, REST)
    x_pass(1, half, b_west, b_east, b_rest)

    squares[...] = jnp.zeros(TILE, jnp.float32)

    def store_mean(at, value):
        value = value / jnp.float32(GROUPS)
        mean[at] = value
        squares[...] += jnp.sum(value * value, axis=0)

    q_rest.wait()
    y_add(0, 0, 2)
    for d in (0, 1):
        base = at_y(half, 0, d).start

        def body(i, n, d=d, base=base):
            at = pl.ds(i, n)
            store_mean(
                pl.ds(base + i, n),
                y_sum[0, pl.ds(d * B + i, n)] + q_second[d, at] + q_third[d, at],
            )

        over_tiles(B, body)

    def gather(group, at, to):
        group.send(mean.at[at], mean.at[at], to)

    q_from_west, q_from_east, q_far = copies.group(), copies.group(), copies.group()
    x_from_west, x_from_east, crossed = copies.group(), copies.group(), copies.group()
    x_cuts = [(cut, copies.group(), copies.group()) for cut in (FIRST, REST)]
    early, late, last_first, last_rest, last_y = [copies.group() for _ in range(5)]

    gather(q_from_west, at_y(half, 0, 0, 2), east)
    gather(q_from_east, at_y(half, 0, 0, 2), west)
    gather(early, at_y(half, 0, 0, 2), across)

    b_rest.wait()
    for d in (0, 1):
        base = at_x(0, half, d).start

        def body(i, n, d=d, base=base):
            at = pl.ds(i, n)
            own = grad[pl.ds(base + i, n)] + x_second[1, d, at] + x_third[1, d, at]
            store_mean(pl.ds(base + i, n), own + x_from_y[pl.ds(d * A + i, n)])

        over_tiles(A, body)

    gather(x_from_west, at_x(0, half, 0), east)
    gather(x_from_east, at_x(0, half, 1), west)
    gather(early, at_x(0, half, 1), east)
    gather(early, at_x(0, half, 0), west)
    gather(crossed, at_x(0, half, 0, 2), across)

    def norm_send(slots, mine, value, to):
        group = copies.group()
        slots[mine] = value
        for peer in to:
            group.send(slots.at[mine], slots.at[mine], peer)
        return group

    def norm_take(slots, group):
        group.wait()
        total = slots[0]
        for i in range(1, slots.shape[0]):
            total = total + slots[i]
        return total

    sent = norm_send(norm_z, z, squares[...], z_peers)

    q_from_west.wait()
    gather(q_far, at_y(half, 3, 0), east)
    gather(early, at_y(half, 3, 0, 2), across)
    q_from_east.wait()
    gather(q_far, at_y(half, 1, 1), west)
    gather(early, at_y(half, 1, 0, 2), across)
    value = norm_take(norm_z, sent)
    sent = norm_send(norm_core, core, value, [core_peer])
    value = norm_take(norm_core, sent)
    sent = norm_send(norm_x, x, value, x_peers)
    x_from_west.wait()
    gather(early, at_x(3, half, 0), east)
    x_from_east.wait()
    gather(early, at_x(1, half, 1), west)
    crossed.wait()
    for cut, from_west, from_east in x_cuts:
        gather(from_west, cut_of(at_x(0, other, 0), cut), east)
        gather(from_east, cut_of(at_x(0, other, 1), cut), west)
    gather(late, at_x(0, other, 1), east)
    gather(late, at_x(0, other, 0), west)
    value = norm_take(norm_x, sent)
    sent = norm_send(norm_y, y, value, y_peers)
    q_far.wait()
    gather(last_y, at_y(half, 2, 0, 2), across)
    for (cut, from_west, from_east), last in zip(x_cuts, (last_first, last_rest)):
        from_west.wait()
        gather(last, cut_of(at_x(3, other, 0), cut), east)
        from_east.wait()
        gather(last, cut_of(at_x(1, other, 1), cut), west)
    total = norm_take(norm_y, sent)
    norm = jnp.sqrt(jnp.sum(total, keepdims=True) + 1e-06)
    factor = jnp.broadcast_to(
        jnp.minimum(1.0, 0.5 * math.sqrt(entries) / norm), TILE
    )[None]

    loads[1].wait()
    loads[2].wait()

    def update(at):
        start, count = at.start, at.size

        def body(i, n):
            at = pl.ds(start + i, n)
            clipped = factor * mean[at]
            moved = 0.9 * momentum[at] + clipped
            new_momentum[at] = moved
            new_params[at] = params[at] - 0.7 * (clipped + 0.9 * moved)

        over_tiles(count, body)

    update(at_x(0, half, 0, 2))
    update(at_x(3, half, 0))
    update(at_x(1, half, 1))
    for chunk in range(4):
        update(at_y(half, chunk, 0, 2))
    update(at_x(0, other, 0, 2))
    update(at_x(3, other, 0))
    update(at_x(1, other, 1))
    early.wait()
    update(at_x(3, half, 1))
    update(at_x(1, half, 0))
    update(at_x(2, half, 0, 2))
    for chunk in (0, 3, 1):
        update(at_y(other, chunk, 0, 2))
    late.wait()
    update(at_x(3, other, 1))
    update(at_x(1, other, 0))
    last_first.wait()
    update(cut_of(at_x(2, other, 0), FIRST))
    update(cut_of(at_x(2, other, 1), FIRST))
    last_y.wait()
    update(at_y(other, 2, 0, 2))
    last_rest.wait()
    update(cut_of(at_x(2, other, 0), REST))
    update(cut_of(at_x(2, other, 1), REST))
    copies.finish()
    assert copies.groups == GROUPS_OF_COPIES, copies.groups


def store_kernel(params, momentum, params_out, momentum_out, sem):
    cuts = 1
    size = TILES // cuts
    copies = []
    for i in range(cuts):
        for j, (src, dst) in enumerate(((params, params_out), (momentum, momentum_out))):
            at = pl.ds(i * size, size)
            copy = pltpu.make_async_copy(src.at[at], dst.at[at], sem.at[i * 2 + j])
            copy.start()
            copies.append(copy)
    for copy in copies:
        copy.wait()


def per_device(pseudo_grad, params, momentum):
    rows, columns = params.shape
    entries = rows * lax.axis_size("inner") * columns
    f32 = jnp.float32
    near = pltpu.VMEM((TILES, *TILE), f32)
    far = jax.ShapeDtypeStruct((TILES, *TILE), f32)

    def vmem(*lead):
        return pltpu.VMEM((*lead, *TILE), f32)

    results = pl.pallas_call(
        functools.partial(kernel, entries),
        out_shape=[near, near],
        in_specs=[pl.BlockSpec(memory_space=pl.ANY)] * 3,
        out_specs=[pl.BlockSpec(memory_space=pltpu.VMEM)] * 2,
        scratch_shapes=[
            vmem(TILES),
            vmem(TILES),
            vmem(TILES),
            vmem(TILES),
            vmem(2, 2, A),
            vmem(2, 2, A),
            vmem(2, 2, A),
            vmem(2 * A),
            vmem(2 * A),
            vmem(4, 2 * B),
            vmem(2, B),
            vmem(2, B),
            vmem(2, B),
            vmem(),
            vmem(4),
            vmem(2),
            vmem(4),
            vmem(4),
            pltpu.SemaphoreType.DMA((4,)),
            pltpu.SemaphoreType.DMA((GROUPS_OF_COPIES,)),
            pltpu.SemaphoreType.DMA((3,)),
            pltpu.SemaphoreType.REGULAR,
            pltpu.SemaphoreType.REGULAR,
            pltpu.SemaphoreType.REGULAR,
            pltpu.SemaphoreType.REGULAR,
        ],
        compiler_params=pltpu.CompilerParams(
            collective_id=0, has_side_effects=True, vmem_limit_bytes=49 * 2**20
        ),
        name="outer_step",
    )(tiles_of(pseudo_grad[0]), tiles_of(params), tiles_of(momentum))
    results = pl.pallas_call(
        store_kernel,
        out_shape=[far, far],
        in_specs=[pl.BlockSpec(memory_space=pltpu.VMEM)] * 2,
        out_specs=[pl.BlockSpec(memory_space=pl.ANY)] * 2,
        scratch_shapes=[pltpu.SemaphoreType.DMA((2,))],
        compiler_params=pltpu.CompilerParams(vmem_limit_bytes=40 * 2**20),
        name="store",
    )(*results)
    return tuple(block_of(result, rows, columns) for result in results)


def solution(mesh):
    placed = (P("outer", "inner", None), P("inner", None), P("inner", None))
    return jax.shard_map(
        per_device,
        mesh=mesh,
        in_specs=placed,
        out_specs=(P("inner", None), P("inner", None)),
        check_vma=False,
    )
```
